128 devices in a mesh: dp: 4 (over y), expert: 32 (over z, x, core).
Axes of the slice: x: 4, y: 4, z: 4, core: 2. Of those that a mesh axis runs over, the one named last changes fastest.
Arguments:
- tokens: bfloat16 [16384, 7168], P(('dp', 'expert')), may hold values from -6 to 6
- grad_out: bfloat16 [16384, 7168], P(('dp', 'expert')), may hold values from -6 to 6
- routes: int32 [16384, 1], P(('dp', 'expert')), may hold values from 0 to 31; in each aligned block of 128 rows (0 to 127, 128 to 255, ...) at most 6 rows name the same one
- gate_prob: float32 [16384, 1], P(('dp', 'expert')), may hold values from 0.1 to 1
- w_gate: bfloat16 [32, 7168, 1024], P('expert', None, 'dp'), may hold values from -0.0625 to 0.0625
- w_up: bfloat16 [32, 7168, 1024], P('expert', None, 'dp'), may hold values from -0.0625 to 0.0625
- w_down: bfloat16 [32, 1024, 7168], P('expert', 'dp'), may hold values from -0.1875 to 0.1875
- moment_prev: float32 [32, 1024], P('expert', 'dp'), may hold values from 5 to 200
Outputs:
- grad_in: bfloat16 [16384, 7168], P(('dp', 'expert'))
- down_update: bfloat16 [32, 1024, 7168], P('expert', 'dp')
- second_moment: float32 [32, 1024], P('expert', 'dp')
The draws below stay inside these ranges and needn't reach their ends.
Inputs may be any that keep to these rules, and one draw needn't show every extreme that they name: The 128 tokens of one device (aligned blocks of rows) name one expert in at most 6 routes; some block reaches 6.
All inputs are finite; a program needn't handle non-finite values.
Results may differ from the reference program's by a relative error of at most 0.0065.
Values may be sent and summed in bfloat16 or wider, within the bound.
A program may use at most 192 MiB of HBM per device.

```python
import math
import jax
import jax.numpy as jnp
import numpy as np
from jax import lax

D = 7168
HID = 1024
TOP = 1
TOK_DEV = 128
EXPERTS = 32
CAP = 6
TOKENS = 16384
N_DP = 4
N_EXPERT = 32


def block_scale(key, shape, shards, low, high):
    gain = 1.0
    for dim, shards_of in shards:
        draws = jax.random.uniform(jax.random.fold_in(jax.random.fold_in(key, 6), dim), (shards_of,), jnp.float32, low / len(shards), high / len(shards))
        gain = gain * jnp.repeat(jnp.exp(draws), shape[dim] // shards_of).reshape((-1,) + (1,) * (len(shape) - 1 - dim))
    return gain


def shared_out(rng, own, number, rows, amount, top, bound, lean):
    sequence = jax.random.permutation(rng, amount)
    crowded, ordinary = load_shares(amount, rows * top, bound, lean, True), load_shares(amount, rows * top, bound, lean, False)
    places = jnp.arange(amount)

    def named(tallies, rotation):
        used = int((tallies > 0).sum())
        fixed = max(1, used // 4)
        passed = fixed + (places - fixed + rotation * (used - fixed)) % max(1, amount - fixed)
        return jnp.zeros((amount,), jnp.int32).at[sequence[jnp.where(places < fixed, places, passed)]].set(jnp.asarray(tallies, jnp.int32))

    tallies = jnp.where(number % 4 == 0, named(crowded, number // 4), named(ordinary, number - number // 4 - 1))
    mixed = jax.random.permutation(jax.random.fold_in(own, 3), amount)
    giver, receiver = mixed[0:amount // 2 * 2:2], mixed[1:amount // 2 * 2:2]
    room = jnp.minimum(tallies[giver] - 1, bound - tallies[receiver]) // 2
    room = jnp.where((giver == sequence[0]) | (receiver == sequence[0]) | (tallies[receiver] == 0), 0, jnp.maximum(room, 0))
    passed = jax.random.randint(jax.random.fold_in(own, 4), (amount // 2,), 0, 1 << 20) % (room + 1)
    tallies = tallies.at[giver].add(-passed).at[receiver].add(passed)
    members = jnp.searchsorted(jnp.cumsum(tallies), jnp.arange(rows * top), side="right").astype(jnp.int32)
    table = members.reshape(top, rows).T
    table = table[jax.random.permutation(jax.random.fold_in(own, 1), rows)]
    rotation = jax.random.randint(jax.random.fold_in(own, 2), (rows, 1), 0, top)
    return jnp.take_along_axis(table, (jnp.arange(top)[None, :] + rotation) % top, axis=1)


def load_shares(amount, total, bound, slope, full):
    weights = [(1 << 20) // math.isqrt(standing ** slope) + 1 for standing in range(1, amount + 1)]
    largest = bound if full else min(bound, max(-(-total // amount), total * weights[0] // sum(weights)))
    least = 1 if total - largest >= amount - 1 else 0
    counts, rest = [largest] + [least] * (amount - 1), total - largest - least * (amount - 1)
    while rest > 0:
        candidates = [i for i in range(1, amount) if counts[i] < largest] or [i for i in range(1, amount) if counts[i] < bound]
        mass, left = sum([weights[i] for i in candidates]), rest
        for i in candidates:
            extra = min(bound - counts[i], max(1, left * weights[i] // mass), rest)
            counts[i] = counts[i] + extra
            rest = rest - extra
    return np.array(counts)


def scatter_about(stream_key, shape, deviation, most, cuts=(), held_as=jnp.bfloat16):
    result = deviation * jax.random.normal(stream_key, shape, jnp.float32)
    if cuts:
        result = result * block_scale(stream_key, shape, cuts, -0.22, 0.18)
    return jnp.clip(result, -most, most).astype(held_as)


def setup_inputs(seed: int = 0) -> dict:
    streams_of = jax.random.split(jax.random.key(seed), 9)
    tokens = scatter_about(streams_of[0], (TOKENS, D), 1.0, 6.0, ((0, 128),))
    grad_out = scatter_about(streams_of[1], (TOKENS, D), 1.0, 6.0, ((0, 128),))
    routes_keys = jax.random.split(jax.random.fold_in(streams_of[2], 1), TOKENS // TOK_DEV)
    routes_turns = jax.random.permutation(jax.random.fold_in(streams_of[2], 3), TOKENS // TOK_DEV)
    routes = jax.vmap(lambda own, number: shared_out(jax.random.fold_in(streams_of[2], 2), own, number, TOK_DEV, EXPERTS, TOP, CAP, 1))(routes_keys, routes_turns).reshape((TOKENS, TOP))
    gate_prob = jnp.clip(0.1 + 0.9 * jax.random.uniform(streams_of[3], (TOKENS, TOP), jnp.float32) ** block_scale(streams_of[3], (TOKENS, TOP), ((0, 128),), -0.2, 0.2), 0.1, 1.0)
    w_gate = scatter_about(streams_of[4], (EXPERTS, D, HID), D ** -0.5, 0.0625, ((0, 32), (2, 4)))
    w_up = scatter_about(streams_of[5], (EXPERTS, D, HID), D ** -0.5, 0.0625, ((0, 32), (2, 4)))
    w_down = scatter_about(streams_of[6], (EXPERTS, HID, D), HID ** -0.5, 0.1875, ((0, 32), (1, 4)))
    moment_prev = jnp.clip(jnp.exp(math.log(200.0) - 3.6888795 * jax.random.uniform(streams_of[7], (EXPERTS, HID), jnp.float32) ** block_scale(streams_of[7], (EXPERTS, HID), ((0, 32), (1, 4)), -0.2, 0.2)), 5.0, 200.0)
    return dict(tokens=tokens, grad_out=grad_out, routes=routes, gate_prob=gate_prob, w_gate=w_gate, w_up=w_up, w_down=w_down, moment_prev=moment_prev)


moment_decay = 0.95
epsilon = 1e-08

def reference(tokens, grad_out, routes, gate_prob, w_gate, w_up, w_down, moment_prev):
    device_count = N_DP * N_EXPERT
    per_device = TOK_DEV * TOP
    route_total = TOKENS * TOP
    buffer_rows = device_count * CAP
    flat_expert = routes.reshape(device_count, per_device).astype(jnp.int32)
    onehot = (flat_expert[:, :, None] == jnp.arange(EXPERTS, dtype=jnp.int32)[None, None, :]).astype(jnp.int32)
    slot_index = lax.optimization_barrier(jnp.sum((jnp.cumsum(onehot, axis=1) - onehot) * onehot, axis=2))
    position = jnp.arange(device_count, dtype=jnp.int32)[:, None] * CAP + slot_index
    route_id = jnp.arange(route_total, dtype=jnp.int32)
    slot_table = jnp.full((EXPERTS, buffer_rows), route_total, dtype=jnp.int32)
    slot_table = slot_table.at[flat_expert.reshape(-1), position.reshape(-1)].set(route_id)
    zero_row = jnp.zeros((1, D), jnp.bfloat16)
    route_rows = jnp.concatenate([jnp.repeat(tokens, TOP, axis=0), zero_row], axis=0)
    scaled = jnp.repeat(grad_out, TOP, axis=0).astype(jnp.float32) * gate_prob.reshape(route_total, 1)
    route_cot = jnp.concatenate([scaled.astype(jnp.bfloat16), zero_row], axis=0)
    quarter = HID // N_DP

    def one_expert(route_grad, pieces):
        table_row, gate_w, up_w, down_w, moment_old = pieces
        rows_in = route_rows[table_row]
        cot_in = route_cot[table_row]
        gate_pre = jnp.dot(rows_in, gate_w, preferred_element_type=jnp.float32)
        up_pre = jnp.dot(rows_in, up_w, preferred_element_type=jnp.float32)
        gate_sig = jax.nn.sigmoid(gate_pre)
        silu_gate = gate_pre * gate_sig
        hidden = (silu_gate * up_pre).astype(jnp.bfloat16)
        hidden_grad = jnp.dot(cot_in, down_w.T, preferred_element_type=jnp.float32)
        gate_grad = (hidden_grad * up_pre * gate_sig * (1.0 + gate_pre * (1.0 - gate_sig))).astype(jnp.bfloat16)
        up_grad = (hidden_grad * silu_gate).astype(jnp.bfloat16)
        partial_sum = jnp.zeros((buffer_rows, D), jnp.float32)
        for part_index in range(N_DP):
            hidden_span = slice(part_index * quarter, (part_index + 1) * quarter)
            term = jnp.dot(gate_grad[:, hidden_span], gate_w[:, hidden_span].T, preferred_element_type=jnp.float32)
            term = term + jnp.dot(up_grad[:, hidden_span], up_w[:, hidden_span].T, preferred_element_type=jnp.float32)
            term = lax.optimization_barrier(term.astype(jnp.bfloat16))
            partial_sum = partial_sum + term.astype(jnp.float32)
        route_grad = route_grad.at[table_row].add(partial_sum)
        down_wgrad = jnp.dot(hidden.T, cot_in, preferred_element_type=jnp.float32)
        gate_wgrad = jnp.dot(rows_in.T, gate_grad, preferred_element_type=jnp.float32)
        up_wgrad = jnp.dot(rows_in.T, up_grad, preferred_element_type=jnp.float32)
        mean_square = (lax.optimization_barrier(jnp.sum(gate_wgrad * gate_wgrad, axis=0)) + lax.optimization_barrier(jnp.sum(up_wgrad * up_wgrad, axis=0)) + lax.optimization_barrier(jnp.sum(down_wgrad * down_wgrad, axis=1))) / (3.0 * D)
        second_moment = moment_decay * moment_old + (1.0 - moment_decay) * mean_square
        down_update = (down_wgrad / (jnp.sqrt(second_moment)[:, None] + epsilon)).astype(jnp.bfloat16)
        return (route_grad, (down_update, second_moment))
    initial = jnp.zeros((route_total + 1, D), jnp.float32)
    route_grad, outputs = lax.scan(one_expert, initial, (slot_table, w_gate, w_up, w_down, moment_prev))
    down_update, second_moment = outputs
    grad_in = lax.optimization_barrier(jnp.sum(route_grad[:route_total].reshape(TOKENS, TOP, D), axis=1)).astype(jnp.bfloat16)
    return (grad_in, down_update, second_moment)
```

```python
import functools

import jax
import jax.numpy as jnp
from jax import lax
from jax.experimental import pallas as pl
from jax.experimental.pallas import tpu as pltpu
from jax.sharding import PartitionSpec as P

MESH = pl.DeviceIdType.MESH
BF = jnp.bfloat16
F32 = jnp.float32

moment_decay = 0.95
epsilon = 1e-08

D = 7168
TOK = 128
CAP = 6
Q = 256
ROWS = 192
HALF = 96
BLK = 48
CW = 1024
NCH = D // CW
SUB = 256
PARTNERS = (
    (0, 0, 0, 1),
    (0, 1, 0, 0),
    (0, 2, 0, 0),
    (0, 3, 0, 0),
    (0, 0, 1, 0),
    (0, 0, 2, 0),
    (0, 0, 3, 0),
    (1, 0, 0, 0),
    (3, 0, 0, 0),
)


def place():
    y = lax.axis_index("dp")
    e = lax.axis_index("expert")
    return y, e // 8, (e // 2) % 4, e % 2


def peer(here, dy, dz, dx, dc):
    y, z, x, c = here
    expert = (((z + dz) % 4) * 4 + (x + dx) % 4) * 2 + (c + dc) % 2
    return {"dp": (y + dy) % 4, "expert": expert}


def remote(src, dst, send, recv, device):
    return pltpu.make_async_remote_copy(
        src_ref=src,
        dst_ref=dst,
        send_sem=send,
        recv_sem=recv,
        device_id=device,
        device_id_type=MESH,
    )


def greet(here):
    barrier = pltpu.get_barrier_semaphore()
    for offset in PARTNERS:
        pl.semaphore_signal(barrier, inc=1, device_id=peer(here, *offset), device_id_type=MESH)
    pl.semaphore_wait(barrier, len(PARTNERS))


def at(index, size, align):
    return pl.ds(pl.multiple_of(index * size, align), size)


def cols(k):
    return at(k, CW, 128)


def tile(k, j):
    return pl.ds(pl.multiple_of(k * CW + j * SUB, 128), SUB)


def nt(a, b):
    return lax.dot_general(a, b, (((1,), (1,)), ((), ())), preferred_element_type=F32)


def tn(a, b):
    return lax.dot_general(a, b, (((0,), (0,)), ((), ())), preferred_element_type=F32)


def nn(a, b):
    return jnp.dot(a, b, preferred_element_type=F32)


def forward_kernel(
    meta_ref,
    perm_ref,
    tok_ref,
    cot_ref,
    wg_hbm,
    wu_hbm,
    wd_hbm,
    rows,
    acts,
    acts_t,
    sel_ref,
    metas,
    gp_ref,
    raw,
    zs,
    za,
    xs,
    stage,
    acc,
    wg,
    wu,
    wd,
    w_sem,
    m_sem,
    raw_l,
    raw_s,
    raw_r,
    z_s,
    z_r,
    x_s,
    x_r,
    x_l,
    y_s,
    y_r,
    f_s,
    f_r,
    st_l,
):
    here = place()
    y, z, x, c = here
    sources = (tok_ref, cot_ref)
    greet(here)

    meta_copy = remote(meta_ref, metas.at[c], m_sem.at[0], m_sem.at[1], peer(here, 0, 0, 0, 1))
    meta_copy.start()
    metas[pl.ds(c, 1)] = meta_ref[...][None]

    def raw_local(a, k):
        return pltpu.make_async_copy(
            sources[a].at[:, cols(k)], raw.at[a, at(c, TOK, TOK), cols(k)], raw_l.at[a, k]
        )

    def raw_remote(a, k):
        return remote(
            sources[a].at[:, cols(k)],
            raw.at[a, at(c, TOK, TOK), cols(k)],
            raw_s.at[a, k],
            raw_r.at[a, k],
            peer(here, 0, 0, 0, 1),
        )

    for k in range(NCH):
        for a in range(2):
            raw_local(a, k).start()
            raw_remote(a, k).start()
    weights = [
        pltpu.make_async_copy(src, dst, w_sem.at[i])
        for i, (src, dst) in enumerate(((wg_hbm, wg), (wu_hbm, wu), (wd_hbm, wd)))
    ]
    for copy in weights:
        copy.start()

    acc[...] = jnp.zeros_like(acc)
    meta_copy.wait()

    earlier = (
        lax.broadcasted_iota(jnp.int32, (TOK, TOK), 0)
        < lax.broadcasted_iota(jnp.int32, (TOK, TOK), 1)
    ).astype(F32).astype(BF)
    gp = jnp.zeros((ROWS, 1), F32)
    for m in range(2):
        route = metas[m, 0:1, :].astype(jnp.int32)
        prob = metas[m, 1:2, :]
        onehot = (lax.broadcasted_iota(jnp.int32, (32, TOK), 0) == route).astype(F32)
        before = nn(onehot.astype(BF), earlier)
        slot = jnp.sum(onehot * before, axis=0, keepdims=True).astype(jnp.int32)
        row = ((route >> 1) * 2 + m) * CAP + slot
        row = jnp.where((route & 1) == c, row, -1)
        chosen = lax.broadcasted_iota(jnp.int32, (ROWS, TOK), 0) == row
        sel_ref[:, m * TOK : (m + 1) * TOK] = chosen.astype(F32).astype(BF)
        gp = gp + jnp.sum(jnp.where(chosen, prob, 0.0), axis=1, keepdims=True)
    gp_ref[...] = jnp.broadcast_to(gp, (ROWS, 128))

    def z_copy(a, k, d):
        return remote(
            zs.at[a, k % 2, at((z + d) % 4, BLK, 16), :],
            za.at[a, at(z, BLK, 16), cols(k)],
            z_s.at[a, k % 2, d - 1],
            z_r.at[a, k, d - 1],
            peer(here, 0, d, 0, 0),
        )

    def x_copy(a, k, d):
        return remote(
            xs.at[a, k % 2, at((x + d) % 4, BLK, 16), :],
            rows.at[a, y, at(x, BLK, 16), cols(k)],
            x_s.at[a, k % 2, d - 1],
            x_r.at[a, k, d - 1],
            peer(here, 0, 0, d, 0),
        )

    def x_own(a, k):
        return pltpu.make_async_copy(
            xs.at[a, k % 2, at(x, BLK, 16), :],
            rows.at[a, y, at(x, BLK, 16), cols(k)],
            x_l.at[a, k % 2],
        )

    def y_copy(a, k, i):
        return remote(
            rows.at[a, y, :, cols(k)],
            rows.at[a, y, :, cols(k)],
            y_s.at[a, k, i],
            y_r.at[a, k, i],
            peer(here, 1 if i == 0 else 3, 0, 0, 0),
        )

    def f_copy(a, k, i):
        src = (y + (3 if i == 0 else 1)) % 4
        half = rows.at[a, src, pl.ds(i * HALF, HALF), cols(k)]
        return remote(
            half, half, f_s.at[a, k, i], f_r.at[a, k, i], peer(here, 1 if i == 0 else 3, 0, 0, 0)
        )

    def stage_copy(a, k):
        return pltpu.make_async_copy(
            rows.at[a, :, :, cols(k)], stage.at[a, k % 2], st_l.at[a, k % 2]
        )

    def when(k, body):
        pl.when((k >= 0) & (k < NCH))(lambda: body(k))

    def drain(copy, count, first):
        def body(k):
            for a in range(2):
                for i in range(count):
                    copy(a, k, first + i).wait_send()

        return body

    def select(k):
        for a in range(2):
            raw_local(a, k).wait()
            raw_remote(a, k).wait()
            for j in range(CW // SUB):
                picked = nn(sel_ref[...], raw[a, :, tile(k, j)])
                if a == 1:
                    picked = picked * gp_ref[:, 0:1]
                zs[a, k % 2, :, j * SUB : (j + 1) * SUB] = picked.astype(BF)
            for d in (2, 1, 3):
                z_copy(a, k, d).start()
            za[a, at(z, BLK, 16), cols(k)] = zs[a, k % 2, at(z, BLK, 16), :]

    def turn(k):
        for a in range(2):
            for d in (1, 2, 3):
                z_copy(a, k, d).wait_recv()
            for j in range(CW // SUB):
                xs[a, k % 2, :, j * SUB : (j + 1) * SUB] = nn(
                    perm_ref[...], za[a, :, tile(k, j)]
                ).astype(BF)
            for d in (2, 1, 3):
                x_copy(a, k, d).start()
            x_own(a, k).start()

    def spread(k):
        for a in range(2):
            for d in (1, 2, 3):
                x_copy(a, k, d).wait_recv()
            x_own(a, k).wait()
            for i in range(2):
                y_copy(a, k, i).start()

    def pass_on(k):
        for a in range(2):
            for i in range(2):
                y_copy(a, k, i).wait_recv()
                f_copy(a, k, i).start()

    def fetch(k):
        for a in range(2):
            for i in range(2):
                f_copy(a, k, i).wait_recv()
            stage_copy(a, k).start()

    def accumulate(k):
        @pl.when(k == 0)
        def _():
            for copy in weights:
                copy.wait()

        for a in range(2):
            stage_copy(a, k).wait()

        def block(b, carry):
            block_rows = at(b, ROWS, 16)
            tokens = stage[0, k % 2, b]
            acc[0, block_rows, :] += nn(tokens, wg[cols(k), :])
            acc[1, block_rows, :] += nn(tokens, wu[cols(k), :])
            acc[2, block_rows, :] += nt(stage[1, k % 2, b], wd[:, cols(k)])
            return carry

        lax.fori_loop(0, 4, block, 0)

    def step(t, carry):
        when(t - 2, drain(z_copy, 3, 1))
        when(t - 3, drain(x_copy, 3, 1))
        when(t - 4, drain(y_copy, 2, 0))
        when(t - 5, drain(f_copy, 2, 0))
        when(t, select)
        when(t - 1, turn)
        when(t - 2, spread)
        when(t - 3, pass_on)
        when(t - 4, fetch)
        when(t - 5, accumulate)
        return carry

    lax.fori_loop(0, NCH + 5, step, 0)

    def finish(b, carry):
        part = at(b, Q, 256)
        gate, up, grad = acc[0, part, :], acc[1, part, :], acc[2, part, :]
        sig = jax.nn.sigmoid(gate)
        silu = gate * sig
        hidden = silu * up
        gate_grad = grad * up * sig * (1.0 + gate * (1.0 - sig))
        up_grad = grad * silu
        acts[0, part, :] = gate_grad.astype(BF)
        acts[1, part, :] = up_grad.astype(BF)
        acts_t[0, :, part] = hidden.T.astype(BF)
        acts_t[1, :, part] = gate_grad.T.astype(BF)
        acts_t[2, :, part] = up_grad.T.astype(BF)
        return carry

    lax.fori_loop(0, 3, finish, 0)


def backward_kernel(
    acts,
    acts_t,
    sel_ref,
    perm_ref,
    rows,
    wg_hbm,
    wu_hbm,
    moment_ref,
    grad_ref,
    update_ref,
    second_ref,
    far,
    relay,
    near,
    summed,
    xs,
    xa,
    zs,
    za,
    cs,
    co,
    cr,
    stage,
    dw,
    squares,
    wg,
    wu,
    w_sem,
    p_s,
    p_r,
    n_s,
    n_r,
    x_s,
    x_r,
    z_s,
    z_r,
    c_s,
    c_r,
    st_l,
):
    here = place()
    y, z, x, c = here
    greet(here)
    weights = [
        pltpu.make_async_copy(src, dst, w_sem.at[i])
        for i, (src, dst) in enumerate(((wg_hbm, wg), (wu_hbm, wu)))
    ]
    for copy in weights:
        copy.start()

    def stage_copy(a, k):
        return pltpu.make_async_copy(
            rows.at[a, :, :, cols(k)], stage.at[a, k % 2], st_l.at[a, k % 2]
        )

    for a in range(2):
        stage_copy(a, 0).start()
    squares[...] = jnp.zeros_like(squares)
    for copy in weights:
        copy.wait()

    def partial(block, k, j):
        block_rows = at(block, ROWS, 16)
        total = nt(acts[0, block_rows, :], wg[tile(k, j), :])
        total = total + nt(acts[1, block_rows, :], wu[tile(k, j), :])
        return total.astype(BF).astype(F32)

    def p_copy(k, i):
        return remote(
            far.at[k % 2, pl.ds(i * HALF, HALF), :],
            relay.at[i, :, cols(k)],
            p_s.at[k % 2, i],
            p_r.at[k, i],
            peer(here, 1 if i == 0 else 3, 0, 0, 0),
        )

    def n_copy(k, i):
        return remote(
            near.at[i, k % 2],
            summed.at[i, :, cols(k)],
            n_s.at[k % 2, i],
            n_r.at[k, i],
            peer(here, 1 if i == 0 else 3, 0, 0, 0),
        )

    def x_copy(k, d):
        return remote(
            xs.at[k % 2, at((x + d) % 4, BLK, 16), :],
            xa.at[at(x, BLK, 16), cols(k)],
            x_s.at[k % 2, d - 1],
            x_r.at[k, d - 1],
            peer(here, 0, 0, d, 0),
        )

    def z_copy(k, d):
        return remote(
            zs.at[k % 2, at((z + d) % 4, BLK, 16), :],
            za.at[at(z, BLK, 16), cols(k)],
            z_s.at[k % 2, d - 1],
            z_r.at[k, d - 1],
            peer(here, 0, d, 0, 0),
        )

    def c_copy(k):
        return remote(
            cs.at[k % 2], cr.at[:, cols(k)], c_s.at[k % 2], c_r.at[k], peer(here, 0, 0, 0, 1)
        )

    def when(k, body):
        pl.when((k >= 0) & (k < NCH))(lambda: body(k))

    def drain(copy, count, first):
        def body(k):
            for i in range(count):
                copy(k, first + i).wait_send()

        return body

    def send_far(k):
        for j in range(CW // SUB):
            far[k % 2, :, j * SUB : (j + 1) * SUB] = partial((y + 2) % 4, k, j).astype(BF)
        for i in range(2):
            p_copy(k, i).start()

    def send_near(k):
        for i in range(2):
            p_copy(k, i).wait_recv()
            for j in range(CW // SUB):
                out = pl.ds(j * SUB, SUB)
                term = partial((y + (1 if i == 0 else 3)) % 4, k, j)
                arrived = relay[i, :, tile(k, j)].astype(F32)
                if i == 0:
                    near[i, k % 2, 0:HALF, out] = (term[0:HALF] + arrived).astype(BF)
                    near[i, k % 2, HALF:ROWS, out] = term[HALF:ROWS].astype(BF)
                else:
                    near[i, k % 2, 0:HALF, out] = term[0:HALF].astype(BF)
                    near[i, k % 2, HALF:ROWS, out] = (term[HALF:ROWS] + arrived).astype(BF)
            n_copy(k, i).start()

    def total(k):
        for i in range(2):
            n_copy(k, i).wait_recv()
        for j in range(CW // SUB):
            whole = partial(y, k, j)
            whole = whole + summed[0, :, tile(k, j)].astype(F32)
            whole = whole + summed[1, :, tile(k, j)].astype(F32)
            xs[k % 2, :, j * SUB : (j + 1) * SUB] = whole.astype(BF)
        for d in (2, 1, 3):
            x_copy(k, d).start()
        xa[at(x, BLK, 16), cols(k)] = xs[k % 2, at(x, BLK, 16), :]

    def turn(k):
        for d in (1, 2, 3):
            x_copy(k, d).wait_recv()
        for j in range(CW // SUB):
            zs[k % 2, :, j * SUB : (j + 1) * SUB] = nn(perm_ref[...], xa[:, tile(k, j)]).astype(BF)
        for d in (2, 1, 3):
            z_copy(k, d).start()
        za[at(z, BLK, 16), cols(k)] = zs[k % 2, at(z, BLK, 16), :]

    def unselect(k):
        for d in (1, 2, 3):
            z_copy(k, d).wait_recv()
        for j in range(CW // SUB):
            out = pl.ds(j * SUB, SUB)
            block = za[:, tile(k, j)]
            cs[k % 2, :, out] = tn(sel_ref[:, at(1 - c, TOK, TOK)], block).astype(BF)
            co[k % 2, :, out] = tn(sel_ref[:, at(c, TOK, TOK)], block).astype(BF)
        c_copy(k).start()

    def join(k):
        c_copy(k).wait()
        mine = co[k % 2].astype(F32) + cr[:, cols(k)].astype(F32)
        grad_ref[:, cols(k)] = mine.astype(BF)

    def weight_grads(k):
        for a in range(2):
            stage_copy(a, k).wait()

        @pl.when(k + 1 < NCH)
        def _():
            for a in range(2):
                stage_copy(a, k + 1).start()

        for j in range(CW // SUB):
            out = slice(j * SUB, (j + 1) * SUB)
            cot_rows = stage[1, k % 2, :, :, out].reshape(4 * ROWS, SUB)
            tok_rows = stage[0, k % 2, :, :, out].reshape(4 * ROWS, SUB)
            down = nn(acts_t[0], cot_rows)
            dw[:, tile(k, j)] = down
            gate = nn(acts_t[1], tok_rows)
            up = nn(acts_t[2], tok_rows)
            sq = down * down + gate * gate + up * up
            squares[...] += sq[:, 0:128] + sq[:, 128:256]

    def update(k):
        @pl.when(k == 0)
        def _():
            mean = jnp.sum(squares[...], axis=1, keepdims=True) / (3.0 * D)
            second = moment_decay * moment_ref[...] + (1.0 - moment_decay) * mean
            second_ref[...] = second
            squares[...] = jnp.broadcast_to(1.0 / (jnp.sqrt(second) + epsilon), squares.shape)

        for j in range(CW // 128):
            out = pl.ds(pl.multiple_of(k * CW + j * 128, 128), 128)
            update_ref[:, out] = (dw[:, out] * squares[...]).astype(BF)

    def step(t, carry):
        when(t - 2, drain(p_copy, 2, 0))
        when(t - 3, drain(n_copy, 2, 0))
        when(t - 4, drain(x_copy, 3, 1))
        when(t - 5, drain(z_copy, 3, 1))
        when(t, send_far)
        when(t - 1, send_near)
        when(t - 2, total)
        when(t - 3, turn)
        when(t - 4, unselect)
        when(t - 5, join)
        when(t, weight_grads)
        when((t - NCH) * 2, update)
        when((t - NCH) * 2 + 1, update)
        return carry

    lax.fori_loop(0, NCH + 5, step, 0)


def shards(tokens, grad_out, routes, gate_prob, w_gate, w_up, w_down, moment_prev):
    meta = jnp.concatenate(
        [routes.reshape(1, TOK).astype(F32), gate_prob.reshape(1, TOK), jnp.zeros((6, TOK), F32)]
    )
    index = jnp.arange(ROWS)
    swapped = (index % BLK) // 12 * BLK + index // BLK * 12 + index % 12
    perm = (swapped[:, None] == index[None, :]).astype(BF)
    vmem = pl.BlockSpec(memory_space=pltpu.VMEM)
    hbm = pl.BlockSpec(memory_space=pltpu.HBM)
    dma = pltpu.SemaphoreType.DMA
    rows, acts, acts_t, sel = pl.pallas_call(
        forward_kernel,
        name="dispatch",
        out_shape=(
            jax.ShapeDtypeStruct((2, 4, ROWS, D), BF),
            jax.ShapeDtypeStruct((2, 4 * ROWS, Q), BF),
            jax.ShapeDtypeStruct((3, Q, 4 * ROWS), BF),
            jax.ShapeDtypeStruct((ROWS, 2 * TOK), BF),
        ),
        in_specs=[vmem, vmem, hbm, hbm, hbm, hbm, hbm],
        out_specs=(hbm, vmem, vmem, vmem),
        scratch_shapes=[
            pltpu.VMEM((2, 8, TOK), F32),
            pltpu.VMEM((ROWS, 128), F32),
            pltpu.VMEM((2, 2 * TOK, D), BF),
            pltpu.VMEM((2, 2, ROWS, CW), BF),
            pltpu.VMEM((2, ROWS, D), BF),
            pltpu.VMEM((2, 2, ROWS, CW), BF),
            pltpu.VMEM((2, 2, 4, ROWS, CW), BF),
            pltpu.VMEM((3, 4 * ROWS, Q), F32),
            pltpu.VMEM((D, Q), BF),
            pltpu.VMEM((D, Q), BF),
            pltpu.VMEM((Q, D), BF),
            dma((3,)),
            dma((2,)),
            dma((2, NCH)),
            dma((2, NCH)),
            dma((2, NCH)),
            dma((2, 2, 3)),
            dma((2, NCH, 3)),
            dma((2, 2, 3)),
            dma((2, NCH, 3)),
            dma((2, 2)),
            dma((2, NCH, 2)),
            dma((2, NCH, 2)),
            dma((2, NCH, 2)),
            dma((2, NCH, 2)),
            dma((2, 2)),
        ],
        compiler_params=pltpu.CompilerParams(
            collective_id=0, has_side_effects=True, vmem_limit_bytes=60 * 2**20
        ),
    )(meta, perm, tokens, grad_out, w_gate[0], w_up[0], w_down[0])
    grad_in, update, second = pl.pallas_call(
        backward_kernel,
        name="combine",
        out_shape=(
            jax.ShapeDtypeStruct((TOK, D), BF),
            jax.ShapeDtypeStruct((Q, D), BF),
            jax.ShapeDtypeStruct((Q, 1), F32),
        ),
        in_specs=[vmem, vmem, vmem, vmem, hbm, hbm, hbm, vmem],
        out_specs=(vmem, vmem, vmem),
        scratch_shapes=[
            pltpu.VMEM((2, ROWS, CW), BF),
            pltpu.VMEM((2, HALF, D), BF),
            pltpu.VMEM((2, 2, ROWS, CW), BF),
            pltpu.VMEM((2, ROWS, D), BF),
            pltpu.VMEM((2, ROWS, CW), BF),
            pltpu.VMEM((ROWS, D), BF),
            pltpu.VMEM((2, ROWS, CW), BF),
            pltpu.VMEM((ROWS, D), BF),
            pltpu.VMEM((2, TOK, CW), BF),
            pltpu.VMEM((2, TOK, CW), BF),
            pltpu.VMEM((TOK, D), BF),
            pltpu.VMEM((2, 2, 4, ROWS, CW), BF),
            pltpu.VMEM((Q, D), F32),
            pltpu.VMEM((Q, 128), F32),
            pltpu.VMEM((D, Q), BF),
            pltpu.VMEM((D, Q), BF),
            dma((2,)),
            dma((2, 2)),
            dma((NCH, 2)),
            dma((2, 2)),
            dma((NCH, 2)),
            dma((2, 3)),
            dma((NCH, 3)),
            dma((2, 3)),
            dma((NCH, 3)),
            dma((2,)),
            dma((NCH,)),
            dma((2, 2)),
        ],
        compiler_params=pltpu.CompilerParams(
            collective_id=1, has_side_effects=True, vmem_limit_bytes=60 * 2**20
        ),
    )(acts, acts_t, sel, perm, rows, w_gate[0], w_up[0], moment_prev.reshape(Q, 1))
    return grad_in, update[None], second.reshape(1, Q)


def solution(mesh):
    placed = (
        P(("dp", "expert"), None),
        P(("dp", "expert"), None),
        P(("dp", "expert"), None),
        P(("dp", "expert"), None),
        P("expert", None, "dp"),
        P("expert", None, "dp"),
        P("expert", "dp", None),
        P("expert", "dp"),
    )
    return jax.shard_map(
        shards,
        mesh=mesh,
        in_specs=placed,
        out_specs=(P(("dp", "expert"), None), P("expert", "dp", None), P("expert", "dp")),
        check_vma=False,
    )
```

```python
import functools

import jax
import jax.numpy as jnp
from jax import lax
from jax.experimental import pallas as pl
from jax.experimental.pallas import tpu as pltpu
from jax.sharding import PartitionSpec as P

MESH = pl.DeviceIdType.MESH
BF = jnp.bfloat16
F32 = jnp.float32

moment_decay = 0.95
epsilon = 1e-08

D = 7168
TOK = 128
CAP = 6
Q = 256
ROWS = 192
BLK = 48
SUB = 256

FW = 512
FC = D // FW
F_EARLY = 12
F_LATE = 2 * FC - F_EARLY
BW = 512
BC = D // BW
B_EARLY = 6
B_LATE = BC - B_EARLY

ACROSS = ((0, 0, 0, 1),) + tuple((0, d, 0, 0) for d in (1, 2, 3)) + tuple((0, 0, d, 0) for d in (1, 2, 3))
COLUMN = ((1, 0, 0, 0), (3, 0, 0, 0), (2, 0, 0, 0), (1, 0, 0, 1), (3, 0, 0, 1), (2, 0, 0, 1))
PLUS_MINUS = (1, 3)


def place():
    y = lax.axis_index("dp")
    e = lax.axis_index("expert")
    return y, e // 8, (e // 2) % 4, e % 2


def peer(here, dy, dz, dx, dc):
    y, z, x, c = here
    expert = (((z + dz) % 4) * 4 + (x + dx) % 4) * 2 + (c + dc) % 2
    return {"dp": (y + dy) % 4, "expert": expert}


def remote(src, dst, send, recv, device):
    return pltpu.make_async_remote_copy(
        src_ref=src,
        dst_ref=dst,
        send_sem=send,
        recv_sem=recv,
        device_id=device,
        device_id_type=MESH,
    )


def greet(here, partners):
    barrier = pltpu.get_barrier_semaphore()
    for offset in partners:
        pl.semaphore_signal(barrier, inc=1, device_id=peer(here, *offset), device_id_type=MESH)
    pl.semaphore_wait(barrier, len(partners))


def at(index, size, align):
    return pl.ds(pl.multiple_of(index * size, align), size)


def nt(a, b):
    return lax.dot_general(a, b, (((1,), (1,)), ((), ())), preferred_element_type=F32)


def tn(a, b):
    return lax.dot_general(a, b, (((0,), (0,)), ((), ())), preferred_element_type=F32)


def nn(a, b):
    return jnp.dot(a, b, preferred_element_type=F32)


def tiles(width):
    return [slice(j, j + SUB) for j in range(0, width, SUB)]


def swap_matrix():
    out = lax.broadcasted_iota(jnp.int32, (ROWS, ROWS), 0)
    row = lax.broadcasted_iota(jnp.int32, (ROWS, ROWS), 1)

    def steps(value, size):
        return sum((value >= size * n).astype(jnp.int32) for n in (1, 2, 3))

    outer = steps(out, 48)
    inner = steps(out - 48 * outer, 12)
    return (row - out == 36 * (inner - outer)).astype(F32).astype(BF)


def when(k, count, body):
    pl.when((k >= 0) & (k < count))(lambda: body(k))


def forward_kernel(
    routes_ref,
    prob_ref,
    tok_ref,
    cot_ref,
    wg_hbm,
    wu_hbm,
    wd_hbm,
    rows,
    acts,
    acts_t,
    sel,
    metas,
    gp,
    perm,
    raw,
    zs,
    za,
    xs,
    raw4,
    zs4,
    za4,
    xs4,
    stage,
    stage4,
    acc,
    wg,
    wu,
    wd,
    w_sem,
    m_s,
    m_r,
    raw_l,
    raw_s,
    raw_r,
    z_s,
    z_r,
    x_s,
    x_r,
    x_l,
    y_s,
    y_r,
    f_s,
    f_r,
    st_l,
    own_l,
    own_s,
    own_r,
    yy_s,
    yy_r,
    ff_s,
    ff_r,
    cc_s,
    cc_r,
    zz_s,
    zz_r,
    xx_s,
    xx_r,
    xx_l,
    st4_l,
):
    here = place()
    y, z, x, c = here
    sources = (tok_ref, cot_ref)
    mine = at(c, TOK, TOK)

    def cols(k):
        return at(k, FW, 128)

    greet(here, ACROSS + COLUMN)

    first = lax.broadcasted_iota(jnp.int32, (8, TOK), 0) == 0
    metas[y, c] = jnp.where(first, routes_ref[...].astype(F32), prob_ref[...])
    others = COLUMN + ((0, 0, 0, 1),)

    def meta_copy(i):
        return remote(
            metas.at[y, c], metas.at[y, c], m_s.at[i], m_r.at[i], peer(here, *others[i])
        )

    for i in range(len(others)):
        meta_copy(i).start()

    def yy_copy(k, i):
        return remote(
            cot_ref.at[:, cols(k)],
            raw4.at[k, y, mine, :],
            yy_s.at[k, i],
            yy_r.at[k, i],
            peer(here, PLUS_MINUS[i], 0, 0, 0),
        )

    def ff_copy(k, i):
        src = (y + PLUS_MINUS[1 - i]) % 4
        half = raw4.at[k, src, pl.ds(pl.multiple_of(c * TOK + i * 64, 64), 64), :]
        return remote(
            half, half, ff_s.at[k, i], ff_r.at[k, i], peer(here, PLUS_MINUS[i], 0, 0, 0)
        )

    def cc_copy(k, i):
        block = raw4.at[k, (y + (3, 1, 2)[i]) % 4, mine, :]
        return remote(block, block, cc_s.at[k, i], cc_r.at[k, i], peer(here, 0, 0, 0, 1))

    def own_local(k):
        return pltpu.make_async_copy(
            cot_ref.at[:, cols(k)], raw4.at[k, y, mine, :], own_l.at[k]
        )

    def own_remote(k):
        return remote(
            cot_ref.at[:, cols(k)],
            raw4.at[k, y, mine, :],
            own_s.at[k],
            own_r.at[k],
            peer(here, 0, 0, 0, 1),
        )

    def zz_copy(k, d):
        return remote(
            zs4.at[k % 2, :, at((z + d) % 4, BLK, 16), :],
            za4.at[k, :, at(z, BLK, 16), :],
            zz_s.at[k % 2, d - 1],
            zz_r.at[k, d - 1],
            peer(here, 0, d, 0, 0),
        )

    def xx_copy(k, d):
        return remote(
            xs4.at[k % 2, :, at((x + d) % 4, BLK, 16), :],
            rows.at[1, :, at(x, BLK, 16), cols(k)],
            xx_s.at[k % 2, d - 1],
            xx_r.at[k, d - 1],
            peer(here, 0, 0, d, 0),
        )

    def xx_own(k):
        return pltpu.make_async_copy(
            xs4.at[k % 2, :, at(x, BLK, 16), :],
            rows.at[1, :, at(x, BLK, 16), cols(k)],
            xx_l.at[k % 2],
        )

    def stage4_copy(k):
        return pltpu.make_async_copy(
            rows.at[1, :, :, cols(k)], stage4.at[k % 2], st4_l.at[k % 2]
        )

    def early_send(k):
        for i in range(2):
            yy_copy(k, i).start()

    def early_pass(k):
        for i in range(2):
            yy_copy(k, i).wait_recv()
            ff_copy(k, i).start()
            cc_copy(k, i).start()

    def early_rest(k):
        for i in range(2):
            ff_copy(k, i).wait_recv()
        cc_copy(k, 2).start()

    def early_select(k):
        own_local(k).wait()
        own_remote(k).wait()
        for i in range(3):
            cc_copy(k, i).wait_recv()

        def block(b, carry):
            for out in tiles(FW):
                picked = nn(sel[b], raw4[k, b, :, out]) * gp[b, :, 0:1]
                zs4[k % 2, b, :, out] = picked.astype(BF)
            za4[k, b, at(z, BLK, 16), :] = zs4[k % 2, b, at(z, BLK, 16), :]
            return carry

        lax.fori_loop(0, 4, block, 0)
        for d in (2, 1, 3):
            zz_copy(k, d).start()

    def early_turn(k):
        for d in (1, 2, 3):
            zz_copy(k, d).wait_recv()

        def block(b, carry):
            for out in tiles(FW):
                xs4[k % 2, b, :, out] = nn(perm[...], za4[k, b, :, out]).astype(BF)
            return carry

        lax.fori_loop(0, 4, block, 0)
        for d in (2, 1, 3):
            xx_copy(k, d).start()
        xx_own(k).start()

    def early_fetch(k):
        for d in (1, 2, 3):
            xx_copy(k, d).wait_recv()
        xx_own(k).wait()
        stage4_copy(k).start()

    def early_accumulate(k):
        stage4_copy(k).wait()

        def block(b, carry):
            acc[2, at(b, ROWS, 16), :] += nt(stage4[k % 2, b], wd[:, cols(k)])
            return carry

        lax.fori_loop(0, 4, block, 0)

    def which(i):
        a = i // FC
        return a, cols(i - a * (FC - F_EARLY))

    def raw_copies(i):
        a = i // FC
        src = sources[a].at[:, cols(i - a * (FC - F_EARLY))]
        dst = raw.at[i, mine, :]
        return (
            pltpu.make_async_copy(src, dst, raw_l.at[i]),
            remote(src, dst, raw_s.at[i], raw_r.at[i], peer(here, 0, 0, 0, 1)),
        )

    def raw_waits(i):
        src = tok_ref.at[:, cols(0)]
        dst = raw.at[i, mine, :]
        return (
            pltpu.make_async_copy(src, dst, raw_l.at[i]),
            remote(src, dst, raw_s.at[i], raw_r.at[i], peer(here, 0, 0, 0, 1)),
        )

    def z_copy(i, d):
        return remote(
            zs.at[i % 2, at((z + d) % 4, BLK, 16), :],
            za.at[i, at(z, BLK, 16), :],
            z_s.at[i % 2, d - 1],
            z_r.at[i, d - 1],
            peer(here, 0, d, 0, 0),
        )

    def x_copy(i, d):
        a, span = which(i)
        return remote(
            xs.at[i % 2, at((x + d) % 4, BLK, 16), :],
            rows.at[a, y, at(x, BLK, 16), span],
            x_s.at[i % 2, d - 1],
            x_r.at[i, d - 1],
            peer(here, 0, 0, d, 0),
        )

    def x_own(i):
        a, span = which(i)
        return pltpu.make_async_copy(
            xs.at[i % 2, at(x, BLK, 16), :], rows.at[a, y, at(x, BLK, 16), span], x_l.at[i % 2]
        )

    def y_copy(i, p):
        a, span = which(i)
        block = rows.at[a, y, :, span]
        return remote(
            block, block, y_s.at[i, p], y_r.at[i, p], peer(here, PLUS_MINUS[p], 0, 0, 0)
        )

    def f_copy(i, p):
        a, span = which(i)
        half = rows.at[a, (y + PLUS_MINUS[1 - p]) % 4, pl.ds(p * 96, 96), span]
        return remote(half, half, f_s.at[i, p], f_r.at[i, p], peer(here, PLUS_MINUS[p], 0, 0, 0))

    def stage_copy(i):
        a, span = which(i)
        return pltpu.make_async_copy(rows.at[a, :, :, span], stage.at[i % 2], st_l.at[i % 2])

    def late_select(i):
        for copy in raw_waits(i):
            copy.wait()
        scale = jnp.where(i // FC == 1, gp[y], 1.0)[:, 0:1]
        for out in tiles(FW):
            zs[i % 2, :, out] = (nn(sel[y], raw[i, :, out]) * scale).astype(BF)
        for d in (2, 1, 3):
            z_copy(i, d).start()
        za[i, at(z, BLK, 16), :] = zs[i % 2, at(z, BLK, 16), :]

    def late_turn(i):
        for d in (1, 2, 3):
            z_copy(i, d).wait_recv()
        for out in tiles(FW):
            xs[i % 2, :, out] = nn(perm[...], za[i, :, out]).astype(BF)
        for d in (2, 1, 3):
            x_copy(i, d).start()
        x_own(i).start()

    def late_spread(i):
        for d in (1, 2, 3):
            x_copy(i, d).wait_recv()
        x_own(i).wait()
        for p in range(2):
            y_copy(i, p).start()

    def late_pass(i):
        for p in range(2):
            y_copy(i, p).wait_recv()
            f_copy(i, p).start()

    def late_fetch(i):
        for p in range(2):
            f_copy(i, p).wait_recv()
        stage_copy(i).start()

    def late_accumulate(i):
        stage_copy(i).wait()
        a, span = which(i)

        @pl.when(a == 0)
        def _():
            def block(b, carry):
                block_rows = at(b, ROWS, 16)
                tokens = stage[i % 2, b]
                acc[0, block_rows, :] += nn(tokens, wg[span, :])
                acc[1, block_rows, :] += nn(tokens, wu[span, :])
                return carry

            lax.fori_loop(0, 4, block, 0)

        @pl.when(a == 1)
        def _():
            def block(b, carry):
                acc[2, at(b, ROWS, 16), :] += nt(stage[i % 2, b], wd[:, span])
                return carry

            lax.fori_loop(0, 4, block, 0)

    def drain(copy, count, base):
        def body(k):
            for i in range(count):
                copy(k, base + i).wait_send()

        return body

    early_send(0)
    for i in range(F_LATE):
        for copy in raw_copies(i):
            copy.start()
        if i < F_EARLY:
            own_local(i).start()
            own_remote(i).start()
    weights = [
        pltpu.make_async_copy(src, dst, w_sem.at[i])
        for i, (src, dst) in enumerate(((wg_hbm, wg), (wu_hbm, wu), (wd_hbm, wd)))
    ]
    for copy in weights:
        copy.start()
    perm[...] = swap_matrix()
    acc[...] = jnp.zeros_like(acc)
    for i in range(len(others)):
        meta_copy(i).wait()

    def plan(b, carry):
        earlier = (
            (
                lax.broadcasted_iota(jnp.int32, (TOK, TOK), 0)
                < lax.broadcasted_iota(jnp.int32, (TOK, TOK), 1)
            )
            .astype(F32)
            .astype(BF)
        )
        weight = jnp.zeros((ROWS, 1), F32)
        for m in range(2):
            route = metas[b, m, 0:1, :].astype(jnp.int32)
            prob = metas[b, m, 1:2, :]
            onehot = (lax.broadcasted_iota(jnp.int32, (32, TOK), 0) == route).astype(F32)
            before = nn(onehot.astype(BF), earlier)
            slot = jnp.sum(onehot * before, axis=0, keepdims=True).astype(jnp.int32)
            row = ((route >> 1) * 2 + m) * CAP + slot
            row = jnp.where((route & 1) == c, row, -1)
            chosen = lax.broadcasted_iota(jnp.int32, (ROWS, TOK), 0) == row
            sel[b, :, m * TOK : (m + 1) * TOK] = chosen.astype(F32).astype(BF)
            weight = weight + jnp.sum(jnp.where(chosen, prob, 0.0), axis=1, keepdims=True)
        gp[b] = jnp.broadcast_to(weight, (ROWS, 128))
        return carry

    lax.fori_loop(0, 4, plan, 0)

    def step(t, carry):
        when(t - 2, F_LATE, drain(z_copy, 3, 1))
        when(t - 3, F_LATE, drain(x_copy, 3, 1))
        when(t - 4, F_LATE, drain(y_copy, 2, 0))
        when(t - 5, F_LATE, drain(f_copy, 2, 0))
        when(t - 1, F_EARLY, drain(yy_copy, 2, 0))
        when(t - 2, F_EARLY, drain(ff_copy, 2, 0))
        when(t - 3, F_EARLY, drain(cc_copy, 3, 0))
        when(t - 4, F_EARLY, drain(zz_copy, 3, 1))
        when(t - 5, F_EARLY, drain(xx_copy, 3, 1))

        when(t, F_LATE, late_select)
        when(t + 1, F_EARLY, early_send)
        when(t, F_EARLY, early_pass)
        when(t - 1, F_LATE, late_turn)
        when(t - 1, F_EARLY, early_rest)
        when(t - 2, F_LATE, late_spread)
        when(t - 2, F_EARLY, early_select)
        when(t - 3, F_LATE, late_pass)
        when(t - 3, F_EARLY, early_turn)
        when(t - 4, F_LATE, late_fetch)
        when(t - 4, F_EARLY, early_fetch)

        @pl.when(t == 5)
        def _():
            for copy in weights:
                copy.wait()

        when(t - 5, F_LATE, late_accumulate)
        when(t - 5, F_EARLY, early_accumulate)
        return carry

    lax.fori_loop(0, F_LATE + 5, step, 0)

    def finish(b, carry):
        part = at(b, Q, 256)
        gate, up, grad = acc[0, part, :], acc[1, part, :], acc[2, part, :]
        sig = jax.nn.sigmoid(gate)
        silu = gate * sig
        hidden = silu * up
        gate_grad = grad * up * sig * (1.0 + gate * (1.0 - sig))
        up_grad = grad * silu
        acts[0, part, :] = gate_grad.astype(BF)
        acts[1, part, :] = up_grad.astype(BF)
        acts_t[0, :, part] = hidden.T.astype(BF)
        acts_t[1, :, part] = gate_grad.T.astype(BF)
        acts_t[2, :, part] = up_grad.T.astype(BF)
        return carry

    lax.fori_loop(0, 3, finish, 0)


def backward_kernel(
    acts,
    acts_t,
    sel,
    rows,
    wg_hbm,
    wu_hbm,
    moment_ref,
    grad_ref,
    update_ref,
    second_ref,
    perm,
    far,
    relay,
    near,
    summed,
    xs,
    xa,
    zs,
    za,
    cs,
    co,
    cr,
    xs4,
    xa4,
    zs4,
    za4,
    cs4,
    co4,
    cr4,
    relay4,
    summed4,
    stage,
    dw,
    squares,
    wg,
    wu,
    w_sem,
    p_s,
    p_r,
    n_s,
    n_r,
    x_s,
    x_r,
    z_s,
    z_r,
    c_s,
    c_r,
    xx_s,
    xx_r,
    zz_s,
    zz_r,
    cc_s,
    cc_r,
    pp_s,
    pp_r,
    nn_s,
    nn_r,
    st_l,
):
    here = place()
    y, z, x, c = here

    def cols(k):
        return at(k, BW, 128)

    def tile(k, out):
        return pl.ds(pl.multiple_of(k * BW + out.start, 128), SUB)

    greet(here, ACROSS + COLUMN[:2])
    weights = [
        pltpu.make_async_copy(src, dst, w_sem.at[i])
        for i, (src, dst) in enumerate(((wg_hbm, wg), (wu_hbm, wu)))
    ]
    for copy in weights:
        copy.start()

    def stage_copy(a, k):
        return pltpu.make_async_copy(
            rows.at[a, :, :, cols(k)], stage.at[a, k % 2], st_l.at[a, k % 2]
        )

    for a in range(2):
        stage_copy(a, 0).start()
    squares[...] = jnp.zeros_like(squares)
    perm[...] = swap_matrix()
    for copy in weights:
        copy.wait()

    def partial(block, k, out):
        block_rows = at(block, ROWS, 16)
        total = nt(acts[0, block_rows, :], wg[tile(k, out), :])
        total = total + nt(acts[1, block_rows, :], wu[tile(k, out), :])
        return total.astype(BF)

    def p_copy(k, i):
        return remote(
            far.at[k % 2, pl.ds(i * 96, 96), :],
            relay.at[k, i],
            p_s.at[k % 2, i],
            p_r.at[k, i],
            peer(here, PLUS_MINUS[i], 0, 0, 0),
        )

    def n_copy(k, i):
        return remote(
            near.at[i, k % 2],
            summed.at[k, i],
            n_s.at[k % 2, i],
            n_r.at[k, i],
            peer(here, PLUS_MINUS[i], 0, 0, 0),
        )

    def x_copy(k, d):
        return remote(
            xs.at[k % 2, at((x + d) % 4, BLK, 16), :],
            xa.at[k, at(x, BLK, 16), :],
            x_s.at[k % 2, d - 1],
            x_r.at[k, d - 1],
            peer(here, 0, 0, d, 0),
        )

    def z_copy(k, d):
        return remote(
            zs.at[k % 2, at((z + d) % 4, BLK, 16), :],
            za.at[k, at(z, BLK, 16), :],
            z_s.at[k % 2, d - 1],
            z_r.at[k, d - 1],
            peer(here, 0, d, 0, 0),
        )

    def c_copy(k):
        return remote(cs.at[k % 2], cr.at[k], c_s.at[k % 2], c_r.at[k], peer(here, 0, 0, 0, 1))

    def late_far(k):
        for out in tiles(BW):
            far[k % 2, :, out] = partial((y + 2) % 4, k, out)
        for i in range(2):
            p_copy(k, i).start()

    def late_near(k):
        for i in range(2):
            p_copy(k, i).wait_recv()
            added, plain = slice(i * 96, i * 96 + 96), slice(96 - i * 96, 192 - i * 96)
            for out in tiles(BW):
                term = partial((y + PLUS_MINUS[i]) % 4, k, out)
                both = term[added].astype(F32) + relay[k, i, :, out].astype(F32)
                near[i, k % 2, added, out] = both.astype(BF)
                near[i, k % 2, plain, out] = term[plain]
            n_copy(k, i).start()

    def late_total(k):
        for i in range(2):
            n_copy(k, i).wait_recv()
        for out in tiles(BW):
            whole = partial(y, k, out).astype(F32)
            whole = whole + summed[k, 0, :, out].astype(F32)
            whole = whole + summed[k, 1, :, out].astype(F32)
            xs[k % 2, :, out] = whole.astype(BF)
        for d in (2, 1, 3):
            x_copy(k, d).start()
        xa[k, at(x, BLK, 16), :] = xs[k % 2, at(x, BLK, 16), :]

    def late_turn(k):
        for d in (1, 2, 3):
            x_copy(k, d).wait_recv()
        for out in tiles(BW):
            zs[k % 2, :, out] = nn(perm[...], xa[k, :, out]).astype(BF)
        for d in (2, 1, 3):
            z_copy(k, d).start()
        za[k, at(z, BLK, 16), :] = zs[k % 2, at(z, BLK, 16), :]

    def late_unselect(k):
        for d in (1, 2, 3):
            z_copy(k, d).wait_recv()
        for out in tiles(BW):
            block = za[k, :, out]
            cs[k % 2, :, out] = tn(sel[y, :, at(1 - c, TOK, TOK)], block).astype(BF)
            co[k % 2, :, out] = tn(sel[y, :, at(c, TOK, TOK)], block).astype(BF)
        c_copy(k).start()

    def late_join(k):
        c_copy(k).wait()
        whole = co[k % 2].astype(F32) + cr[k].astype(F32)
        grad_ref[:, cols(k)] = whole.astype(BF)

    def xx_copy(k, d):
        return remote(
            xs4.at[k % 2, :, at((x + d) % 4, BLK, 16), :],
            xa4.at[k, :, at(x, BLK, 16), :],
            xx_s.at[k % 2, d - 1],
            xx_r.at[k, d - 1],
            peer(here, 0, 0, d, 0),
        )

    def zz_copy(k, d):
        return remote(
            zs4.at[k % 2, :, at((z + d) % 4, BLK, 16), :],
            za4.at[k, :, at(z, BLK, 16), :],
            zz_s.at[k % 2, d - 1],
            zz_r.at[k, d - 1],
            peer(here, 0, d, 0, 0),
        )

    def cc_copy(k):
        return remote(
            cs4.at[k % 2], cr4.at[k], cc_s.at[k % 2], cc_r.at[k], peer(here, 0, 0, 0, 1)
        )

    def pp_copy(k, i):
        return remote(
            cr4.at[k, (y + 2) % 4, pl.ds(i * 64, 64), :],
            relay4.at[k, i],
            pp_s.at[k, i],
            pp_r.at[k, i],
            peer(here, PLUS_MINUS[i], 0, 0, 0),
        )

    def nn_copy(k, i):
        return remote(
            cr4.at[k, (y + PLUS_MINUS[i]) % 4],
            summed4.at[k, i],
            nn_s.at[k, i],
            nn_r.at[k, i],
            peer(here, PLUS_MINUS[i], 0, 0, 0),
        )

    def early_terms(k):
        def block(b, carry):
            for out in tiles(BW):
                xs4[k % 2, b, :, out] = partial(b, k + B_LATE, out)
            xa4[k, b, at(x, BLK, 16), :] = xs4[k % 2, b, at(x, BLK, 16), :]
            return carry

        lax.fori_loop(0, 4, block, 0)
        for d in (2, 1, 3):
            xx_copy(k, d).start()

    def early_turn(k):
        for d in (1, 2, 3):
            xx_copy(k, d).wait_recv()

        def block(b, carry):
            for out in tiles(BW):
                zs4[k % 2, b, :, out] = nn(perm[...], xa4[k, b, :, out]).astype(BF)
            za4[k, b, at(z, BLK, 16), :] = zs4[k % 2, b, at(z, BLK, 16), :]
            return carry

        lax.fori_loop(0, 4, block, 0)
        for d in (2, 1, 3):
            zz_copy(k, d).start()

    def early_unselect(k):
        for d in (1, 2, 3):
            zz_copy(k, d).wait_recv()

        def block(b, carry):
            for out in tiles(BW):
                whole = za4[k, b, :, out]
                cs4[k % 2, b, :, out] = tn(sel[b, :, at(1 - c, TOK, TOK)], whole).astype(BF)
                co4[k % 2, b, :, out] = tn(sel[b, :, at(c, TOK, TOK)], whole).astype(BF)
            return carry

        lax.fori_loop(0, 4, block, 0)
        cc_copy(k).start()

    def early_far(k):
        cc_copy(k).wait()

        def block(b, carry):
            whole = co4[k % 2, b].astype(F32) + cr4[k, b].astype(F32)
            cr4[k, b] = whole.astype(BF)
            return carry

        lax.fori_loop(0, 4, block, 0)
        for i in range(2):
            pp_copy(k, i).start()

    def early_near(k):
        for i in range(2):
            pp_copy(k, i).wait_recv()
            block, added = (y + PLUS_MINUS[i]) % 4, slice(i * 64, i * 64 + 64)
            both = cr4[k, block, added, :].astype(F32) + relay4[k, i].astype(F32)
            cr4[k, block, added, :] = both.astype(BF)
            nn_copy(k, i).start()

    def early_join(k):
        whole = cr4[k, y].astype(F32)
        for i in range(2):
            nn_copy(k, i).wait()
            whole = whole + summed4[k, i].astype(F32)
        grad_ref[:, cols(k + B_LATE)] = whole.astype(BF)

    def weight_grads(k):
        for a in range(2):
            stage_copy(a, k).wait()

        @pl.when(k + 1 < BC)
        def _():
            for a in range(2):
                stage_copy(a, k + 1).start()

        for out in tiles(BW):
            cot_rows = stage[1, k % 2, :, :, out].reshape(4 * ROWS, SUB)
            tok_rows = stage[0, k % 2, :, :, out].reshape(4 * ROWS, SUB)
            down = nn(acts_t[0], cot_rows)
            dw[:, tile(k, out)] = down
            gate = nn(acts_t[1], tok_rows)
            up = nn(acts_t[2], tok_rows)
            sq = down * down + gate * gate + up * up
            squares[...] += sq[:, 0:128] + sq[:, 128:256]

    def update(k):
        @pl.when(k == 0)
        def _():
            mean = jnp.sum(squares[...], axis=1, keepdims=True) / (3.0 * D)
            old = jnp.broadcast_to(moment_ref[...], (128, Q)).T
            second = moment_decay * old + (1.0 - moment_decay) * mean
            second_ref[...] = second.T[0:1, :]
            squares[...] = 1.0 / (jnp.sqrt(second) + epsilon)

        for j in range(BW // 128):
            out = pl.ds(pl.multiple_of(k * BW + j * 128, 128), 128)
            update_ref[:, out] = (dw[:, out] * squares[...]).astype(BF)

    def drain(copy, count, base):
        def body(k):
            for i in range(count):
                copy(k, base + i).wait_send()

        return body

    def step(t, carry):
        when(t - 2, B_LATE, drain(p_copy, 2, 0))
        when(t - 3, B_LATE, drain(n_copy, 2, 0))
        when(t - 4, B_LATE, drain(x_copy, 3, 1))
        when(t - 5, B_LATE, drain(z_copy, 3, 1))
        when(t - 2, B_EARLY, drain(xx_copy, 3, 1))
        when(t - 3, B_EARLY, drain(zz_copy, 3, 1))
        when(t - 5, B_EARLY, drain(pp_copy, 2, 0))

        when(t, B_LATE, late_far)
        when(t, B_EARLY, early_terms)
        when(t - 1, B_LATE, late_near)
        when(t - 1, B_EARLY, early_turn)
        when(t - 2, B_LATE, late_total)
        when(t - 2, B_EARLY, early_unselect)
        when(t - 3, B_LATE, late_turn)
        when(t - 3, B_EARLY, early_far)
        when(t - 4, B_LATE, late_unselect)
        when(t - 4, B_EARLY, early_near)
        when(t - 5, B_LATE, late_join)
        when(t - 5, B_EARLY, early_join)
        for n in range(2):
            when(t * 2 + n, BC, weight_grads)
        for n in range(3):
            when((t - BC // 2) * 3 + n, BC, update)
        return carry

    lax.fori_loop(0, B_LATE + 5, step, 0)


def shards(tokens, grad_out, routes, gate_prob, w_gate, w_up, w_down, moment_prev):
    vmem = pl.BlockSpec(memory_space=pltpu.VMEM)
    hbm = pl.BlockSpec(memory_space=pltpu.HBM)
    dma = pltpu.SemaphoreType.DMA

    def held(*shape):
        return pltpu.VMEM(shape, BF)

    rows, acts, acts_t, sel = pl.pallas_call(
        forward_kernel,
        name="dispatch",
        out_shape=(
            jax.ShapeDtypeStruct((2, 4, ROWS, D), BF),
            jax.ShapeDtypeStruct((2, 4 * ROWS, Q), BF),
            jax.ShapeDtypeStruct((3, Q, 4 * ROWS), BF),
            jax.ShapeDtypeStruct((4, ROWS, 2 * TOK), BF),
        ),
        in_specs=[vmem, vmem, hbm, hbm, hbm, hbm, hbm],
        out_specs=(hbm, vmem, vmem, vmem),
        scratch_shapes=[
            pltpu.VMEM((4, 2, 8, TOK), F32),
            pltpu.VMEM((4, ROWS, 128), F32),
            held(ROWS, ROWS),
            held(F_LATE, 2 * TOK, FW),
            held(2, ROWS, FW),
            held(F_LATE, ROWS, FW),
            held(2, ROWS, FW),
            held(F_EARLY, 4, 2 * TOK, FW),
            held(2, 4, ROWS, FW),
            held(F_EARLY, 4, ROWS, FW),
            held(2, 4, ROWS, FW),
            held(2, 4, ROWS, FW),
            held(2, 4, ROWS, FW),
            pltpu.VMEM((3, 4 * ROWS, Q), F32),
            held(D, Q),
            held(D, Q),
            held(Q, D),
            dma((3,)),
            dma((7,)),
            dma((7,)),
            dma((F_LATE,)),
            dma((F_LATE,)),
            dma((F_LATE,)),
            dma((2, 3)),
            dma((F_LATE, 3)),
            dma((2, 3)),
            dma((F_LATE, 3)),
            dma((2,)),
            dma((F_LATE, 2)),
            dma((F_LATE, 2)),
            dma((F_LATE, 2)),
            dma((F_LATE, 2)),
            dma((2,)),
            dma((F_EARLY,)),
            dma((F_EARLY,)),
            dma((F_EARLY,)),
            dma((F_EARLY, 2)),
            dma((F_EARLY, 2)),
            dma((F_EARLY, 2)),
            dma((F_EARLY, 2)),
            dma((F_EARLY, 3)),
            dma((F_EARLY, 3)),
            dma((2, 3)),
            dma((F_EARLY, 3)),
            dma((2, 3)),
            dma((F_EARLY, 3)),
            dma((2,)),
            dma((2,)),
        ],
        compiler_params=pltpu.CompilerParams(
            collective_id=0, has_side_effects=True, vmem_limit_bytes=60 * 2**20
        ),
    )(
        routes.reshape(1, TOK),
        gate_prob.reshape(1, TOK),
        tokens,
        grad_out,
        w_gate[0],
        w_up[0],
        w_down[0],
    )
    grad_in, update, second = pl.pallas_call(
        backward_kernel,
        name="combine",
        out_shape=(
            jax.ShapeDtypeStruct((TOK, D), BF),
            jax.ShapeDtypeStruct((Q, D), BF),
            jax.ShapeDtypeStruct((1, Q), F32),
        ),
        in_specs=[vmem, vmem, vmem, hbm, hbm, hbm, vmem],
        out_specs=(vmem, vmem, vmem),
        scratch_shapes=[
            held(ROWS, ROWS),
            held(2, ROWS, BW),
            held(B_LATE, 2, 96, BW),
            held(2, 2, ROWS, BW),
            held(B_LATE, 2, ROWS, BW),
            held(2, ROWS, BW),
            held(B_LATE, ROWS, BW),
            held(2, ROWS, BW),
            held(B_LATE, ROWS, BW),
            held(2, TOK, BW),
            held(2, TOK, BW),
            held(B_LATE, TOK, BW),
            held(2, 4, ROWS, BW),
            held(B_EARLY, 4, ROWS, BW),
            held(2, 4, ROWS, BW),
            held(B_EARLY, 4, ROWS, BW),
            held(2, 4, TOK, BW),
            held(2, 4, TOK, BW),
            held(B_EARLY, 4, TOK, BW),
            held(B_EARLY, 2, 64, BW),
            held(B_EARLY, 2, TOK, BW),
            held(2, 2, 4, ROWS, BW),
            pltpu.VMEM((Q, D), F32),
            pltpu.VMEM((Q, 128), F32),
            held(D, Q),
            held(D, Q),
            dma((2,)),
            dma((2, 2)),
            dma((B_LATE, 2)),
            dma((2, 2)),
            dma((B_LATE, 2)),
            dma((2, 3)),
            dma((B_LATE, 3)),
            dma((2, 3)),
            dma((B_LATE, 3)),
            dma((2,)),
            dma((B_LATE,)),
            dma((2, 3)),
            dma((B_EARLY, 3)),
            dma((2, 3)),
            dma((B_EARLY, 3)),
            dma((2,)),
            dma((B_EARLY,)),
            dma((B_EARLY, 2)),
            dma((B_EARLY, 2)),
            dma((B_EARLY, 2)),
            dma((B_EARLY, 2)),
            dma((2, 2)),
        ],
        compiler_params=pltpu.CompilerParams(
            collective_id=1, has_side_effects=True, vmem_limit_bytes=60 * 2**20
        ),
    )(acts, acts_t, sel, rows, w_gate[0], w_up[0], moment_prev)
    return grad_in, update[None], second


def solution(mesh):
    placed = (
        P(("dp", "expert"), None),
        P(("dp", "expert"), None),
        P(("dp", "expert"), None),
        P(("dp", "expert"), None),
        P("expert", None, "dp"),
        P("expert", None, "dp"),
        P("expert", "dp", None),
        P("expert", "dp"),
    )
    return jax.shard_map(
        shards,
        mesh=mesh,
        in_specs=placed,
        out_specs=(P(("dp", "expert"), None), P("expert", "dp", None), P("expert", "dp")),
        check_vma=False,
    )
```

```python
import functools

import jax
import jax.numpy as jnp
from jax import lax
from jax.experimental import pallas as pl
from jax.experimental.pallas import tpu as pltpu
from jax.sharding import PartitionSpec as P

MESH = pl.DeviceIdType.MESH
BF = jnp.bfloat16
F32 = jnp.float32

moment_decay = 0.95
epsilon = 1e-08

D = 7168
TOK = 128
CAP = 6
Q = 256
ROWS = 192
BLK = 48
SUB = 256

FW = 512
FC = D // FW
EW = 384
F_EARLY = 16
F_DONE = F_EARLY * EW // FW
F_LATE = 2 * FC - F_DONE
BW = 512
BC = D // BW
CW = 384
B_EARLY = 8
B_LATE = (D - B_EARLY * CW) // BW
B_FROM = B_LATE * BW

ACROSS = ((0, 0, 0, 1),) + tuple((0, d, 0, 0) for d in (1, 2, 3)) + tuple((0, 0, d, 0) for d in (1, 2, 3))
COLUMN = ((1, 0, 0, 0), (3, 0, 0, 0), (2, 0, 0, 0), (1, 0, 0, 1), (3, 0, 0, 1), (2, 0, 0, 1))
PLUS_MINUS = (1, 3)


def place():
    y = lax.axis_index("dp")
    e = lax.axis_index("expert")
    return y, e // 8, (e // 2) % 4, e % 2


def peer(here, dy, dz, dx, dc):
    y, z, x, c = here
    expert = (((z + dz) % 4) * 4 + (x + dx) % 4) * 2 + (c + dc) % 2
    return {"dp": (y + dy) % 4, "expert": expert}


def remote(src, dst, send, recv, device):
    return pltpu.make_async_remote_copy(
        src_ref=src,
        dst_ref=dst,
        send_sem=send,
        recv_sem=recv,
        device_id=device,
        device_id_type=MESH,
    )


def greet(here, partners):
    barrier = pltpu.get_barrier_semaphore()
    for offset in partners:
        pl.semaphore_signal(barrier, inc=1, device_id=peer(here, *offset), device_id_type=MESH)
    return lambda: pl.semaphore_wait(barrier, len(partners))


def at(index, size, align):
    return pl.ds(pl.multiple_of(index * size, align), size)


def nt(a, b):
    return lax.dot_general(a, b, (((1,), (1,)), ((), ())), preferred_element_type=F32)


def tn(a, b):
    return lax.dot_general(a, b, (((0,), (0,)), ((), ())), preferred_element_type=F32)


def nn(a, b):
    return jnp.dot(a, b, preferred_element_type=F32)


def tiles(width):
    return [slice(j, min(j + SUB, width)) for j in range(0, width, SUB)]


def swap_matrix():
    out = lax.broadcasted_iota(jnp.int32, (ROWS, ROWS), 0)
    row = lax.broadcasted_iota(jnp.int32, (ROWS, ROWS), 1)

    def steps(value, size):
        return sum((value >= size * n).astype(jnp.int32) for n in (1, 2, 3))

    outer = steps(out, 48)
    inner = steps(out - 48 * outer, 12)
    return (row - out == 36 * (inner - outer)).astype(F32).astype(BF)


def when(k, count, body):
    pl.when((k >= 0) & (k < count))(lambda: body(k))


def forward_kernel(
    routes_ref,
    prob_ref,
    tok_ref,
    cot_ref,
    wg_hbm,
    wu_hbm,
    wd_hbm,
    rows,
    acts,
    acts_t,
    sel,
    metas,
    gp,
    perm,
    raw,
    zs,
    za,
    xs,
    raw4,
    zs4,
    za4,
    xs4,
    stage,
    stage4,
    acc,
    wg,
    wu,
    wd,
    w_sem,
    m_s,
    m_r,
    raw_l,
    raw_s,
    raw_r,
    z_s,
    z_r,
    x_s,
    x_r,
    x_l,
    y_s,
    y_r,
    f_s,
    f_r,
    st_l,
    own_l,
    own_s,
    own_r,
    yy_s,
    yy_r,
    ff_s,
    ff_r,
    cc_s,
    cc_r,
    zz_s,
    zz_r,
    xx_s,
    xx_r,
    xx_l,
    st4_l,
):
    here = place()
    y, z, x, c = here
    mine = at(c, TOK, TOK)

    def cols(k):
        return at(k, FW, 128)

    def ecols(k):
        return at(k, EW, 128)

    met = greet(here, ACROSS + COLUMN)
    weights = [
        pltpu.make_async_copy(src, dst, w_sem.at[i])
        for i, (src, dst) in enumerate(((wg_hbm, wg), (wu_hbm, wu), (wd_hbm, wd)))
    ]

    first = lax.broadcasted_iota(jnp.int32, (8, TOK), 0) == 0
    metas[y, c] = jnp.where(first, routes_ref[...].astype(F32), prob_ref[...])
    others = COLUMN + ((0, 0, 0, 1),)

    def meta_copy(i):
        return remote(
            metas.at[y, c], metas.at[y, c], m_s.at[i], m_r.at[i], peer(here, *others[i])
        )

    def yy_copy(k, i):
        return remote(
            cot_ref.at[:, ecols(k)],
            raw4.at[k, y, mine, :],
            yy_s.at[k],
            yy_r.at[k],
            peer(here, PLUS_MINUS[i], 0, 0, 0),
        )

    def ff_copy(k, i):
        src = (y + PLUS_MINUS[1 - i]) % 4
        half = raw4.at[k, src, pl.ds(pl.multiple_of(c * TOK + i * 64, 64), 64), :]
        return remote(
            half, half, ff_s.at[k], ff_r.at[k], peer(here, PLUS_MINUS[i], 0, 0, 0)
        )

    def cc_copy(k, i):
        block = raw4.at[k, (y + (3, 1, 2)[i]) % 4, mine, :]
        return remote(block, block, cc_s.at[k], cc_r.at[k], peer(here, 0, 0, 0, 1))

    def own_local(k):
        return pltpu.make_async_copy(
            cot_ref.at[:, ecols(k)], raw4.at[k, y, mine, :], own_l.at[k]
        )

    def own_remote(k):
        return remote(
            cot_ref.at[:, ecols(k)],
            raw4.at[k, y, mine, :],
            own_s.at[k],
            own_r.at[k],
            peer(here, 0, 0, 0, 1),
        )

    def zz_copy(k, d):
        return remote(
            zs4.at[k % 2, :, at((z + d) % 4, BLK, 16), :],
            za4.at[k, :, at(z, BLK, 16), :],
            zz_s.at[k % 2],
            zz_r.at[k],
            peer(here, 0, d, 0, 0),
        )

    def xx_copy(k, d):
        return remote(
            xs4.at[k % 2, :, at((x + d) % 4, BLK, 16), :],
            rows.at[1, :, at(x, BLK, 16), ecols(k)],
            xx_s.at[k % 2],
            xx_r.at[k],
            peer(here, 0, 0, d, 0),
        )

    def xx_own(k):
        return pltpu.make_async_copy(
            xs4.at[k % 2, :, at(x, BLK, 16), :],
            rows.at[1, :, at(x, BLK, 16), ecols(k)],
            xx_l.at[k % 2],
        )

    def stage4_copy(k):
        return pltpu.make_async_copy(
            rows.at[1, :, :, ecols(k)], stage4.at[k % 2], st4_l.at[k % 2]
        )

    def yy_all(k):
        both = raw4.at[k, pl.ds(0, 2), mine, :]
        return remote(both, both, yy_s.at[k], yy_r.at[k], peer(here, 1, 0, 0, 0))

    def ff_all(k):
        both = raw4.at[k, 0, mine, :]
        return remote(both, both, ff_s.at[k], ff_r.at[k], peer(here, 1, 0, 0, 0))

    def cc_all(k):
        three = raw4.at[k, pl.ds(0, 3), mine, :]
        return remote(three, three, cc_s.at[k], cc_r.at[k], peer(here, 0, 0, 0, 1))

    def zz_all(k):
        return remote(
            zs4.at[k % 2, :, pl.ds(0, 3 * BLK), :],
            za4.at[k, :, pl.ds(0, 3 * BLK), :],
            zz_s.at[k % 2],
            zz_r.at[k],
            peer(here, 0, 1, 0, 0),
        )

    def xx_all(k):
        return remote(
            xs4.at[k % 2, :, pl.ds(0, 3 * BLK), :],
            rows.at[1, :, pl.ds(0, 3 * BLK), ecols(k)],
            xx_s.at[k % 2],
            xx_r.at[k],
            peer(here, 0, 0, 1, 0),
        )

    def early_send(k):
        for i in range(2):
            yy_copy(k, i).start()

    def early_own(k):
        own_local(k).start()
        own_remote(k).start()

    def early_pass(k):
        yy_all(k).wait_recv()
        for i in range(2):
            ff_copy(k, i).start()
            cc_copy(k, i).start()

    def early_rest(k):
        ff_all(k).wait_recv()
        cc_copy(k, 2).start()

    def early_select(k):
        own_local(k).wait()
        own_remote(k).wait()
        cc_all(k).wait_recv()

        def block(b, carry):
            for out in tiles(EW):
                picked = nn(sel[b], raw4[k, b, :, out]) * gp[b, :, 0:1]
                zs4[k % 2, b, :, out] = picked.astype(BF)
            za4[k, b, at(z, BLK, 16), :] = zs4[k % 2, b, at(z, BLK, 16), :]
            return carry

        lax.fori_loop(0, 4, block, 0)
        for d in (2, 1, 3):
            zz_copy(k, d).start()

    def early_turn(k):
        zz_all(k).wait_recv()

        def block(b, carry):
            for out in tiles(EW):
                xs4[k % 2, b, :, out] = nn(perm[...], za4[k, b, :, out]).astype(BF)
            return carry

        lax.fori_loop(0, 4, block, 0)
        for d in (2, 1, 3):
            xx_copy(k, d).start()
        xx_own(k).start()

    def early_fetch(k):
        xx_all(k).wait_recv()
        xx_own(k).wait()
        stage4_copy(k).start()

    def early_accumulate(k):
        stage4_copy(k).wait()
        acc[2] += nt(stage4[k % 2].reshape(4 * ROWS, EW), wd[:, ecols(k)])

    def which(i):
        a = i // FC
        return a, cols(i - a * (FC - F_DONE))

    def raw_start(i):
        def begin(src):
            dst = raw.at[i, mine, :]
            pltpu.make_async_copy(src, dst, raw_l.at[i]).start()
            remote(src, dst, raw_s.at[i], raw_r.at[i], peer(here, 0, 0, 0, 1)).start()

        pl.when(i // FC == 0)(lambda: begin(tok_ref.at[:, cols(i)]))
        pl.when(i // FC == 1)(lambda: begin(cot_ref.at[:, cols(i - FC + F_DONE)]))

    def raw_waits(i):
        src = tok_ref.at[:, cols(0)]
        dst = raw.at[i, mine, :]
        return (
            pltpu.make_async_copy(src, dst, raw_l.at[i]),
            remote(src, dst, raw_s.at[i], raw_r.at[i], peer(here, 0, 0, 0, 1)),
        )

    def z_copy(i, d):
        return remote(
            zs.at[i % 2, at((z + d) % 4, BLK, 16), :],
            za.at[i, at(z, BLK, 16), :],
            z_s.at[i % 2],
            z_r.at[i],
            peer(here, 0, d, 0, 0),
        )

    def x_copy(i, d):
        a, span = which(i)
        return remote(
            xs.at[i % 2, at((x + d) % 4, BLK, 16), :],
            rows.at[a, y, at(x, BLK, 16), span],
            x_s.at[i % 2],
            x_r.at[i],
            peer(here, 0, 0, d, 0),
        )

    def x_own(i):
        a, span = which(i)
        return pltpu.make_async_copy(
            xs.at[i % 2, at(x, BLK, 16), :], rows.at[a, y, at(x, BLK, 16), span], x_l.at[i % 2]
        )

    def y_copy(i, p):
        a, span = which(i)
        block = rows.at[a, y, :, span]
        return remote(
            block, block, y_s.at[i], y_r.at[i], peer(here, PLUS_MINUS[p], 0, 0, 0)
        )

    def f_copy(i, p):
        a, span = which(i)
        half = rows.at[a, (y + PLUS_MINUS[1 - p]) % 4, pl.ds(p * 96, 96), span]
        return remote(half, half, f_s.at[i], f_r.at[i], peer(here, PLUS_MINUS[p], 0, 0, 0))

    def stage_copy(i):
        a, span = which(i)
        return pltpu.make_async_copy(rows.at[a, :, :, span], stage.at[i % 2], st_l.at[i % 2])

    def z_all(i):
        return remote(
            zs.at[i % 2, pl.ds(0, 3 * BLK), :],
            za.at[i, pl.ds(0, 3 * BLK), :],
            z_s.at[i % 2],
            z_r.at[i],
            peer(here, 0, 1, 0, 0),
        )

    def x_all(i):
        a, span = which(i)
        return remote(
            xs.at[i % 2, pl.ds(0, 3 * BLK), :],
            rows.at[a, y, pl.ds(0, 3 * BLK), span],
            x_s.at[i % 2],
            x_r.at[i],
            peer(here, 0, 0, 1, 0),
        )

    def y_all(i):
        a, span = which(i)
        both = rows.at[a, pl.ds(0, 2), :, span]
        return remote(both, both, y_s.at[i], y_r.at[i], peer(here, 1, 0, 0, 0))

    def f_all(i):
        a, span = which(i)
        both = rows.at[a, y, :, span]
        return remote(both, both, f_s.at[i], f_r.at[i], peer(here, 1, 0, 0, 0))

    def late_select(i):
        for copy in raw_waits(i):
            copy.wait()
        scale = jnp.where(i // FC == 1, gp[y], 1.0)[:, 0:1]
        for out in tiles(FW):
            zs[i % 2, :, out] = (nn(sel[y], raw[i, :, out]) * scale).astype(BF)
        for d in (2, 1, 3):
            z_copy(i, d).start()
        za[i, at(z, BLK, 16), :] = zs[i % 2, at(z, BLK, 16), :]

    def late_turn(i):
        z_all(i).wait_recv()
        for out in tiles(FW):
            xs[i % 2, :, out] = nn(perm[...], za[i, :, out]).astype(BF)
        for d in (2, 1, 3):
            x_copy(i, d).start()
        x_own(i).start()

    def late_spread(i):
        x_all(i).wait_recv()
        x_own(i).wait()
        for p in range(2):
            y_copy(i, p).start()

    def late_pass(i):
        y_all(i).wait_recv()
        for p in range(2):
            f_copy(i, p).start()

    def late_fetch(i):
        f_all(i).wait_recv()
        stage_copy(i).start()

    def late_accumulate(i):
        stage_copy(i).wait()
        a, span = which(i)

        @pl.when(a == 0)
        def _():
            held = stage[i % 2].reshape(4 * ROWS, FW)
            acc[0] += nn(held, wg[span, :])
            acc[1] += nn(held, wu[span, :])

        @pl.when(a == 1)
        def _():
            acc[2] += nt(stage[i % 2].reshape(4 * ROWS, FW), wd[:, span])

    def drain(copy):
        return lambda k: copy(k).wait_send()

    perm[...] = swap_matrix()
    acc[...] = jnp.zeros_like(acc)
    met()
    for i in range(len(others)):
        meta_copy(i).start()
    early_send(0)
    for i in range(2):
        raw_start(i)
    early_own(0)
    for copy in weights:
        copy.start()
    for i in range(len(others)):
        meta_copy(i).wait()

    def plan(b, carry):
        earlier = (
            (
                lax.broadcasted_iota(jnp.int32, (TOK, TOK), 0)
                < lax.broadcasted_iota(jnp.int32, (TOK, TOK), 1)
            )
            .astype(F32)
            .astype(BF)
        )
        weight = jnp.zeros((ROWS, 1), F32)
        for m in range(2):
            route = metas[b, m, 0:1, :].astype(jnp.int32)
            prob = metas[b, m, 1:2, :]
            onehot = (lax.broadcasted_iota(jnp.int32, (32, TOK), 0) == route).astype(F32)
            before = nn(onehot.astype(BF), earlier)
            slot = jnp.sum(onehot * before, axis=0, keepdims=True).astype(jnp.int32)
            row = ((route >> 1) * 2 + m) * CAP + slot
            row = jnp.where((route & 1) == c, row, -1)
            chosen = lax.broadcasted_iota(jnp.int32, (ROWS, TOK), 0) == row
            sel[b, :, m * TOK : (m + 1) * TOK] = chosen.astype(F32).astype(BF)
            weight = weight + jnp.sum(jnp.where(chosen, prob, 0.0), axis=1, keepdims=True)
        gp[b] = jnp.broadcast_to(weight, (ROWS, 128))
        return carry

    lax.fori_loop(0, 4, plan, 0)

    def step(t, carry):
        when(t - 2, F_LATE, drain(z_all))
        when(t - 3, F_LATE, drain(x_all))
        when(t - 4, F_LATE, drain(y_all))
        when(t - 5, F_LATE, drain(f_all))
        when(t - 1, F_EARLY, drain(yy_all))
        when(t - 2, F_EARLY, drain(ff_all))
        when(t - 3, F_EARLY, drain(cc_all))
        when(t - 4, F_EARLY, drain(zz_all))
        when(t - 5, F_EARLY, drain(xx_all))

        when(t, F_LATE, late_select)
        when(t + 1, F_EARLY, early_send)
        when(t + 1, F_EARLY, early_own)
        when(t + 2, F_LATE, raw_start)
        when(t, F_EARLY, early_pass)
        when(t - 1, F_LATE, late_turn)
        when(t - 1, F_EARLY, early_rest)
        when(t - 2, F_LATE, late_spread)
        when(t - 2, F_EARLY, early_select)
        when(t - 3, F_LATE, late_pass)
        when(t - 3, F_EARLY, early_turn)
        when(t - 4, F_LATE, late_fetch)
        when(t - 4, F_EARLY, early_fetch)

        @pl.when(t == 5)
        def _():
            for copy in weights:
                copy.wait()

        when(t - 5, F_LATE, late_accumulate)
        when(t - 5, F_EARLY, early_accumulate)
        return carry

    lax.fori_loop(0, F_LATE + 5, step, 0)

    def finish(b, carry):
        part = at(b, Q, 256)
        gate, up, grad = acc[0, part, :], acc[1, part, :], acc[2, part, :]
        sig = jax.nn.sigmoid(gate)
        silu = gate * sig
        hidden = silu * up
        gate_grad = grad * up * sig * (1.0 + gate * (1.0 - sig))
        up_grad = grad * silu
        acts[0, part, :] = gate_grad.astype(BF)
        acts[1, part, :] = up_grad.astype(BF)
        acts_t[0, :, part] = hidden.T.astype(BF)
        acts_t[1, :, part] = gate_grad.T.astype(BF)
        acts_t[2, :, part] = up_grad.T.astype(BF)
        return carry

    lax.fori_loop(0, 3, finish, 0)


def backward_kernel(
    acts,
    acts_t,
    sel,
    rows,
    wg_hbm,
    wu_hbm,
    moment_ref,
    grad_ref,
    update_ref,
    second_ref,
    perm,
    far,
    relay,
    near,
    summed,
    xs,
    xa,
    zs,
    za,
    co,
    cr,
    xs4,
    xa4,
    zs4,
    za4,
    co4,
    cr4,
    relay4,
    summed4,
    stage,
    dw,
    squares,
    wg,
    wu,
    w_sem,
    p_s,
    p_r,
    n_s,
    n_r,
    x_s,
    x_r,
    z_s,
    z_r,
    c_s,
    c_r,
    xx_s,
    xx_r,
    zz_s,
    zz_r,
    cc_s,
    cc_r,
    pp_s,
    pp_r,
    nn_s,
    nn_r,
    st_l,
):
    here = place()
    y, z, x, c = here

    def cols(k):
        return at(k, BW, 128)

    def ecols(k):
        return pl.ds(pl.multiple_of(B_FROM + k * CW, 128), CW)

    def tile(k, out):
        return pl.ds(pl.multiple_of(k * BW + out.start, 128), out.stop - out.start)

    def etile(k, out):
        return pl.ds(pl.multiple_of(B_FROM + k * CW + out.start, 128), out.stop - out.start)

    met = greet(here, ACROSS + COLUMN[:2])
    spans = ((0, BW), (B_FROM, CW), (BW, B_FROM - BW), (B_FROM + CW, D - B_FROM - CW))
    weights = [
        pltpu.make_async_copy(
            src.at[pl.ds(first, size)], dst.at[pl.ds(first, size)], w_sem.at[n, i]
        )
        for n, (first, size) in enumerate(spans)
        for i, (src, dst) in enumerate(((wg_hbm, wg), (wu_hbm, wu)))
    ]
    for copy in weights:
        copy.start()

    def stage_copy(a, k):
        return pltpu.make_async_copy(
            rows.at[a, :, :, cols(k)], stage.at[a, k % 2], st_l.at[a, k % 2]
        )

    for a in range(2):
        stage_copy(a, 0).start()
    squares[...] = jnp.zeros_like(squares)
    perm[...] = swap_matrix()
    met()
    for copy in weights[:4]:
        copy.wait()

    def partial(block, span):
        block_rows = at(block, ROWS, 16)
        total = nt(acts[0, block_rows, :], wg[span, :])
        total = total + nt(acts[1, block_rows, :], wu[span, :])
        return total.astype(BF)

    def p_copy(k, i):
        return remote(
            far.at[k % 2, pl.ds(i * 96, 96), :],
            relay.at[k, i],
            p_s.at[k % 2],
            p_r.at[k],
            peer(here, PLUS_MINUS[i], 0, 0, 0),
        )

    def n_copy(k, i):
        return remote(
            near.at[i, k % 2],
            summed.at[k, i],
            n_s.at[k % 2],
            n_r.at[k],
            peer(here, PLUS_MINUS[i], 0, 0, 0),
        )

    def x_copy(k, d):
        return remote(
            xs.at[k % 2, at((x + d) % 4, BLK, 16), :],
            xa.at[k, at(x, BLK, 16), :],
            x_s.at[k % 2],
            x_r.at[k],
            peer(here, 0, 0, d, 0),
        )

    def z_copy(k, d):
        return remote(
            zs.at[k % 2, at((z + d) % 4, BLK, 16), :],
            za.at[k, at(z, BLK, 16), :],
            z_s.at[k % 2],
            z_r.at[k],
            peer(here, 0, d, 0, 0),
        )

    def c_copy(k):
        return remote(
            co.at[k % 2, at(1 - c, TOK, TOK), :],
            cr.at[k],
            c_s.at[k % 2],
            c_r.at[k],
            peer(here, 0, 0, 0, 1),
        )

    def whole(src, dst, send, recv):
        return remote(src, dst, send, recv, peer(here, 1, 0, 0, 0))

    def p_all(k):
        return whole(far.at[k % 2], relay.at[k], p_s.at[k % 2], p_r.at[k])

    def n_all(k):
        return whole(near.at[:, k % 2], summed.at[k], n_s.at[k % 2], n_r.at[k])

    def x_all(k):
        three = pl.ds(0, 3 * BLK)
        return whole(xs.at[k % 2, three, :], xa.at[k, three, :], x_s.at[k % 2], x_r.at[k])

    def z_all(k):
        three = pl.ds(0, 3 * BLK)
        return whole(zs.at[k % 2, three, :], za.at[k, three, :], z_s.at[k % 2], z_r.at[k])

    def xx_all(k):
        three = pl.ds(0, 3 * BLK)
        return whole(
            xs4.at[k % 2, :, three, :], xa4.at[k, :, three, :], xx_s.at[k % 2], xx_r.at[k]
        )

    def zz_all(k):
        three = pl.ds(0, 3 * BLK)
        return whole(
            zs4.at[k % 2, :, three, :], za4.at[k, :, three, :], zz_s.at[k % 2], zz_r.at[k]
        )

    def pp_all(k):
        return whole(cr4.at[k, 0], relay4.at[k], pp_s.at[k], pp_r.at[k])

    def nn_all(k):
        return whole(cr4.at[k, pl.ds(0, 2)], summed4.at[k], nn_s.at[k], nn_r.at[k])

    def late_far(k):
        for out in tiles(BW):
            far[k % 2, :, out] = partial((y + 2) % 4, tile(k, out))
        for i in range(2):
            p_copy(k, i).start()

    def late_near(k):
        p_all(k).wait_recv()
        for i in range(2):
            added, plain = slice(i * 96, i * 96 + 96), slice(96 - i * 96, 192 - i * 96)
            for out in tiles(BW):
                term = partial((y + PLUS_MINUS[i]) % 4, tile(k, out))
                both = term[added].astype(F32) + relay[k, i, :, out].astype(F32)
                near[i, k % 2, added, out] = both.astype(BF)
                near[i, k % 2, plain, out] = term[plain]
            n_copy(k, i).start()

    def late_total(k):
        n_all(k).wait_recv()
        for out in tiles(BW):
            whole = partial(y, tile(k, out)).astype(F32)
            whole = whole + summed[k, 0, :, out].astype(F32)
            whole = whole + summed[k, 1, :, out].astype(F32)
            xs[k % 2, :, out] = whole.astype(BF)
        for d in (2, 1, 3):
            x_copy(k, d).start()
        xa[k, at(x, BLK, 16), :] = xs[k % 2, at(x, BLK, 16), :]

    def late_turn(k):
        x_all(k).wait_recv()
        for out in tiles(BW):
            zs[k % 2, :, out] = nn(perm[...], xa[k, :, out]).astype(BF)
        for d in (2, 1, 3):
            z_copy(k, d).start()
        za[k, at(z, BLK, 16), :] = zs[k % 2, at(z, BLK, 16), :]

    def late_unselect(k):
        z_all(k).wait_recv()
        for out in tiles(BW):
            block = za[k, :, out]
            co[k % 2, :, out] = tn(sel[y], block).astype(BF)
        c_copy(k).start()

    def late_join(k):
        c_copy(k).wait()
        both = co[k % 2, at(c, TOK, TOK), :].astype(F32) + cr[k].astype(F32)
        grad_ref[:, cols(k)] = both.astype(BF)

    def xx_copy(k, d):
        return remote(
            xs4.at[k % 2, :, at((x + d) % 4, BLK, 16), :],
            xa4.at[k, :, at(x, BLK, 16), :],
            xx_s.at[k % 2],
            xx_r.at[k],
            peer(here, 0, 0, d, 0),
        )

    def zz_copy(k, d):
        return remote(
            zs4.at[k % 2, :, at((z + d) % 4, BLK, 16), :],
            za4.at[k, :, at(z, BLK, 16), :],
            zz_s.at[k % 2],
            zz_r.at[k],
            peer(here, 0, d, 0, 0),
        )

    def cc_copy(k):
        return remote(
            co4.at[k % 2, :, at(1 - c, TOK, TOK), :],
            cr4.at[k],
            cc_s.at[k % 2],
            cc_r.at[k],
            peer(here, 0, 0, 0, 1),
        )

    def pp_copy(k, i):
        return remote(
            cr4.at[k, (y + 2) % 4, pl.ds(i * 64, 64), :],
            relay4.at[k, i],
            pp_s.at[k],
            pp_r.at[k],
            peer(here, PLUS_MINUS[i], 0, 0, 0),
        )

    def nn_copy(k, i):
        return remote(
            cr4.at[k, (y + PLUS_MINUS[i]) % 4],
            summed4.at[k, i],
            nn_s.at[k],
            nn_r.at[k],
            peer(here, PLUS_MINUS[i], 0, 0, 0),
        )

    def early_terms(k):
        for out in tiles(CW):
            span = etile(k, out)
            term = nt(acts[0], wg[span, :]) + nt(acts[1], wu[span, :])
            xs4[k % 2, :, :, out] = term.astype(BF).reshape(4, ROWS, out.stop - out.start)
        xa4[k, :, at(x, BLK, 16), :] = xs4[k % 2, :, at(x, BLK, 16), :]
        for d in (2, 1, 3):
            xx_copy(k, d).start()

    def early_turn(k):
        xx_all(k).wait_recv()

        def block(b, carry):
            for out in tiles(CW):
                zs4[k % 2, b, :, out] = nn(perm[...], xa4[k, b, :, out]).astype(BF)
            za4[k, b, at(z, BLK, 16), :] = zs4[k % 2, b, at(z, BLK, 16), :]
            return carry

        lax.fori_loop(0, 4, block, 0)
        for d in (2, 1, 3):
            zz_copy(k, d).start()

    def early_unselect(k):
        zz_all(k).wait_recv()

        def block(b, carry):
            for out in tiles(CW):
                co4[k % 2, b, :, out] = tn(sel[b], za4[k, b, :, out]).astype(BF)
            return carry

        lax.fori_loop(0, 4, block, 0)
        cc_copy(k).start()

    def early_far(k):
        cc_copy(k).wait()

        def block(b, carry):
            both = co4[k % 2, b, at(c, TOK, TOK), :].astype(F32) + cr4[k, b].astype(F32)
            cr4[k, b] = both.astype(BF)
            return carry

        lax.fori_loop(0, 4, block, 0)
        for i in range(2):
            pp_copy(k, i).start()

    def early_near(k):
        pp_all(k).wait_recv()
        for i in range(2):
            block, added = (y + PLUS_MINUS[i]) % 4, slice(i * 64, i * 64 + 64)
            both = cr4[k, block, added, :].astype(F32) + relay4[k, i].astype(F32)
            cr4[k, block, added, :] = both.astype(BF)
            nn_copy(k, i).start()

    def early_join(k):
        nn_all(k).wait()
        both = cr4[k, y].astype(F32)
        for i in range(2):
            both = both + summed4[k, i].astype(F32)
        grad_ref[:, ecols(k)] = both.astype(BF)

    def weight_grads(k):
        for a in range(2):
            stage_copy(a, k).wait()

        @pl.when(k + 1 < BC)
        def _():
            for a in range(2):
                stage_copy(a, k + 1).start()

        for out in tiles(BW):
            cot_rows = stage[1, k % 2, :, :, out].reshape(4 * ROWS, SUB)
            tok_rows = stage[0, k % 2, :, :, out].reshape(4 * ROWS, SUB)
            down = nn(acts_t[0], cot_rows)
            dw[:, tile(k, out)] = down
            gate = nn(acts_t[1], tok_rows)
            up = nn(acts_t[2], tok_rows)
            sq = down * down + gate * gate + up * up
            squares[...] += sq[:, 0:128] + sq[:, 128:256]

    def update(k):
        @pl.when(k == 0)
        def _():
            mean = jnp.sum(squares[...], axis=1, keepdims=True) / (3.0 * D)
            old = jnp.broadcast_to(moment_ref[...], (128, Q)).T
            second = moment_decay * old + (1.0 - moment_decay) * mean
            second_ref[...] = second.T[0:1, :]
            squares[...] = 1.0 / (jnp.sqrt(second) + epsilon)

        for j in range(BW // 128):
            out = pl.ds(pl.multiple_of(k * BW + j * 128, 128), 128)
            update_ref[:, out] = (dw[:, out] * squares[...]).astype(BF)

    def drain(copy):
        return lambda k: copy(k).wait_send()

    def step(t, carry):
        when(t - 2, B_LATE, drain(p_all))
        when(t - 3, B_LATE, drain(n_all))
        when(t - 4, B_LATE, drain(x_all))
        when(t - 5, B_LATE, drain(z_all))
        when(t - 2, B_EARLY, drain(xx_all))
        when(t - 3, B_EARLY, drain(zz_all))
        when(t - 5, B_EARLY, drain(pp_all))

        @pl.when(t == 1)
        def _():
            for copy in weights[4:]:
                copy.wait()

        when(t, B_LATE, late_far)
        when(t, B_EARLY, early_terms)
        when(t - 1, B_LATE, late_near)
        when(t - 1, B_EARLY, early_turn)
        when(t - 2, B_LATE, late_total)
        when(t - 2, B_EARLY, early_unselect)
        when(t - 3, B_LATE, late_turn)
        when(t - 3, B_EARLY, early_far)
        when(t - 4, B_LATE, late_unselect)
        when(t - 4, B_EARLY, early_near)
        when(t - 5, B_LATE, late_join)
        when(t - 5, B_EARLY, early_join)
        for n in range(2):
            when(t * 2 + n, BC, weight_grads)
        for n in range(3):
            when((t - BC // 2) * 3 + n, BC, update)
        return carry

    lax.fori_loop(0, B_LATE + 5, step, 0)


def shards(tokens, grad_out, routes, gate_prob, w_gate, w_up, w_down, moment_prev):
    vmem = pl.BlockSpec(memory_space=pltpu.VMEM)
    hbm = pl.BlockSpec(memory_space=pltpu.HBM)
    dma = pltpu.SemaphoreType.DMA

    def held(*shape):
        return pltpu.VMEM(shape, BF)

    rows, acts, acts_t, sel = pl.pallas_call(
        forward_kernel,
        name="dispatch",
        out_shape=(
            jax.ShapeDtypeStruct((2, 4, ROWS, D), BF),
            jax.ShapeDtypeStruct((2, 4 * ROWS, Q), BF),
            jax.ShapeDtypeStruct((3, Q, 4 * ROWS), BF),
            jax.ShapeDtypeStruct((4, ROWS, 2 * TOK), BF),
        ),
        in_specs=[vmem, vmem, hbm, hbm, hbm, hbm, hbm],
        out_specs=(hbm, vmem, vmem, vmem),
        scratch_shapes=[
            pltpu.VMEM((4, 2, 8, TOK), F32),
            pltpu.VMEM((4, ROWS, 128), F32),
            held(ROWS, ROWS),
            held(F_LATE, 2 * TOK, FW),
            held(2, ROWS, FW),
            held(F_LATE, ROWS, FW),
            held(2, ROWS, FW),
            held(F_EARLY, 4, 2 * TOK, EW),
            held(2, 4, ROWS, EW),
            held(F_EARLY, 4, ROWS, EW),
            held(2, 4, ROWS, EW),
            held(2, 4, ROWS, FW),
            held(2, 4, ROWS, EW),
            pltpu.VMEM((3, 4 * ROWS, Q), F32),
            held(D, Q),
            held(D, Q),
            held(Q, D),
            dma((3,)),
            dma((7,)),
            dma((7,)),
            dma((F_LATE,)),
            dma((F_LATE,)),
            dma((F_LATE,)),
            dma((2,)),
            dma((F_LATE,)),
            dma((2,)),
            dma((F_LATE,)),
            dma((2,)),
            dma((F_LATE,)),
            dma((F_LATE,)),
            dma((F_LATE,)),
            dma((F_LATE,)),
            dma((2,)),
            dma((F_EARLY,)),
            dma((F_EARLY,)),
            dma((F_EARLY,)),
            dma((F_EARLY,)),
            dma((F_EARLY,)),
            dma((F_EARLY,)),
            dma((F_EARLY,)),
            dma((F_EARLY,)),
            dma((F_EARLY,)),
            dma((2,)),
            dma((F_EARLY,)),
            dma((2,)),
            dma((F_EARLY,)),
            dma((2,)),
            dma((2,)),
        ],
        compiler_params=pltpu.CompilerParams(
            collective_id=0, has_side_effects=True, vmem_limit_bytes=60 * 2**20
        ),
    )(
        routes.reshape(1, TOK),
        gate_prob.reshape(1, TOK),
        tokens,
        grad_out,
        w_gate[0],
        w_up[0],
        w_down[0],
    )
    grad_in, update, second = pl.pallas_call(
        backward_kernel,
        name="combine",
        out_shape=(
            jax.ShapeDtypeStruct((TOK, D), BF),
            jax.ShapeDtypeStruct((Q, D), BF),
            jax.ShapeDtypeStruct((1, Q), F32),
        ),
        in_specs=[vmem, vmem, vmem, hbm, hbm, hbm, vmem],
        out_specs=(vmem, vmem, vmem),
        scratch_shapes=[
            held(ROWS, ROWS),
            held(2, ROWS, BW),
            held(B_LATE, 2, 96, BW),
            held(2, 2, ROWS, BW),
            held(B_LATE, 2, ROWS, BW),
            held(2, ROWS, BW),
            held(B_LATE, ROWS, BW),
            held(2, ROWS, BW),
            held(B_LATE, ROWS, BW),
            held(2, 2 * TOK, BW),
            held(B_LATE, TOK, BW),
            held(2, 4, ROWS, CW),
            held(B_EARLY, 4, ROWS, CW),
            held(2, 4, ROWS, CW),
            held(B_EARLY, 4, ROWS, CW),
            held(2, 4, 2 * TOK, CW),
            held(B_EARLY, 4, TOK, CW),
            held(B_EARLY, 2, 64, CW),
            held(B_EARLY, 2, TOK, CW),
            held(2, 2, 4, ROWS, BW),
            pltpu.VMEM((Q, D), F32),
            pltpu.VMEM((Q, 128), F32),
            held(D, Q),
            held(D, Q),
            dma((4, 2)),
            dma((2,)),
            dma((B_LATE,)),
            dma((2,)),
            dma((B_LATE,)),
            dma((2,)),
            dma((B_LATE,)),
            dma((2,)),
            dma((B_LATE,)),
            dma((2,)),
            dma((B_LATE,)),
            dma((2,)),
            dma((B_EARLY,)),
            dma((2,)),
            dma((B_EARLY,)),
            dma((2,)),
            dma((B_EARLY,)),
            dma((B_EARLY,)),
            dma((B_EARLY,)),
            dma((B_EARLY,)),
            dma((B_EARLY,)),
            dma((2, 2)),
        ],
        compiler_params=pltpu.CompilerParams(
            collective_id=1, has_side_effects=True, vmem_limit_bytes=60 * 2**20
        ),
    )(acts, acts_t, sel, rows, w_gate[0], w_up[0], moment_prev)
    return grad_in, update[None], second


def solution(mesh):
    placed = (
        P(("dp", "expert"), None),
        P(("dp", "expert"), None),
        P(("dp", "expert"), None),
        P(("dp", "expert"), None),
        P("expert", None, "dp"),
        P("expert", None, "dp"),
        P("expert", "dp", None),
        P("expert", "dp"),
    )
    return jax.shard_map(
        shards,
        mesh=mesh,
        in_specs=placed,
        out_specs=(P(("dp", "expert"), None), P("expert", "dp", None), P("expert", "dp")),
        check_vma=False,
    )
```

```python
import functools

import jax
import jax.numpy as jnp
from jax import lax
from jax.experimental import pallas as pl
from jax.experimental.pallas import tpu as pltpu
from jax.sharding import PartitionSpec as P

MESH = pl.DeviceIdType.MESH
BF = jnp.bfloat16
F32 = jnp.float32

moment_decay = 0.95
epsilon = 1e-08

D = 7168
TOK = 128
CAP = 6
Q = 256
ROWS = 192
BLK = 48
SUB = 256

FW = 512
FC = D // FW
EW = 384
F_EARLY = 16
F_DONE = F_EARLY * EW // FW
F_LATE = 2 * FC - F_DONE
BW = 512
BC = D // BW
CW = 384
B_EARLY = 8
B_LATE = (D - B_EARLY * CW) // BW
B_FROM = B_LATE * BW

ACROSS = ((0, 0, 0, 1),) + tuple((0, d, 0, 0) for d in (1, 2, 3)) + tuple((0, 0, d, 0) for d in (1, 2, 3))
COLUMN = ((1, 0, 0, 0), (3, 0, 0, 0), (2, 0, 0, 0), (1, 0, 0, 1), (3, 0, 0, 1), (2, 0, 0, 1))
PLUS_MINUS = (1, 3)


def place():
    y = lax.axis_index("dp")
    e = lax.axis_index("expert")
    return y, e // 8, (e // 2) % 4, e % 2


def peer(here, dy, dz, dx, dc):
    y, z, x, c = here
    expert = (((z + dz) % 4) * 4 + (x + dx) % 4) * 2 + (c + dc) % 2
    return {"dp": (y + dy) % 4, "expert": expert}


def remote(src, dst, send, recv, device):
    return pltpu.make_async_remote_copy(
        src_ref=src,
        dst_ref=dst,
        send_sem=send,
        recv_sem=recv,
        device_id=device,
        device_id_type=MESH,
    )


def greet(here, partners):
    barrier = pltpu.get_barrier_semaphore()
    for offset in partners:
        pl.semaphore_signal(barrier, inc=1, device_id=peer(here, *offset), device_id_type=MESH)
    return lambda: pl.semaphore_wait(barrier, len(partners))


def at(index, size, align):
    return pl.ds(pl.multiple_of(index * size, align), size)


def nt(a, b):
    return lax.dot_general(a, b, (((1,), (1,)), ((), ())), preferred_element_type=F32)


def tn(a, b):
    return lax.dot_general(a, b, (((0,), (0,)), ((), ())), preferred_element_type=F32)


def nn(a, b):
    return jnp.dot(a, b, preferred_element_type=F32)


def tiles(width):
    return [slice(j, min(j + SUB, width)) for j in range(0, width, SUB)]


def swap_matrix():
    out = lax.broadcasted_iota(jnp.int32, (ROWS, ROWS), 0)
    row = lax.broadcasted_iota(jnp.int32, (ROWS, ROWS), 1)

    def steps(value, size):
        return sum((value >= size * n).astype(jnp.int32) for n in (1, 2, 3))

    outer = steps(out, 48)
    inner = steps(out - 48 * outer, 12)
    return (row - out == 36 * (inner - outer)).astype(F32).astype(BF)


def when(k, count, body):
    pl.when((k >= 0) & (k < count))(lambda: body(k))


def forward_kernel(
    routes_ref,
    prob_ref,
    tok_ref,
    cot_ref,
    wg_hbm,
    wu_hbm,
    wd_hbm,
    rows,
    acts,
    sel,
    metas,
    gp,
    perm,
    raw,
    zs,
    za,
    xs,
    raw4,
    zs4,
    za4,
    xs4,
    stage,
    stage4,
    acc,
    wg,
    wu,
    wd,
    w_sem,
    m_s,
    m_r,
    raw_l,
    raw_s,
    raw_r,
    z_s,
    z_r,
    x_s,
    x_r,
    x_l,
    y_s,
    y_r,
    f_s,
    f_r,
    st_l,
    own_l,
    own_s,
    own_r,
    yy_s,
    yy_r,
    ff_s,
    ff_r,
    cc_s,
    cc_r,
    zz_s,
    zz_r,
    xx_s,
    xx_r,
    xx_l,
    st4_l,
):
    here = place()
    y, z, x, c = here
    mine = at(c, TOK, TOK)

    def cols(k):
        return at(k, FW, 128)

    def ecols(k):
        return at(k, EW, 128)

    met = greet(here, ACROSS + COLUMN)
    weights = [
        pltpu.make_async_copy(src, dst, w_sem.at[i])
        for i, (src, dst) in enumerate(((wg_hbm, wg), (wu_hbm, wu), (wd_hbm, wd)))
    ]

    first = lax.broadcasted_iota(jnp.int32, (8, TOK), 0) == 0
    metas[y, c] = jnp.where(first, routes_ref[...].astype(F32), prob_ref[...])
    others = COLUMN + ((0, 0, 0, 1),)

    def meta_copy(i):
        return remote(
            metas.at[y, c], metas.at[y, c], m_s.at[i], m_r.at[i], peer(here, *others[i])
        )

    def yy_copy(k, i):
        return remote(
            cot_ref.at[:, ecols(k)],
            raw4.at[k, y, mine, :],
            yy_s.at[k],
            yy_r.at[k],
            peer(here, PLUS_MINUS[i], 0, 0, 0),
        )

    def ff_copy(k, i):
        src = (y + PLUS_MINUS[1 - i]) % 4
        half = raw4.at[k, src, pl.ds(pl.multiple_of(c * TOK + i * 64, 64), 64), :]
        return remote(
            half, half, ff_s.at[k], ff_r.at[k], peer(here, PLUS_MINUS[i], 0, 0, 0)
        )

    def cc_copy(k, i):
        block = raw4.at[k, (y + (3, 1, 2)[i]) % 4, mine, :]
        return remote(block, block, cc_s.at[k], cc_r.at[k], peer(here, 0, 0, 0, 1))

    def own_local(k):
        return pltpu.make_async_copy(
            cot_ref.at[:, ecols(k)], raw4.at[k, y, mine, :], own_l.at[k]
        )

    def own_remote(k):
        return remote(
            cot_ref.at[:, ecols(k)],
            raw4.at[k, y, mine, :],
            own_s.at[k],
            own_r.at[k],
            peer(here, 0, 0, 0, 1),
        )

    def zz_copy(k, d):
        return remote(
            zs4.at[k % 2, :, at((z + d) % 4, BLK, 16), :],
            za4.at[k, :, at(z, BLK, 16), :],
            zz_s.at[k % 2],
            zz_r.at[k],
            peer(here, 0, d, 0, 0),
        )

    def xx_copy(k, d):
        return remote(
            xs4.at[k % 2, :, at((x + d) % 4, BLK, 16), :],
            rows.at[1, :, at(x, BLK, 16), ecols(k)],
            xx_s.at[k % 2],
            xx_r.at[k],
            peer(here, 0, 0, d, 0),
        )

    def xx_own(k):
        return pltpu.make_async_copy(
            xs4.at[k % 2, :, at(x, BLK, 16), :],
            rows.at[1, :, at(x, BLK, 16), ecols(k)],
            xx_l.at[k % 2],
        )

    def stage4_copy(k):
        return pltpu.make_async_copy(
            rows.at[1, :, :, ecols(k)], stage4.at[k % 2], st4_l.at[k % 2]
        )

    def yy_all(k):
        both = raw4.at[k, pl.ds(0, 2), mine, :]
        return remote(both, both, yy_s.at[k], yy_r.at[k], peer(here, 1, 0, 0, 0))

    def ff_all(k):
        both = raw4.at[k, 0, mine, :]
        return remote(both, both, ff_s.at[k], ff_r.at[k], peer(here, 1, 0, 0, 0))

    def cc_all(k):
        three = raw4.at[k, pl.ds(0, 3), mine, :]
        return remote(three, three, cc_s.at[k], cc_r.at[k], peer(here, 0, 0, 0, 1))

    def zz_all(k):
        return remote(
            zs4.at[k % 2, :, pl.ds(0, 3 * BLK), :],
            za4.at[k, :, pl.ds(0, 3 * BLK), :],
            zz_s.at[k % 2],
            zz_r.at[k],
            peer(here, 0, 1, 0, 0),
        )

    def xx_all(k):
        return remote(
            xs4.at[k % 2, :, pl.ds(0, 3 * BLK), :],
            rows.at[1, :, pl.ds(0, 3 * BLK), ecols(k)],
            xx_s.at[k % 2],
            xx_r.at[k],
            peer(here, 0, 0, 1, 0),
        )

    def early_send(k):
        for i in range(2):
            yy_copy(k, i).start()

    def early_own(k):
        own_local(k).start()
        own_remote(k).start()

    def early_pass(k):
        yy_all(k).wait_recv()
        for i in range(2):
            ff_copy(k, i).start()
            cc_copy(k, i).start()

    def early_rest(k):
        ff_all(k).wait_recv()
        cc_copy(k, 2).start()

    def early_select(k):
        own_local(k).wait()
        own_remote(k).wait()
        cc_all(k).wait_recv()

        def block(b, carry):
            for out in tiles(EW):
                picked = nn(sel[b], raw4[k, b, :, out]) * gp[b, :, 0:1]
                zs4[k % 2, b, :, out] = picked.astype(BF)
            za4[k, b, at(z, BLK, 16), :] = zs4[k % 2, b, at(z, BLK, 16), :]
            return carry

        lax.fori_loop(0, 4, block, 0)
        for d in (2, 1, 3):
            zz_copy(k, d).start()

    def early_turn(k):
        zz_all(k).wait_recv()

        def block(b, carry):
            for out in tiles(EW):
                xs4[k % 2, b, :, out] = nn(perm[...], za4[k, b, :, out]).astype(BF)
            return carry

        lax.fori_loop(0, 4, block, 0)
        for d in (2, 1, 3):
            xx_copy(k, d).start()
        xx_own(k).start()

    def early_fetch(k):
        xx_all(k).wait_recv()
        xx_own(k).wait()
        stage4_copy(k).start()

    def early_accumulate(k):
        stage4_copy(k).wait()
        acc[2] += nt(stage4[k % 2].reshape(4 * ROWS, EW), wd[:, ecols(k)])

    def which(i):
        a = i // FC
        return a, cols(i - a * (FC - F_DONE))

    def raw_start(i):
        def begin(src):
            dst = raw.at[i, mine, :]
            pltpu.make_async_copy(src, dst, raw_l.at[i]).start()
            remote(src, dst, raw_s.at[i], raw_r.at[i], peer(here, 0, 0, 0, 1)).start()

        pl.when(i // FC == 0)(lambda: begin(tok_ref.at[:, cols(i)]))
        pl.when(i // FC == 1)(lambda: begin(cot_ref.at[:, cols(i - FC + F_DONE)]))

    def raw_waits(i):
        src = tok_ref.at[:, cols(0)]
        dst = raw.at[i, mine, :]
        return (
            pltpu.make_async_copy(src, dst, raw_l.at[i]),
            remote(src, dst, raw_s.at[i], raw_r.at[i], peer(here, 0, 0, 0, 1)),
        )

    def z_copy(i, d):
        return remote(
            zs.at[i % 2, at((z + d) % 4, BLK, 16), :],
            za.at[i, at(z, BLK, 16), :],
            z_s.at[i % 2],
            z_r.at[i],
            peer(here, 0, d, 0, 0),
        )

    def x_copy(i, d):
        a, span = which(i)
        return remote(
            xs.at[i % 2, at((x + d) % 4, BLK, 16), :],
            rows.at[a, y, at(x, BLK, 16), span],
            x_s.at[i % 2],
            x_r.at[i],
            peer(here, 0, 0, d, 0),
        )

    def x_own(i):
        a, span = which(i)
        return pltpu.make_async_copy(
            xs.at[i % 2, at(x, BLK, 16), :], rows.at[a, y, at(x, BLK, 16), span], x_l.at[i % 2]
        )

    def y_copy(i, p):
        a, span = which(i)
        block = rows.at[a, y, :, span]
        return remote(
            block, block, y_s.at[i], y_r.at[i], peer(here, PLUS_MINUS[p], 0, 0, 0)
        )

    def f_copy(i, p):
        a, span = which(i)
        half = rows.at[a, (y + PLUS_MINUS[1 - p]) % 4, pl.ds(p * 96, 96), span]
        return remote(half, half, f_s.at[i], f_r.at[i], peer(here, PLUS_MINUS[p], 0, 0, 0))

    def stage_copy(i):
        a, span = which(i)
        return pltpu.make_async_copy(rows.at[a, :, :, span], stage.at[i % 2], st_l.at[i % 2])

    def z_all(i):
        return remote(
            zs.at[i % 2, pl.ds(0, 3 * BLK), :],
            za.at[i, pl.ds(0, 3 * BLK), :],
            z_s.at[i % 2],
            z_r.at[i],
            peer(here, 0, 1, 0, 0),
        )

    def x_all(i):
        a, span = which(i)
        return remote(
            xs.at[i % 2, pl.ds(0, 3 * BLK), :],
            rows.at[a, y, pl.ds(0, 3 * BLK), span],
            x_s.at[i % 2],
            x_r.at[i],
            peer(here, 0, 0, 1, 0),
        )

    def y_all(i):
        a, span = which(i)
        both = rows.at[a, pl.ds(0, 2), :, span]
        return remote(both, both, y_s.at[i], y_r.at[i], peer(here, 1, 0, 0, 0))

    def f_all(i):
        a, span = which(i)
        both = rows.at[a, y, :, span]
        return remote(both, both, f_s.at[i], f_r.at[i], peer(here, 1, 0, 0, 0))

    def late_select(i):
        for copy in raw_waits(i):
            copy.wait()
        scale = jnp.where(i // FC == 1, gp[y], 1.0)[:, 0:1]
        for out in tiles(FW):
            zs[i % 2, :, out] = (nn(sel[y], raw[i, :, out]) * scale).astype(BF)
        for d in (2, 1, 3):
            z_copy(i, d).start()
        za[i, at(z, BLK, 16), :] = zs[i % 2, at(z, BLK, 16), :]

    def late_turn(i):
        z_all(i).wait_recv()
        for out in tiles(FW):
            xs[i % 2, :, out] = nn(perm[...], za[i, :, out]).astype(BF)
        for d in (2, 1, 3):
            x_copy(i, d).start()
        x_own(i).start()

    def late_spread(i):
        x_all(i).wait_recv()
        x_own(i).wait()
        for p in range(2):
            y_copy(i, p).start()

    def late_pass(i):
        y_all(i).wait_recv()
        for p in range(2):
            f_copy(i, p).start()

    def late_fetch(i):
        f_all(i).wait_recv()
        stage_copy(i).start()

    def late_accumulate(i):
        stage_copy(i).wait()
        a, span = which(i)

        @pl.when(a == 0)
        def _():
            held = stage[i % 2].reshape(4 * ROWS, FW)
            acc[0] += nn(held, wg[span, :])
            acc[1] += nn(held, wu[span, :])

        @pl.when(a == 1)
        def _():
            acc[2] += nt(stage[i % 2].reshape(4 * ROWS, FW), wd[:, span])

    def drain(copy):
        return lambda k: copy(k).wait_send()

    perm[...] = swap_matrix()
    acc[...] = jnp.zeros_like(acc)
    met()
    for i in range(len(others)):
        meta_copy(i).start()
    early_send(0)
    early_send(1)
    for i in range(2):
        raw_start(i)
    early_own(0)
    early_own(1)
    for copy in weights:
        copy.start()
    for i in range(len(others)):
        meta_copy(i).wait()

    def plan(b, carry):
        earlier = (
            (
                lax.broadcasted_iota(jnp.int32, (TOK, TOK), 0)
                < lax.broadcasted_iota(jnp.int32, (TOK, TOK), 1)
            )
            .astype(F32)
            .astype(BF)
        )
        weight = jnp.zeros((ROWS, 1), F32)
        for m in range(2):
            route = metas[b, m, 0:1, :].astype(jnp.int32)
            prob = metas[b, m, 1:2, :]
            onehot = (lax.broadcasted_iota(jnp.int32, (32, TOK), 0) == route).astype(F32)
            before = nn(onehot.astype(BF), earlier)
            slot = jnp.sum(onehot * before, axis=0, keepdims=True).astype(jnp.int32)
            row = ((route >> 1) * 2 + m) * CAP + slot
            row = jnp.where((route & 1) == c, row, -1)
            chosen = lax.broadcasted_iota(jnp.int32, (ROWS, TOK), 0) == row
            sel[b, :, m * TOK : (m + 1) * TOK] = chosen.astype(F32).astype(BF)
            weight = weight + jnp.sum(jnp.where(chosen, prob, 0.0), axis=1, keepdims=True)
        gp[b] = jnp.broadcast_to(weight, (ROWS, 128))
        return carry

    lax.fori_loop(0, 4, plan, 0)

    def step(t, carry):
        when(t - 2, F_LATE, drain(z_all))
        when(t - 3, F_LATE, drain(x_all))
        when(t - 4, F_LATE, drain(y_all))
        when(t - 5, F_LATE, drain(f_all))
        when(t, F_EARLY, drain(yy_all))
        when(t - 1, F_EARLY, drain(ff_all))
        when(t - 2, F_EARLY, drain(cc_all))
        when(t - 3, F_EARLY, drain(zz_all))
        when(t - 4, F_EARLY, drain(xx_all))

        when(t, F_LATE, late_select)
        when(t + 2, F_EARLY, early_send)
        when(t + 2, F_EARLY, early_own)
        when(t + 2, F_LATE, raw_start)
        when(t + 1, F_EARLY, early_pass)
        when(t - 1, F_LATE, late_turn)
        when(t, F_EARLY, early_rest)
        when(t - 2, F_LATE, late_spread)
        when(t - 1, F_EARLY, early_select)
        when(t - 3, F_LATE, late_pass)
        when(t - 2, F_EARLY, early_turn)
        when(t - 4, F_LATE, late_fetch)
        when(t - 3, F_EARLY, early_fetch)

        @pl.when(t == 4)
        def _():
            for copy in weights:
                copy.wait()

        when(t - 5, F_LATE, late_accumulate)
        when(t - 4, F_EARLY, early_accumulate)
        return carry

    early_pass(0)
    lax.fori_loop(0, F_LATE + 5, step, 0)

    def finish(b, carry):
        part = at(b, Q, 256)
        gate, up, grad = acc[0, part, :], acc[1, part, :], acc[2, part, :]
        sig = jax.nn.sigmoid(gate)
        silu = gate * sig
        hidden = silu * up
        gate_grad = grad * up * sig * (1.0 + gate * (1.0 - sig))
        up_grad = grad * silu
        acts[0, part, :] = gate_grad.astype(BF)
        acts[1, part, :] = up_grad.astype(BF)
        acts[2, part, :] = hidden.astype(BF)
        return carry

    lax.fori_loop(0, 3, finish, 0)


def backward_kernel(
    acts,
    sel,
    rows,
    wg_hbm,
    wu_hbm,
    moment_ref,
    grad_hbm,
    update_hbm,
    second_ref,
    acts_t,
    grad_ref,
    update_ref,
    perm,
    far,
    relay,
    near,
    summed,
    xs,
    xa,
    zs,
    za,
    co,
    cr,
    xs4,
    xa4,
    zs4,
    za4,
    co4,
    cr4,
    relay4,
    summed4,
    stage,
    dw,
    squares,
    wg,
    wu,
    w_sem,
    p_s,
    p_r,
    n_s,
    n_r,
    x_s,
    x_r,
    z_s,
    z_r,
    c_s,
    c_r,
    xx_s,
    xx_r,
    zz_s,
    zz_r,
    cc_s,
    cc_r,
    pp_s,
    pp_r,
    nn_s,
    nn_r,
    st_l,
    out_l,
):
    here = place()
    y, z, x, c = here

    def cols(k):
        return at(k, BW, 128)

    def grad_out(span):
        return pltpu.make_async_copy(grad_ref.at[:, span], grad_hbm.at[:, span], out_l.at[0])

    def update_out(span):
        return pltpu.make_async_copy(update_ref.at[:, span], update_hbm.at[:, span], out_l.at[1])

    def ecols(k):
        return pl.ds(pl.multiple_of(B_FROM + k * CW, 128), CW)

    def tile(k, out):
        return pl.ds(pl.multiple_of(k * BW + out.start, 128), out.stop - out.start)

    def etile(k, out):
        return pl.ds(pl.multiple_of(B_FROM + k * CW + out.start, 128), out.stop - out.start)

    met = greet(here, ACROSS + COLUMN[:2])
    spans = ((0, BW), (B_FROM, CW), (BW, B_FROM - BW), (B_FROM + CW, D - B_FROM - CW))
    weights = [
        pltpu.make_async_copy(
            src.at[pl.ds(first, size)], dst.at[pl.ds(first, size)], w_sem.at[n, i]
        )
        for n, (first, size) in enumerate(spans)
        for i, (src, dst) in enumerate(((wg_hbm, wg), (wu_hbm, wu)))
    ]
    for copy in weights:
        copy.start()

    def stage_copy(a, k):
        return pltpu.make_async_copy(
            rows.at[a, :, :, cols(k)], stage.at[a, k % 2], st_l.at[a, k % 2]
        )

    for a in range(2):
        stage_copy(a, 0).start()
    squares[...] = jnp.zeros_like(squares)
    perm[...] = swap_matrix()
    met()
    for copy in weights[:4]:
        copy.wait()

    def partial(block, span):
        block_rows = at(block, ROWS, 16)
        total = nt(acts[0, block_rows, :], wg[span, :])
        total = total + nt(acts[1, block_rows, :], wu[span, :])
        return total.astype(BF)

    def p_copy(k, i):
        return remote(
            far.at[k % 2, pl.ds(i * 96, 96), :],
            relay.at[k, i],
            p_s.at[k % 2],
            p_r.at[k],
            peer(here, PLUS_MINUS[i], 0, 0, 0),
        )

    def n_copy(k, i):
        return remote(
            near.at[i, k % 2],
            summed.at[k, i],
            n_s.at[k % 2],
            n_r.at[k],
            peer(here, PLUS_MINUS[i], 0, 0, 0),
        )

    def x_copy(k, d):
        return remote(
            xs.at[k % 2, at((x + d) % 4, BLK, 16), :],
            xa.at[k, at(x, BLK, 16), :],
            x_s.at[k % 2],
            x_r.at[k],
            peer(here, 0, 0, d, 0),
        )

    def z_copy(k, d):
        return remote(
            zs.at[k % 2, at((z + d) % 4, BLK, 16), :],
            za.at[k, at(z, BLK, 16), :],
            z_s.at[k % 2],
            z_r.at[k],
            peer(here, 0, d, 0, 0),
        )

    def c_copy(k):
        return remote(
            co.at[k % 2, at(1 - c, TOK, TOK), :],
            cr.at[k],
            c_s.at[k % 2],
            c_r.at[k],
            peer(here, 0, 0, 0, 1),
        )

    def whole(src, dst, send, recv):
        return remote(src, dst, send, recv, peer(here, 1, 0, 0, 0))

    def p_all(k):
        return whole(far.at[k % 2], relay.at[k], p_s.at[k % 2], p_r.at[k])

    def n_all(k):
        return whole(near.at[:, k % 2], summed.at[k], n_s.at[k % 2], n_r.at[k])

    def x_all(k):
        three = pl.ds(0, 3 * BLK)
        return whole(xs.at[k % 2, three, :], xa.at[k, three, :], x_s.at[k % 2], x_r.at[k])

    def z_all(k):
        three = pl.ds(0, 3 * BLK)
        return whole(zs.at[k % 2, three, :], za.at[k, three, :], z_s.at[k % 2], z_r.at[k])

    def xx_all(k):
        three = pl.ds(0, 3 * BLK)
        return whole(
            xs4.at[k % 2, :, three, :], xa4.at[k, :, three, :], xx_s.at[k % 2], xx_r.at[k]
        )

    def zz_all(k):
        three = pl.ds(0, 3 * BLK)
        return whole(
            zs4.at[k % 2, :, three, :], za4.at[k, :, three, :], zz_s.at[k % 2], zz_r.at[k]
        )

    def pp_all(k):
        return whole(cr4.at[k, 0], relay4.at[k], pp_s.at[k], pp_r.at[k])

    def nn_all(k):
        return whole(cr4.at[k, pl.ds(0, 2)], summed4.at[k], nn_s.at[k], nn_r.at[k])

    def late_far(k):
        for out in tiles(BW):
            far[k % 2, :, out] = partial((y + 2) % 4, tile(k, out))
        for i in range(2):
            p_copy(k, i).start()

    def late_near(k):
        p_all(k).wait_recv()
        for i in range(2):
            added, plain = slice(i * 96, i * 96 + 96), slice(96 - i * 96, 192 - i * 96)
            for out in tiles(BW):
                term = partial((y + PLUS_MINUS[i]) % 4, tile(k, out))
                both = term[added].astype(F32) + relay[k, i, :, out].astype(F32)
                near[i, k % 2, added, out] = both.astype(BF)
                near[i, k % 2, plain, out] = term[plain]
            n_copy(k, i).start()

    def late_total(k):
        n_all(k).wait_recv()
        for out in tiles(BW):
            whole = partial(y, tile(k, out)).astype(F32)
            whole = whole + summed[k, 0, :, out].astype(F32)
            whole = whole + summed[k, 1, :, out].astype(F32)
            xs[k % 2, :, out] = whole.astype(BF)
        for d in (2, 1, 3):
            x_copy(k, d).start()
        xa[k, at(x, BLK, 16), :] = xs[k % 2, at(x, BLK, 16), :]

    def late_turn(k):
        x_all(k).wait_recv()
        for out in tiles(BW):
            zs[k % 2, :, out] = nn(perm[...], xa[k, :, out]).astype(BF)
        for d in (2, 1, 3):
            z_copy(k, d).start()
        za[k, at(z, BLK, 16), :] = zs[k % 2, at(z, BLK, 16), :]

    def late_unselect(k):
        z_all(k).wait_recv()
        for out in tiles(BW):
            block = za[k, :, out]
            co[k % 2, :, out] = tn(sel[y], block).astype(BF)
        c_copy(k).start()

    def late_join(k):
        c_copy(k).wait()
        both = co[k % 2, at(c, TOK, TOK), :].astype(F32) + cr[k].astype(F32)
        grad_ref[:, cols(k)] = both.astype(BF)
        grad_out(cols(k)).start()

    def xx_copy(k, d):
        return remote(
            xs4.at[k % 2, :, at((x + d) % 4, BLK, 16), :],
            xa4.at[k, :, at(x, BLK, 16), :],
            xx_s.at[k % 2],
            xx_r.at[k],
            peer(here, 0, 0, d, 0),
        )

    def zz_copy(k, d):
        return remote(
            zs4.at[k % 2, :, at((z + d) % 4, BLK, 16), :],
            za4.at[k, :, at(z, BLK, 16), :],
            zz_s.at[k % 2],
            zz_r.at[k],
            peer(here, 0, d, 0, 0),
        )

    def cc_copy(k):
        return remote(
            co4.at[k % 2, :, at(1 - c, TOK, TOK), :],
            cr4.at[k],
            cc_s.at[k % 2],
            cc_r.at[k],
            peer(here, 0, 0, 0, 1),
        )

    def pp_copy(k, i):
        return remote(
            cr4.at[k, (y + 2) % 4, pl.ds(i * 64, 64), :],
            relay4.at[k, i],
            pp_s.at[k],
            pp_r.at[k],
            peer(here, PLUS_MINUS[i], 0, 0, 0),
        )

    def nn_copy(k, i):
        return remote(
            cr4.at[k, (y + PLUS_MINUS[i]) % 4],
            summed4.at[k, i],
            nn_s.at[k],
            nn_r.at[k],
            peer(here, PLUS_MINUS[i], 0, 0, 0),
        )

    def early_terms(k):
        for out in tiles(CW):
            span = etile(k, out)
            term = nt(acts[0], wg[span, :]) + nt(acts[1], wu[span, :])
            xs4[k % 2, :, :, out] = term.astype(BF).reshape(4, ROWS, out.stop - out.start)
        xa4[k, :, at(x, BLK, 16), :] = xs4[k % 2, :, at(x, BLK, 16), :]
        for d in (2, 1, 3):
            xx_copy(k, d).start()

    def early_turn(k):
        xx_all(k).wait_recv()

        def block(b, carry):
            for out in tiles(CW):
                zs4[k % 2, b, :, out] = nn(perm[...], xa4[k, b, :, out]).astype(BF)
            za4[k, b, at(z, BLK, 16), :] = zs4[k % 2, b, at(z, BLK, 16), :]
            return carry

        lax.fori_loop(0, 4, block, 0)
        for d in (2, 1, 3):
            zz_copy(k, d).start()

    def early_unselect(k):
        zz_all(k).wait_recv()

        def block(b, carry):
            for out in tiles(CW):
                co4[k % 2, b, :, out] = tn(sel[b], za4[k, b, :, out]).astype(BF)
            return carry

        lax.fori_loop(0, 4, block, 0)
        cc_copy(k).start()

    def early_far(k):
        cc_copy(k).wait()

        def block(b, carry):
            both = co4[k % 2, b, at(c, TOK, TOK), :].astype(F32) + cr4[k, b].astype(F32)
            cr4[k, b] = both.astype(BF)
            return carry

        lax.fori_loop(0, 4, block, 0)
        for i in range(2):
            pp_copy(k, i).start()

    def early_near(k):
        pp_all(k).wait_recv()
        for i in range(2):
            block, added = (y + PLUS_MINUS[i]) % 4, slice(i * 64, i * 64 + 64)
            both = cr4[k, block, added, :].astype(F32) + relay4[k, i].astype(F32)
            cr4[k, block, added, :] = both.astype(BF)
            nn_copy(k, i).start()

    def early_join(k):
        nn_all(k).wait()
        both = cr4[k, y].astype(F32)
        for i in range(2):
            both = both + summed4[k, i].astype(F32)
        grad_ref[:, ecols(k)] = both.astype(BF)
        grad_out(ecols(k)).start()

    def turn_acts():
        def block(b, carry):
            part = at(b, Q, 256)
            for n, source in enumerate((2, 0, 1)):
                acts_t[n, :, part] = acts[source, part, :].astype(F32).T.astype(BF)
            return carry

        lax.fori_loop(0, 3, block, 0)

    def weight_grads(k):
        for a in range(2):
            stage_copy(a, k).wait()

        @pl.when(k + 1 < BC)
        def _():
            for a in range(2):
                stage_copy(a, k + 1).start()

        for out in tiles(BW):
            cot_rows = stage[1, k % 2, :, :, out].reshape(4 * ROWS, SUB)
            tok_rows = stage[0, k % 2, :, :, out].reshape(4 * ROWS, SUB)
            down = nn(acts_t[0], cot_rows)
            dw[:, tile(k, out)] = down
            gate = nn(acts_t[1], tok_rows)
            up = nn(acts_t[2], tok_rows)
            sq = down * down + gate * gate + up * up
            squares[...] += sq[:, 0:128] + sq[:, 128:256]

    def update(k):
        @pl.when(k == 0)
        def _():
            mean = jnp.sum(squares[...], axis=1, keepdims=True) / (3.0 * D)
            old = jnp.broadcast_to(moment_ref[...], (128, Q)).T
            second = moment_decay * old + (1.0 - moment_decay) * mean
            second_ref[...] = second.T[0:1, :]
            squares[...] = 1.0 / (jnp.sqrt(second) + epsilon)

        for j in range(BW // 128):
            out = pl.ds(pl.multiple_of(k * BW + j * 128, 128), 128)
            update_ref[:, out] = (dw[:, out] * squares[...]).astype(BF)
        update_out(cols(k)).start()

    def drain(copy):
        return lambda k: copy(k).wait_send()

    def step(t, carry):
        when(t - 2, B_LATE, drain(p_all))
        when(t - 3, B_LATE, drain(n_all))
        when(t - 4, B_LATE, drain(x_all))
        when(t - 5, B_LATE, drain(z_all))
        when(t - 2, B_EARLY, drain(xx_all))
        when(t - 3, B_EARLY, drain(zz_all))
        when(t - 5, B_EARLY, drain(pp_all))

        @pl.when(t == 1)
        def _():
            for copy in weights[4:]:
                copy.wait()

        when(t, B_LATE, late_far)
        when(t, B_EARLY, early_terms)
        when(t - 1, B_LATE, late_near)
        when(t - 1, B_EARLY, early_turn)
        when(t - 2, B_LATE, late_total)
        when(t - 2, B_EARLY, early_unselect)
        when(t - 3, B_LATE, late_turn)
        when(t - 3, B_EARLY, early_far)
        when(t - 4, B_LATE, late_unselect)
        when(t - 4, B_EARLY, early_near)
        when(t - 5, B_LATE, late_join)
        when(t - 5, B_EARLY, early_join)
        pl.when(t == 0)(turn_acts)
        for n in range(2):
            when(t * 2 + n, BC, weight_grads)
        for n in range(3):
            when((t - BC // 2) * 3 + n, BC, update)
        return carry

    lax.fori_loop(0, B_LATE + 5, step, 0)
    grad_out(pl.ds(0, D)).wait()
    update_out(pl.ds(0, D)).wait()


def shards(tokens, grad_out, routes, gate_prob, w_gate, w_up, w_down, moment_prev):
    vmem = pl.BlockSpec(memory_space=pltpu.VMEM)
    hbm = pl.BlockSpec(memory_space=pltpu.HBM)
    dma = pltpu.SemaphoreType.DMA

    def held(*shape):
        return pltpu.VMEM(shape, BF)

    rows, acts, sel = pl.pallas_call(
        forward_kernel,
        name="dispatch",
        out_shape=(
            jax.ShapeDtypeStruct((2, 4, ROWS, D), BF),
            jax.ShapeDtypeStruct((3, 4 * ROWS, Q), BF),
            jax.ShapeDtypeStruct((4, ROWS, 2 * TOK), BF),
        ),
        in_specs=[vmem, vmem, hbm, hbm, hbm, hbm, hbm],
        out_specs=(hbm, vmem, vmem),
        scratch_shapes=[
            pltpu.VMEM((4, 2, 8, TOK), F32),
            pltpu.VMEM((4, ROWS, 128), F32),
            held(ROWS, ROWS),
            held(F_LATE, 2 * TOK, FW),
            held(2, ROWS, FW),
            held(F_LATE, ROWS, FW),
            held(2, ROWS, FW),
            held(F_EARLY, 4, 2 * TOK, EW),
            held(2, 4, ROWS, EW),
            held(F_EARLY, 4, ROWS, EW),
            held(2, 4, ROWS, EW),
            held(2, 4, ROWS, FW),
            held(2, 4, ROWS, EW),
            pltpu.VMEM((3, 4 * ROWS, Q), F32),
            held(D, Q),
            held(D, Q),
            held(Q, D),
            dma((3,)),
            dma((7,)),
            dma((7,)),
            dma((F_LATE,)),
            dma((F_LATE,)),
            dma((F_LATE,)),
            dma((2,)),
            dma((F_LATE,)),
            dma((2,)),
            dma((F_LATE,)),
            dma((2,)),
            dma((F_LATE,)),
            dma((F_LATE,)),
            dma((F_LATE,)),
            dma((F_LATE,)),
            dma((2,)),
            dma((F_EARLY,)),
            dma((F_EARLY,)),
            dma((F_EARLY,)),
            dma((F_EARLY,)),
            dma((F_EARLY,)),
            dma((F_EARLY,)),
            dma((F_EARLY,)),
            dma((F_EARLY,)),
            dma((F_EARLY,)),
            dma((2,)),
            dma((F_EARLY,)),
            dma((2,)),
            dma((F_EARLY,)),
            dma((2,)),
            dma((2,)),
        ],
        compiler_params=pltpu.CompilerParams(
            collective_id=0, has_side_effects=True, vmem_limit_bytes=60 * 2**20
        ),
    )(
        routes.reshape(1, TOK),
        gate_prob.reshape(1, TOK),
        tokens,
        grad_out,
        w_gate[0],
        w_up[0],
        w_down[0],
    )
    grad_in, update, second = pl.pallas_call(
        backward_kernel,
        name="combine",
        out_shape=(
            jax.ShapeDtypeStruct((TOK, D), BF),
            jax.ShapeDtypeStruct((Q, D), BF),
            jax.ShapeDtypeStruct((1, Q), F32),
        ),
        in_specs=[vmem, vmem, hbm, hbm, hbm, vmem],
        out_specs=(hbm, hbm, vmem),
        scratch_shapes=[
            held(3, Q, 4 * ROWS),
            held(TOK, D),
            held(Q, D),
            held(ROWS, ROWS),
            held(2, ROWS, BW),
            held(B_LATE, 2, 96, BW),
            held(2, 2, ROWS, BW),
            held(B_LATE, 2, ROWS, BW),
            held(2, ROWS, BW),
            held(B_LATE, ROWS, BW),
            held(2, ROWS, BW),
            held(B_LATE, ROWS, BW),
            held(2, 2 * TOK, BW),
            held(B_LATE, TOK, BW),
            held(2, 4, ROWS, CW),
            held(B_EARLY, 4, ROWS, CW),
            held(2, 4, ROWS, CW),
            held(B_EARLY, 4, ROWS, CW),
            held(2, 4, 2 * TOK, CW),
            held(B_EARLY, 4, TOK, CW),
            held(B_EARLY, 2, 64, CW),
            held(B_EARLY, 2, TOK, CW),
            held(2, 2, 4, ROWS, BW),
            pltpu.VMEM((Q, D), F32),
            pltpu.VMEM((Q, 128), F32),
            held(D, Q),
            held(D, Q),
            dma((4, 2)),
            dma((2,)),
            dma((B_LATE,)),
            dma((2,)),
            dma((B_LATE,)),
            dma((2,)),
            dma((B_LATE,)),
            dma((2,)),
            dma((B_LATE,)),
            dma((2,)),
            dma((B_LATE,)),
            dma((2,)),
            dma((B_EARLY,)),
            dma((2,)),
            dma((B_EARLY,)),
            dma((2,)),
            dma((B_EARLY,)),
            dma((B_EARLY,)),
            dma((B_EARLY,)),
            dma((B_EARLY,)),
            dma((B_EARLY,)),
            dma((2, 2)),
            dma((2,)),
        ],
        compiler_params=pltpu.CompilerParams(
            collective_id=1, has_side_effects=True, vmem_limit_bytes=60 * 2**20
        ),
    )(acts, sel, rows, w_gate[0], w_up[0], moment_prev)
    return grad_in, update[None], second


def solution(mesh):
    placed = (
        P(("dp", "expert"), None),
        P(("dp", "expert"), None),
        P(("dp", "expert"), None),
        P(("dp", "expert"), None),
        P("expert", None, "dp"),
        P("expert", None, "dp"),
        P("expert", "dp", None),
        P("expert", "dp"),
    )
    return jax.shard_map(
        shards,
        mesh=mesh,
        in_specs=placed,
        out_specs=(P(("dp", "expert"), None), P("expert", "dp", None), P("expert", "dp")),
        check_vma=False,
    )
```

```python
import functools

import jax
import jax.numpy as jnp
from jax import lax
from jax.experimental import pallas as pl
from jax.experimental.pallas import tpu as pltpu
from jax.sharding import PartitionSpec as P

MESH = pl.DeviceIdType.MESH
BF = jnp.bfloat16
F32 = jnp.float32

moment_decay = 0.95
epsilon = 1e-08

D = 7168
TOK = 128
CAP = 6
Q = 256
ROWS = 192
BLK = 48
SUB = 256

FW = 512
FC = D // FW
EW = 384
F_EARLY = 16
F_DONE = F_EARLY * EW // FW
F_LATE = 2 * FC - F_DONE
BW = 512
BC = D // BW
CW = 384
B_EARLY = 8
B_LATE = (D - B_EARLY * CW) // BW
B_FROM = B_LATE * BW

ACROSS = ((0, 0, 0, 1),) + tuple((0, d, 0, 0) for d in (1, 2, 3)) + tuple((0, 0, d, 0) for d in (1, 2, 3))
COLUMN = ((1, 0, 0, 0), (3, 0, 0, 0), (2, 0, 0, 0), (1, 0, 0, 1), (3, 0, 0, 1), (2, 0, 0, 1))
PLUS_MINUS = (1, 3)


def place():
    y = lax.axis_index("dp")
    e = lax.axis_index("expert")
    return y, e // 8, (e // 2) % 4, e % 2


def peer(here, dy, dz, dx, dc):
    y, z, x, c = here
    expert = (((z + dz) % 4) * 4 + (x + dx) % 4) * 2 + (c + dc) % 2
    return {"dp": (y + dy) % 4, "expert": expert}


def remote(src, dst, send, recv, device):
    return pltpu.make_async_remote_copy(
        src_ref=src,
        dst_ref=dst,
        send_sem=send,
        recv_sem=recv,
        device_id=device,
        device_id_type=MESH,
    )


def greet(here, partners):
    barrier = pltpu.get_barrier_semaphore()
    for offset in partners:
        pl.semaphore_signal(barrier, inc=1, device_id=peer(here, *offset), device_id_type=MESH)
    return lambda: pl.semaphore_wait(barrier, len(partners))


def at(index, size, align):
    return pl.ds(pl.multiple_of(index * size, align), size)


def nt(a, b):
    return lax.dot_general(a, b, (((1,), (1,)), ((), ())), preferred_element_type=F32)


def tn(a, b):
    return lax.dot_general(a, b, (((0,), (0,)), ((), ())), preferred_element_type=F32)


def nn(a, b):
    return jnp.dot(a, b, preferred_element_type=F32)


def tiles(width):
    return [slice(j, min(j + SUB, width)) for j in range(0, width, SUB)]


def swap_matrix():
    out = lax.broadcasted_iota(jnp.int32, (ROWS, ROWS), 0)
    row = lax.broadcasted_iota(jnp.int32, (ROWS, ROWS), 1)

    def steps(value, size):
        return sum((value >= size * n).astype(jnp.int32) for n in (1, 2, 3))

    outer = steps(out, 48)
    inner = steps(out - 48 * outer, 12)
    return (row - out == 36 * (inner - outer)).astype(F32).astype(BF)


def when(k, count, body):
    pl.when((k >= 0) & (k < count))(lambda: body(k))


def forward_kernel(
    routes_ref,
    prob_ref,
    tok_ref,
    cot_ref,
    wg_hbm,
    wu_hbm,
    wd_hbm,
    rows,
    acts,
    sel,
    metas,
    gp,
    perm,
    raw,
    zs,
    za,
    xs,
    raw4,
    zs4,
    za4,
    xs4,
    stage,
    stage4,
    acc,
    wg,
    wu,
    wd,
    w_sem,
    m_s,
    m_r,
    raw_l,
    raw_s,
    raw_r,
    z_s,
    z_r,
    x_s,
    x_r,
    x_l,
    y_s,
    y_r,
    f_s,
    f_r,
    st_l,
    own_l,
    own_s,
    own_r,
    yy_s,
    yy_r,
    ff_s,
    ff_r,
    cc_s,
    cc_r,
    zz_s,
    zz_r,
    xx_s,
    xx_r,
    xx_l,
    st4_l,
):
    here = place()
    y, z, x, c = here
    mine = at(c, TOK, TOK)

    def cols(k):
        return at(k, FW, 128)

    def ecols(k):
        return at(k, EW, 128)

    met = greet(here, ACROSS + COLUMN)
    weights = [
        pltpu.make_async_copy(src, dst, w_sem.at[i])
        for i, (src, dst) in enumerate(((wg_hbm, wg), (wu_hbm, wu), (wd_hbm, wd)))
    ]

    first = lax.broadcasted_iota(jnp.int32, (8, TOK), 0) == 0
    metas[y, c] = jnp.where(first, routes_ref[...].astype(F32), prob_ref[...])
    others = COLUMN + ((0, 0, 0, 1),)

    def meta_copy(i):
        return remote(
            metas.at[y, c], metas.at[y, c], m_s.at[i], m_r.at[i], peer(here, *others[i])
        )

    def yy_copy(k, i):
        return remote(
            cot_ref.at[:, ecols(k)],
            raw4.at[k, y, mine, :],
            yy_s.at[k],
            yy_r.at[k],
            peer(here, PLUS_MINUS[i], 0, 0, 0),
        )

    def ff_copy(k, i):
        src = (y + PLUS_MINUS[1 - i]) % 4
        half = raw4.at[k, src, pl.ds(pl.multiple_of(c * TOK + i * 64, 64), 64), :]
        return remote(
            half, half, ff_s.at[k], ff_r.at[k], peer(here, PLUS_MINUS[i], 0, 0, 0)
        )

    def cc_copy(k, i):
        block = raw4.at[k, (y + (3, 1, 2)[i]) % 4, mine, :]
        return remote(block, block, cc_s.at[k], cc_r.at[k], peer(here, 0, 0, 0, 1))

    def own_local(k):
        return pltpu.make_async_copy(
            cot_ref.at[:, ecols(k)], raw4.at[k, y, mine, :], own_l.at[k]
        )

    def own_remote(k):
        return remote(
            cot_ref.at[:, ecols(k)],
            raw4.at[k, y, mine, :],
            own_s.at[k],
            own_r.at[k],
            peer(here, 0, 0, 0, 1),
        )

    def zz_copy(k, d):
        return remote(
            zs4.at[k % 2, :, at((z + d) % 4, BLK, 16), :],
            za4.at[k, :, at(z, BLK, 16), :],
            zz_s.at[k % 2],
            zz_r.at[k],
            peer(here, 0, d, 0, 0),
        )

    def xx_copy(k, d):
        return remote(
            xs4.at[k % 2, :, at((x + d) % 4, BLK, 16), :],
            rows.at[1, :, at(x, BLK, 16), ecols(k)],
            xx_s.at[k % 2],
            xx_r.at[k],
            peer(here, 0, 0, d, 0),
        )

    def xx_own(k):
        return pltpu.make_async_copy(
            xs4.at[k % 2, :, at(x, BLK, 16), :],
            rows.at[1, :, at(x, BLK, 16), ecols(k)],
            xx_l.at[k % 2],
        )

    def stage4_copy(k):
        return pltpu.make_async_copy(
            rows.at[1, :, :, ecols(k)], stage4.at[k % 2], st4_l.at[k % 2]
        )

    def yy_all(k):
        both = raw4.at[k, pl.ds(0, 2), mine, :]
        return remote(both, both, yy_s.at[k], yy_r.at[k], peer(here, 1, 0, 0, 0))

    def ff_all(k):
        both = raw4.at[k, 0, mine, :]
        return remote(both, both, ff_s.at[k], ff_r.at[k], peer(here, 1, 0, 0, 0))

    def cc_all(k):
        three = raw4.at[k, pl.ds(0, 3), mine, :]
        return remote(three, three, cc_s.at[k], cc_r.at[k], peer(here, 0, 0, 0, 1))

    def zz_all(k):
        return remote(
            zs4.at[k % 2, :, pl.ds(0, 3 * BLK), :],
            za4.at[k, :, pl.ds(0, 3 * BLK), :],
            zz_s.at[k % 2],
            zz_r.at[k],
            peer(here, 0, 1, 0, 0),
        )

    def xx_all(k):
        return remote(
            xs4.at[k % 2, :, pl.ds(0, 3 * BLK), :],
            rows.at[1, :, pl.ds(0, 3 * BLK), ecols(k)],
            xx_s.at[k % 2],
            xx_r.at[k],
            peer(here, 0, 0, 1, 0),
        )

    def early_send(k):
        for i in range(2):
            yy_copy(k, i).start()

    def early_own(k):
        own_local(k).start()
        own_remote(k).start()

    def early_pass(k):
        yy_all(k).wait_recv()
        for i in range(2):
            ff_copy(k, i).start()
            cc_copy(k, i).start()

    def early_rest(k):
        ff_all(k).wait_recv()
        cc_copy(k, 2).start()

    def early_select(k):
        own_local(k).wait()
        own_remote(k).wait()
        cc_all(k).wait_recv()

        def block(b, carry):
            for out in tiles(EW):
                picked = nn(sel[b], raw4[k, b, :, out]) * gp[b, :, 0:1]
                zs4[k % 2, b, :, out] = picked.astype(BF)
            za4[k, b, at(z, BLK, 16), :] = zs4[k % 2, b, at(z, BLK, 16), :]
            return carry

        lax.fori_loop(0, 4, block, 0)
        for d in (2, 1, 3):
            zz_copy(k, d).start()

    def early_turn(k):
        zz_all(k).wait_recv()

        def block(b, carry):
            for out in tiles(EW):
                xs4[k % 2, b, :, out] = nn(perm[...], za4[k, b, :, out]).astype(BF)
            return carry

        lax.fori_loop(0, 4, block, 0)
        for d in (2, 1, 3):
            xx_copy(k, d).start()
        xx_own(k).start()

    def early_fetch(k):
        xx_all(k).wait_recv()
        xx_own(k).wait()
        stage4_copy(k).start()

    def early_accumulate(k):
        stage4_copy(k).wait()
        acc[2] += nt(stage4[k % 2].reshape(4 * ROWS, EW), wd[:, ecols(k)])

    def which(i):
        a = i // FC
        return a, cols(i - a * (FC - F_DONE))

    def raw_start(i):
        def begin(src):
            dst = raw.at[i, mine, :]
            pltpu.make_async_copy(src, dst, raw_l.at[i]).start()
            remote(src, dst, raw_s.at[i], raw_r.at[i], peer(here, 0, 0, 0, 1)).start()

        pl.when(i // FC == 0)(lambda: begin(tok_ref.at[:, cols(i)]))
        pl.when(i // FC == 1)(lambda: begin(cot_ref.at[:, cols(i - FC + F_DONE)]))

    def raw_waits(i):
        src = tok_ref.at[:, cols(0)]
        dst = raw.at[i, mine, :]
        return (
            pltpu.make_async_copy(src, dst, raw_l.at[i]),
            remote(src, dst, raw_s.at[i], raw_r.at[i], peer(here, 0, 0, 0, 1)),
        )

    def z_copy(i, d):
        return remote(
            zs.at[i % 2, at((z + d) % 4, BLK, 16), :],
            za.at[i, at(z, BLK, 16), :],
            z_s.at[i % 2],
            z_r.at[i],
            peer(here, 0, d, 0, 0),
        )

    def x_copy(i, d):
        a, span = which(i)
        return remote(
            xs.at[i % 2, at((x + d) % 4, BLK, 16), :],
            rows.at[a, y, at(x, BLK, 16), span],
            x_s.at[i % 2],
            x_r.at[i],
            peer(here, 0, 0, d, 0),
        )

    def x_own(i):
        a, span = which(i)
        return pltpu.make_async_copy(
            xs.at[i % 2, at(x, BLK, 16), :], rows.at[a, y, at(x, BLK, 16), span], x_l.at[i % 2]
        )

    def y_copy(i, p):
        a, span = which(i)
        block = rows.at[a, y, :, span]
        return remote(
            block, block, y_s.at[i], y_r.at[i], peer(here, PLUS_MINUS[p], 0, 0, 0)
        )

    def f_copy(i, p):
        a, span = which(i)
        half = rows.at[a, (y + PLUS_MINUS[1 - p]) % 4, pl.ds(p * 96, 96), span]
        return remote(half, half, f_s.at[i], f_r.at[i], peer(here, PLUS_MINUS[p], 0, 0, 0))

    def stage_copy(i):
        a, span = which(i)
        return pltpu.make_async_copy(rows.at[a, :, :, span], stage.at[i % 2], st_l.at[i % 2])

    def z_all(i):
        return remote(
            zs.at[i % 2, pl.ds(0, 3 * BLK), :],
            za.at[i, pl.ds(0, 3 * BLK), :],
            z_s.at[i % 2],
            z_r.at[i],
            peer(here, 0, 1, 0, 0),
        )

    def x_all(i):
        a, span = which(i)
        return remote(
            xs.at[i % 2, pl.ds(0, 3 * BLK), :],
            rows.at[a, y, pl.ds(0, 3 * BLK), span],
            x_s.at[i % 2],
            x_r.at[i],
            peer(here, 0, 0, 1, 0),
        )

    def y_all(i):
        a, span = which(i)
        both = rows.at[a, pl.ds(0, 2), :, span]
        return remote(both, both, y_s.at[i], y_r.at[i], peer(here, 1, 0, 0, 0))

    def f_all(i):
        a, span = which(i)
        both = rows.at[a, y, :, span]
        return remote(both, both, f_s.at[i], f_r.at[i], peer(here, 1, 0, 0, 0))

    def late_select(i):
        for copy in raw_waits(i):
            copy.wait()
        scale = jnp.where(i // FC == 1, gp[y], 1.0)[:, 0:1]
        for out in tiles(FW):
            zs[i % 2, :, out] = (nn(sel[y], raw[i, :, out]) * scale).astype(BF)
        for d in (2, 1, 3):
            z_copy(i, d).start()
        za[i, at(z, BLK, 16), :] = zs[i % 2, at(z, BLK, 16), :]

    def late_turn(i):
        z_all(i).wait_recv()
        for out in tiles(FW):
            xs[i % 2, :, out] = nn(perm[...], za[i, :, out]).astype(BF)
        for d in (2, 1, 3):
            x_copy(i, d).start()
        x_own(i).start()

    def late_spread(i):
        x_all(i).wait_recv()
        x_own(i).wait()
        for p in range(2):
            y_copy(i, p).start()

    def late_pass(i):
        y_all(i).wait_recv()
        for p in range(2):
            f_copy(i, p).start()

    def late_fetch(i):
        f_all(i).wait_recv()
        stage_copy(i).start()

    def late_accumulate(i):
        stage_copy(i).wait()
        a, span = which(i)

        @pl.when(a == 0)
        def _():
            held = stage[i % 2].reshape(4 * ROWS, FW)
            acc[0] += nn(held, wg[span, :])
            acc[1] += nn(held, wu[span, :])

        @pl.when(a == 1)
        def _():
            acc[2] += nt(stage[i % 2].reshape(4 * ROWS, FW), wd[:, span])

    def drain(copy):
        return lambda k: copy(k).wait_send()

    perm[...] = swap_matrix()
    acc[...] = jnp.zeros_like(acc)
    met()
    for i in range(len(others)):
        meta_copy(i).start()
    early_send(0)
    early_send(1)
    for i in range(2):
        raw_start(i)
    early_own(0)
    early_own(1)
    for copy in weights:
        copy.start()
    for i in range(len(others)):
        meta_copy(i).wait()

    def plan(b, carry):
        earlier = (
            (
                lax.broadcasted_iota(jnp.int32, (TOK, TOK), 0)
                < lax.broadcasted_iota(jnp.int32, (TOK, TOK), 1)
            )
            .astype(F32)
            .astype(BF)
        )
        weight = jnp.zeros((ROWS, 1), F32)
        for m in range(2):
            route = metas[b, m, 0:1, :].astype(jnp.int32)
            prob = metas[b, m, 1:2, :]
            onehot = (lax.broadcasted_iota(jnp.int32, (32, TOK), 0) == route).astype(F32)
            before = nn(onehot.astype(BF), earlier)
            slot = jnp.sum(onehot * before, axis=0, keepdims=True).astype(jnp.int32)
            row = ((route >> 1) * 2 + m) * CAP + slot
            row = jnp.where((route & 1) == c, row, -1)
            chosen = lax.broadcasted_iota(jnp.int32, (ROWS, TOK), 0) == row
            sel[b, :, m * TOK : (m + 1) * TOK] = chosen.astype(F32).astype(BF)
            weight = weight + jnp.sum(jnp.where(chosen, prob, 0.0), axis=1, keepdims=True)
        gp[b] = jnp.broadcast_to(weight, (ROWS, 128))
        return carry

    lax.fori_loop(0, 4, plan, 0)

    def step(t, carry):
        when(t - 2, F_LATE, drain(z_all))
        when(t - 3, F_LATE, drain(x_all))
        when(t - 4, F_LATE, drain(y_all))
        when(t, F_EARLY, drain(yy_all))
        when(t - 1, F_EARLY, drain(ff_all))
        when(t - 2, F_EARLY, drain(cc_all))
        when(t - 3, F_EARLY, drain(zz_all))
        when(t - 4, F_EARLY, drain(xx_all))

        when(t, F_LATE, late_select)
        when(t + 2, F_EARLY, early_send)
        when(t + 2, F_EARLY, early_own)
        when(t + 2, F_LATE, raw_start)
        when(t + 1, F_EARLY, early_pass)
        when(t - 1, F_LATE, late_turn)
        when(t, F_EARLY, early_rest)
        when(t - 2, F_LATE, late_spread)
        when(t - 1, F_EARLY, early_select)
        when(t - 3, F_LATE, late_pass)
        when(t - 2, F_EARLY, early_turn)
        when(t - 4, F_LATE, late_fetch)
        when(t - 4, F_LATE, drain(f_all))
        when(t - 3, F_EARLY, early_fetch)

        @pl.when(t == 4)
        def _():
            for copy in weights:
                copy.wait()

        when(t - 4, F_EARLY, early_accumulate)
        when(t - 4, F_LATE, late_accumulate)
        return carry

    early_pass(0)
    lax.fori_loop(0, F_LATE + 4, step, 0)

    def finish(b, carry):
        part = at(b, Q, 256)
        gate, up, grad = acc[0, part, :], acc[1, part, :], acc[2, part, :]
        sig = jax.nn.sigmoid(gate)
        silu = gate * sig
        hidden = silu * up
        gate_grad = grad * up * sig * (1.0 + gate * (1.0 - sig))
        up_grad = grad * silu
        acts[0, part, :] = gate_grad.astype(BF)
        acts[1, part, :] = up_grad.astype(BF)
        acts[2, part, :] = hidden.astype(BF)
        return carry

    lax.fori_loop(0, 3, finish, 0)


def backward_kernel(
    acts,
    sel,
    rows,
    wg_hbm,
    wu_hbm,
    moment_ref,
    grad_hbm,
    update_hbm,
    second_ref,
    acts_t,
    grad_ref,
    update_ref,
    perm,
    far,
    relay,
    near,
    summed,
    xs,
    xa,
    zs,
    za,
    co,
    cr,
    xs4,
    xa4,
    zs4,
    za4,
    co4,
    cr4,
    relay4,
    summed4,
    stage,
    dw,
    squares,
    wg,
    wu,
    w_sem,
    p_s,
    p_r,
    n_s,
    n_r,
    x_s,
    x_r,
    z_s,
    z_r,
    c_s,
    c_r,
    xx_s,
    xx_r,
    zz_s,
    zz_r,
    cc_s,
    cc_r,
    pp_s,
    pp_r,
    nn_s,
    nn_r,
    st_l,
    out_l,
):
    here = place()
    y, z, x, c = here

    def cols(k):
        return at(k, BW, 128)

    def grad_out(span):
        return pltpu.make_async_copy(grad_ref.at[:, span], grad_hbm.at[:, span], out_l.at[0])

    def update_out(span):
        return pltpu.make_async_copy(update_ref.at[:, span], update_hbm.at[:, span], out_l.at[1])

    def ecols(k):
        return pl.ds(pl.multiple_of(B_FROM + k * CW, 128), CW)

    def tile(k, out):
        return pl.ds(pl.multiple_of(k * BW + out.start, 128), out.stop - out.start)

    def etile(k, out):
        return pl.ds(pl.multiple_of(B_FROM + k * CW + out.start, 128), out.stop - out.start)

    met = greet(here, ACROSS + COLUMN[:2])
    spans = ((0, BW), (B_FROM, CW), (BW, B_FROM - BW), (B_FROM + CW, D - B_FROM - CW))
    weights = [
        pltpu.make_async_copy(
            src.at[pl.ds(first, size)], dst.at[pl.ds(first, size)], w_sem.at[n, i]
        )
        for n, (first, size) in enumerate(spans)
        for i, (src, dst) in enumerate(((wg_hbm, wg), (wu_hbm, wu)))
    ]
    for copy in weights:
        copy.start()

    def stage_copy(a, k):
        return pltpu.make_async_copy(
            rows.at[a, :, :, cols(k)], stage.at[a, k % 2], st_l.at[a, k % 2]
        )

    for a in range(2):
        stage_copy(a, 0).start()
    squares[...] = jnp.zeros_like(squares)
    perm[...] = swap_matrix()
    met()
    for copy in weights[:4]:
        copy.wait()

    def partial(block, span):
        block_rows = at(block, ROWS, 16)
        total = nt(acts[0, block_rows, :], wg[span, :])
        total = total + nt(acts[1, block_rows, :], wu[span, :])
        return total.astype(BF)

    def p_copy(k, i):
        return remote(
            far.at[k % 2, pl.ds(i * 96, 96), :],
            relay.at[k, i],
            p_s.at[k % 2],
            p_r.at[k],
            peer(here, PLUS_MINUS[i], 0, 0, 0),
        )

    def n_copy(k, i):
        return remote(
            near.at[i, k % 2],
            summed.at[k, i],
            n_s.at[k % 2],
            n_r.at[k],
            peer(here, PLUS_MINUS[i], 0, 0, 0),
        )

    def x_copy(k, d):
        return remote(
            xs.at[k % 2, at((x + d) % 4, BLK, 16), :],
            xa.at[k, at(x, BLK, 16), :],
            x_s.at[k % 2],
            x_r.at[k],
            peer(here, 0, 0, d, 0),
        )

    def z_copy(k, d):
        return remote(
            zs.at[k % 2, at((z + d) % 4, BLK, 16), :],
            za.at[k, at(z, BLK, 16), :],
            z_s.at[k % 2],
            z_r.at[k],
            peer(here, 0, d, 0, 0),
        )

    def c_copy(k):
        return remote(
            co.at[k % 2, at(1 - c, TOK, TOK), :],
            cr.at[k],
            c_s.at[k % 2],
            c_r.at[k],
            peer(here, 0, 0, 0, 1),
        )

    def whole(src, dst, send, recv):
        return remote(src, dst, send, recv, peer(here, 1, 0, 0, 0))

    def p_all(k):
        return whole(far.at[k % 2], relay.at[k], p_s.at[k % 2], p_r.at[k])

    def n_all(k):
        return whole(near.at[:, k % 2], summed.at[k], n_s.at[k % 2], n_r.at[k])

    def x_all(k):
        three = pl.ds(0, 3 * BLK)
        return whole(xs.at[k % 2, three, :], xa.at[k, three, :], x_s.at[k % 2], x_r.at[k])

    def z_all(k):
        three = pl.ds(0, 3 * BLK)
        return whole(zs.at[k % 2, three, :], za.at[k, three, :], z_s.at[k % 2], z_r.at[k])

    def xx_all(k):
        three = pl.ds(0, 3 * BLK)
        return whole(
            xs4.at[k % 2, :, three, :], xa4.at[k, :, three, :], xx_s.at[k % 2], xx_r.at[k]
        )

    def zz_all(k):
        three = pl.ds(0, 3 * BLK)
        return whole(
            zs4.at[k % 2, :, three, :], za4.at[k, :, three, :], zz_s.at[k % 2], zz_r.at[k]
        )

    def pp_all(k):
        return whole(cr4.at[k, 0], relay4.at[k], pp_s.at[k], pp_r.at[k])

    def nn_all(k):
        return whole(cr4.at[k, pl.ds(0, 2)], summed4.at[k], nn_s.at[k], nn_r.at[k])

    def late_far(k):
        for out in tiles(BW):
            far[k % 2, :, out] = partial((y + 2) % 4, tile(k, out))
        for i in range(2):
            p_copy(k, i).start()

    def late_near(k):
        p_all(k).wait_recv()
        for i in range(2):
            added, plain = slice(i * 96, i * 96 + 96), slice(96 - i * 96, 192 - i * 96)
            for out in tiles(BW):
                term = partial((y + PLUS_MINUS[i]) % 4, tile(k, out))
                both = term[added].astype(F32) + relay[k, i, :, out].astype(F32)
                near[i, k % 2, added, out] = both.astype(BF)
                near[i, k % 2, plain, out] = term[plain]
            n_copy(k, i).start()

    def late_total(k):
        n_all(k).wait_recv()
        for out in tiles(BW):
            whole = partial(y, tile(k, out)).astype(F32)
            whole = whole + summed[k, 0, :, out].astype(F32)
            whole = whole + summed[k, 1, :, out].astype(F32)
            xs[k % 2, :, out] = whole.astype(BF)
        for d in (2, 1, 3):
            x_copy(k, d).start()
        xa[k, at(x, BLK, 16), :] = xs[k % 2, at(x, BLK, 16), :]

    def late_turn(k):
        x_all(k).wait_recv()
        for out in tiles(BW):
            zs[k % 2, :, out] = nn(perm[...], xa[k, :, out]).astype(BF)
        for d in (2, 1, 3):
            z_copy(k, d).start()
        za[k, at(z, BLK, 16), :] = zs[k % 2, at(z, BLK, 16), :]

    def late_unselect(k):
        z_all(k).wait_recv()
        for out in tiles(BW):
            block = za[k, :, out]
            co[k % 2, :, out] = tn(sel[y], block).astype(BF)
        c_copy(k).start()

    def late_join(k):
        c_copy(k).wait()
        both = co[k % 2, at(c, TOK, TOK), :].astype(F32) + cr[k].astype(F32)
        grad_ref[:, cols(k)] = both.astype(BF)
        grad_out(cols(k)).start()

    def xx_copy(k, d):
        return remote(
            xs4.at[k % 2, :, at((x + d) % 4, BLK, 16), :],
            xa4.at[k, :, at(x, BLK, 16), :],
            xx_s.at[k % 2],
            xx_r.at[k],
            peer(here, 0, 0, d, 0),
        )

    def zz_copy(k, d):
        return remote(
            zs4.at[k % 2, :, at((z + d) % 4, BLK, 16), :],
            za4.at[k, :, at(z, BLK, 16), :],
            zz_s.at[k % 2],
            zz_r.at[k],
            peer(here, 0, d, 0, 0),
        )

    def cc_copy(k):
        return remote(
            co4.at[k % 2, :, at(1 - c, TOK, TOK), :],
            cr4.at[k],
            cc_s.at[k % 2],
            cc_r.at[k],
            peer(here, 0, 0, 0, 1),
        )

    def pp_copy(k, i):
        return remote(
            cr4.at[k, (y + 2) % 4, pl.ds(i * 64, 64), :],
            relay4.at[k, i],
            pp_s.at[k],
            pp_r.at[k],
            peer(here, PLUS_MINUS[i], 0, 0, 0),
        )

    def nn_copy(k, i):
        return remote(
            cr4.at[k, (y + PLUS_MINUS[i]) % 4],
            summed4.at[k, i],
            nn_s.at[k],
            nn_r.at[k],
            peer(here, PLUS_MINUS[i], 0, 0, 0),
        )

    def early_terms(k):
        for out in tiles(CW):
            span = etile(k, out)
            term = nt(acts[0], wg[span, :]) + nt(acts[1], wu[span, :])
            xs4[k % 2, :, :, out] = term.astype(BF).reshape(4, ROWS, out.stop - out.start)
        xa4[k, :, at(x, BLK, 16), :] = xs4[k % 2, :, at(x, BLK, 16), :]
        for d in (2, 1, 3):
            xx_copy(k, d).start()

    def early_turn(k):
        xx_all(k).wait_recv()

        def block(b, carry):
            for out in tiles(CW):
                zs4[k % 2, b, :, out] = nn(perm[...], xa4[k, b, :, out]).astype(BF)
            za4[k, b, at(z, BLK, 16), :] = zs4[k % 2, b, at(z, BLK, 16), :]
            return carry

        lax.fori_loop(0, 4, block, 0)
        for d in (2, 1, 3):
            zz_copy(k, d).start()

    def early_unselect(k):
        zz_all(k).wait_recv()

        def block(b, carry):
            for out in tiles(CW):
                co4[k % 2, b, :, out] = tn(sel[b], za4[k, b, :, out]).astype(BF)
            return carry

        lax.fori_loop(0, 4, block, 0)
        cc_copy(k).start()

    def early_far(k):
        cc_copy(k).wait()

        def block(b, carry):
            both = co4[k % 2, b, at(c, TOK, TOK), :].astype(F32) + cr4[k, b].astype(F32)
            cr4[k, b] = both.astype(BF)
            return carry

        lax.fori_loop(0, 4, block, 0)
        for i in range(2):
            pp_copy(k, i).start()

    def early_near(k):
        pp_all(k).wait_recv()
        for i in range(2):
            block, added = (y + PLUS_MINUS[i]) % 4, slice(i * 64, i * 64 + 64)
            both = cr4[k, block, added, :].astype(F32) + relay4[k, i].astype(F32)
            cr4[k, block, added, :] = both.astype(BF)
            nn_copy(k, i).start()

    def early_join(k):
        nn_all(k).wait()
        both = cr4[k, y].astype(F32)
        for i in range(2):
            both = both + summed4[k, i].astype(F32)
        grad_ref[:, ecols(k)] = both.astype(BF)
        grad_out(ecols(k)).start()

    def turn_acts():
        def block(b, carry):
            part = at(b, Q, 256)
            for n, source in enumerate((2, 0, 1)):
                acts_t[n, :, part] = acts[source, part, :].astype(F32).T.astype(BF)
            return carry

        lax.fori_loop(0, 3, block, 0)

    def weight_grads(k):
        for a in range(2):
            stage_copy(a, k).wait()

        @pl.when(k + 1 < BC)
        def _():
            for a in range(2):
                stage_copy(a, k + 1).start()

        for out in tiles(BW):
            cot_rows = stage[1, k % 2, :, :, out].reshape(4 * ROWS, SUB)
            tok_rows = stage[0, k % 2, :, :, out].reshape(4 * ROWS, SUB)
            down = nn(acts_t[0], cot_rows)
            dw[:, tile(k, out)] = down
            gate = nn(acts_t[1], tok_rows)
            up = nn(acts_t[2], tok_rows)
            sq = down * down + gate * gate + up * up
            squares[...] += sq[:, 0:128] + sq[:, 128:256]

    def update(k):
        @pl.when(k == 0)
        def _():
            mean = jnp.sum(squares[...], axis=1, keepdims=True) / (3.0 * D)
            old = jnp.broadcast_to(moment_ref[...], (128, Q)).T
            second = moment_decay * old + (1.0 - moment_decay) * mean
            second_ref[...] = second.T[0:1, :]
            squares[...] = 1.0 / (jnp.sqrt(second) + epsilon)

        for j in range(BW // 128):
            out = pl.ds(pl.multiple_of(k * BW + j * 128, 128), 128)
            update_ref[:, out] = (dw[:, out] * squares[...]).astype(BF)
        update_out(cols(k)).start()

    def drain(copy):
        return lambda k: copy(k).wait_send()

    def step(t, carry):
        when(t - 2, B_LATE, drain(p_all))
        when(t - 3, B_LATE, drain(n_all))
        when(t - 4, B_LATE, drain(x_all))
        when(t - 5, B_LATE, drain(z_all))
        when(t - 2, B_EARLY, drain(xx_all))
        when(t - 3, B_EARLY, drain(zz_all))
        when(t - 5, B_EARLY, drain(pp_all))

        @pl.when(t == 1)
        def _():
            for copy in weights[4:]:
                copy.wait()

        when(t, B_LATE, late_far)
        when(t - 1, B_LATE, late_near)
        when(t, B_EARLY, early_terms)
        pl.when(t == 0)(turn_acts)
        when(t * 2, BC, weight_grads)
        when(t - 1, B_EARLY, early_turn)
        when(t - 2, B_LATE, late_total)
        when(t - 2, B_EARLY, early_unselect)
        when(t - 3, B_LATE, late_turn)
        when(t * 2 + 1, BC, weight_grads)
        when(t - 3, B_EARLY, early_far)
        when(t - 4, B_LATE, late_unselect)
        when(t - 4, B_EARLY, early_near)
        when(t - 5, B_LATE, late_join)
        when(t - 5, B_EARLY, early_join)
        for n in range(3):
            when((t - BC // 2) * 3 + n, BC, update)
        return carry

    lax.fori_loop(0, B_LATE + 5, step, 0)
    grad_out(pl.ds(0, D)).wait()
    update_out(pl.ds(0, D)).wait()


def shards(tokens, grad_out, routes, gate_prob, w_gate, w_up, w_down, moment_prev):
    vmem = pl.BlockSpec(memory_space=pltpu.VMEM)
    hbm = pl.BlockSpec(memory_space=pltpu.HBM)
    dma = pltpu.SemaphoreType.DMA

    def held(*shape):
        return pltpu.VMEM(shape, BF)

    rows, acts, sel = pl.pallas_call(
        forward_kernel,
        name="dispatch",
        out_shape=(
            jax.ShapeDtypeStruct((2, 4, ROWS, D), BF),
            jax.ShapeDtypeStruct((3, 4 * ROWS, Q), BF),
            jax.ShapeDtypeStruct((4, ROWS, 2 * TOK), BF),
        ),
        in_specs=[vmem, vmem, hbm, hbm, hbm, hbm, hbm],
        out_specs=(hbm, vmem, vmem),
        scratch_shapes=[
            pltpu.VMEM((4, 2, 8, TOK), F32),
            pltpu.VMEM((4, ROWS, 128), F32),
            held(ROWS, ROWS),
            held(F_LATE, 2 * TOK, FW),
            held(2, ROWS, FW),
            held(F_LATE, ROWS, FW),
            held(2, ROWS, FW),
            held(F_EARLY, 4, 2 * TOK, EW),
            held(2, 4, ROWS, EW),
            held(F_EARLY, 4, ROWS, EW),
            held(2, 4, ROWS, EW),
            held(2, 4, ROWS, FW),
            held(2, 4, ROWS, EW),
            pltpu.VMEM((3, 4 * ROWS, Q), F32),
            held(D, Q),
            held(D, Q),
            held(Q, D),
            dma((3,)),
            dma((7,)),
            dma((7,)),
            dma((F_LATE,)),
            dma((F_LATE,)),
            dma((F_LATE,)),
            dma((2,)),
            dma((F_LATE,)),
            dma((2,)),
            dma((F_LATE,)),
            dma((2,)),
            dma((F_LATE,)),
            dma((F_LATE,)),
            dma((F_LATE,)),
            dma((F_LATE,)),
            dma((2,)),
            dma((F_EARLY,)),
            dma((F_EARLY,)),
            dma((F_EARLY,)),
            dma((F_EARLY,)),
            dma((F_EARLY,)),
            dma((F_EARLY,)),
            dma((F_EARLY,)),
            dma((F_EARLY,)),
            dma((F_EARLY,)),
            dma((2,)),
            dma((F_EARLY,)),
            dma((2,)),
            dma((F_EARLY,)),
            dma((2,)),
            dma((2,)),
        ],
        compiler_params=pltpu.CompilerParams(
            collective_id=0, has_side_effects=True, vmem_limit_bytes=60 * 2**20
        ),
    )(
        routes.reshape(1, TOK),
        gate_prob.reshape(1, TOK),
        tokens,
        grad_out,
        w_gate[0],
        w_up[0],
        w_down[0],
    )
    grad_in, update, second = pl.pallas_call(
        backward_kernel,
        name="combine",
        out_shape=(
            jax.ShapeDtypeStruct((TOK, D), BF),
            jax.ShapeDtypeStruct((Q, D), BF),
            jax.ShapeDtypeStruct((1, Q), F32),
        ),
        in_specs=[vmem, vmem, hbm, hbm, hbm, vmem],
        out_specs=(hbm, hbm, vmem),
        scratch_shapes=[
            held(3, Q, 4 * ROWS),
            held(TOK, D),
            held(Q, D),
            held(ROWS, ROWS),
            held(2, ROWS, BW),
            held(B_LATE, 2, 96, BW),
            held(2, 2, ROWS, BW),
            held(B_LATE, 2, ROWS, BW),
            held(2, ROWS, BW),
            held(B_LATE, ROWS, BW),
            held(2, ROWS, BW),
            held(B_LATE, ROWS, BW),
            held(2, 2 * TOK, BW),
            held(B_LATE, TOK, BW),
            held(2, 4, ROWS, CW),
            held(B_EARLY, 4, ROWS, CW),
            held(2, 4, ROWS, CW),
            held(B_EARLY, 4, ROWS, CW),
            held(2, 4, 2 * TOK, CW),
            held(B_EARLY, 4, TOK, CW),
            held(B_EARLY, 2, 64, CW),
            held(B_EARLY, 2, TOK, CW),
            held(2, 2, 4, ROWS, BW),
            pltpu.VMEM((Q, D), F32),
            pltpu.VMEM((Q, 128), F32),
            held(D, Q),
            held(D, Q),
            dma((4, 2)),
            dma((2,)),
            dma((B_LATE,)),
            dma((2,)),
            dma((B_LATE,)),
            dma((2,)),
            dma((B_LATE,)),
            dma((2,)),
            dma((B_LATE,)),
            dma((2,)),
            dma((B_LATE,)),
            dma((2,)),
            dma((B_EARLY,)),
            dma((2,)),
            dma((B_EARLY,)),
            dma((2,)),
            dma((B_EARLY,)),
            dma((B_EARLY,)),
            dma((B_EARLY,)),
            dma((B_EARLY,)),
            dma((B_EARLY,)),
            dma((2, 2)),
            dma((2,)),
        ],
        compiler_params=pltpu.CompilerParams(
            collective_id=1, has_side_effects=True, vmem_limit_bytes=60 * 2**20
        ),
    )(acts, sel, rows, w_gate[0], w_up[0], moment_prev)
    return grad_in, update[None], second


def solution(mesh):
    placed = (
        P(("dp", "expert"), None),
        P(("dp", "expert"), None),
        P(("dp", "expert"), None),
        P(("dp", "expert"), None),
        P("expert", None, "dp"),
        P("expert", None, "dp"),
        P("expert", "dp", None),
        P("expert", "dp"),
    )
    return jax.shard_map(
        shards,
        mesh=mesh,
        in_specs=placed,
        out_specs=(P(("dp", "expert"), None), P("expert", "dp", None), P("expert", "dp")),
        check_vma=False,
    )
```

```python
import functools

import jax
import jax.numpy as jnp
from jax import lax
from jax.experimental import pallas as pl
from jax.experimental.pallas import tpu as pltpu
from jax.sharding import PartitionSpec as P

MESH = pl.DeviceIdType.MESH
BF = jnp.bfloat16
F32 = jnp.float32

moment_decay = 0.95
epsilon = 1e-08

D = 7168
TOK = 128
CAP = 6
Q = 256
ROWS = 192
BLK = 48
SUB = 256

FW = 512
FC = D // FW
EW = 384
F_EARLY = 16
F_DONE = F_EARLY * EW // FW
F_LATE = 2 * FC - F_DONE
BW = 512
BC = D // BW
CW = 384
B_EARLY = 8
B_LATE = (D - B_EARLY * CW) // BW
B_FROM = B_LATE * BW

ACROSS = ((0, 0, 0, 1),) + tuple((0, d, 0, 0) for d in (1, 2, 3)) + tuple((0, 0, d, 0) for d in (1, 2, 3))
COLUMN = ((1, 0, 0, 0), (3, 0, 0, 0), (2, 0, 0, 0), (1, 0, 0, 1), (3, 0, 0, 1), (2, 0, 0, 1))
PLUS_MINUS = (1, 3)


def place():
    y = lax.axis_index("dp")
    e = lax.axis_index("expert")
    return y, e // 8, (e // 2) % 4, e % 2


def peer(here, dy, dz, dx, dc):
    y, z, x, c = here
    expert = (((z + dz) % 4) * 4 + (x + dx) % 4) * 2 + (c + dc) % 2
    return {"dp": (y + dy) % 4, "expert": expert}


def remote(src, dst, send, recv, device):
    return pltpu.make_async_remote_copy(
        src_ref=src,
        dst_ref=dst,
        send_sem=send,
        recv_sem=recv,
        device_id=device,
        device_id_type=MESH,
    )


def greet(here, partners):
    barrier = pltpu.get_barrier_semaphore()
    for offset in partners:
        pl.semaphore_signal(barrier, inc=1, device_id=peer(here, *offset), device_id_type=MESH)
    return lambda: pl.semaphore_wait(barrier, len(partners))


def at(index, size, align):
    return pl.ds(pl.multiple_of(index * size, align), size)


def nt(a, b):
    return lax.dot_general(a, b, (((1,), (1,)), ((), ())), preferred_element_type=F32)


def tn(a, b):
    return lax.dot_general(a, b, (((0,), (0,)), ((), ())), preferred_element_type=F32)


def nn(a, b):
    return jnp.dot(a, b, preferred_element_type=F32)


def tiles(width):
    return [slice(j, min(j + SUB, width)) for j in range(0, width, SUB)]


def swap_matrix():
    out = lax.broadcasted_iota(jnp.int32, (ROWS, ROWS), 0)
    row = lax.broadcasted_iota(jnp.int32, (ROWS, ROWS), 1)

    def steps(value, size):
        return sum((value >= size * n).astype(jnp.int32) for n in (1, 2, 3))

    outer = steps(out, 48)
    inner = steps(out - 48 * outer, 12)
    return (row - out == 36 * (inner - outer)).astype(F32).astype(BF)


def when(k, count, body):
    pl.when((k >= 0) & (k < count))(lambda: body(k))


def forward_kernel(
    routes_ref,
    prob_ref,
    tok_ref,
    cot_ref,
    wg_hbm,
    wu_hbm,
    wd_hbm,
    rows,
    acts,
    sel,
    metas,
    gp,
    perm,
    raw,
    zs,
    za,
    xs,
    raw4,
    zs4,
    za4,
    xs4,
    stage,
    stage4,
    acc,
    wg,
    wu,
    wd,
    w_sem,
    m_s,
    m_r,
    raw_l,
    raw_s,
    raw_r,
    z_s,
    z_r,
    x_s,
    x_r,
    x_l,
    y_s,
    y_r,
    f_s,
    f_r,
    st_l,
    own_l,
    own_s,
    own_r,
    yy_s,
    yy_r,
    ff_s,
    ff_r,
    cc_s,
    cc_r,
    zz_s,
    zz_r,
    xx_s,
    xx_r,
    xx_l,
    st4_l,
):
    here = place()
    y, z, x, c = here
    mine = at(c, TOK, TOK)

    def cols(k):
        return at(k, FW, 128)

    def ecols(k):
        return at(k, EW, 128)

    met = greet(here, ACROSS + COLUMN)
    weights = [
        pltpu.make_async_copy(src, dst, w_sem.at[i])
        for i, (src, dst) in enumerate(((wg_hbm, wg), (wu_hbm, wu), (wd_hbm, wd)))
    ]

    first = lax.broadcasted_iota(jnp.int32, (8, TOK), 0) == 0
    metas[y, c] = jnp.where(first, routes_ref[...].astype(F32), prob_ref[...])
    others = COLUMN + ((0, 0, 0, 1),)

    def meta_copy(i):
        return remote(
            metas.at[y, c], metas.at[y, c], m_s.at[i], m_r.at[i], peer(here, *others[i])
        )

    def yy_copy(k, i):
        return remote(
            cot_ref.at[:, ecols(k)],
            raw4.at[k, y, mine, :],
            yy_s.at[k],
            yy_r.at[k],
            peer(here, PLUS_MINUS[i], 0, 0, 0),
        )

    def ff_copy(k, i):
        src = (y + PLUS_MINUS[1 - i]) % 4
        half = raw4.at[k, src, pl.ds(pl.multiple_of(c * TOK + i * 64, 64), 64), :]
        return remote(
            half, half, ff_s.at[k], ff_r.at[k], peer(here, PLUS_MINUS[i], 0, 0, 0)
        )

    def cc_copy(k, i):
        block = raw4.at[k, (y + (3, 1, 2)[i]) % 4, mine, :]
        return remote(block, block, cc_s.at[k], cc_r.at[k], peer(here, 0, 0, 0, 1))

    def own_local(k):
        return pltpu.make_async_copy(
            cot_ref.at[:, ecols(k)], raw4.at[k, y, mine, :], own_l.at[k]
        )

    def own_remote(k):
        return remote(
            cot_ref.at[:, ecols(k)],
            raw4.at[k, y, mine, :],
            own_s.at[k],
            own_r.at[k],
            peer(here, 0, 0, 0, 1),
        )

    def zz_copy(k, d):
        return remote(
            zs4.at[k % 2, :, at((z + d) % 4, BLK, 16), :],
            za4.at[k, :, at(z, BLK, 16), :],
            zz_s.at[k % 2],
            zz_r.at[k],
            peer(here, 0, d, 0, 0),
        )

    def xx_copy(k, d):
        return remote(
            xs4.at[k % 2, :, at((x + d) % 4, BLK, 16), :],
            rows.at[1, :, at(x, BLK, 16), ecols(k)],
            xx_s.at[k % 2],
            xx_r.at[k],
            peer(here, 0, 0, d, 0),
        )

    def xx_own(k):
        return pltpu.make_async_copy(
            xs4.at[k % 2, :, at(x, BLK, 16), :],
            rows.at[1, :, at(x, BLK, 16), ecols(k)],
            xx_l.at[k % 2],
        )

    def stage4_copy(k):
        return pltpu.make_async_copy(
            rows.at[1, :, :, ecols(k)], stage4.at[k % 2], st4_l.at[k % 2]
        )

    def yy_all(k):
        both = raw4.at[k, pl.ds(0, 2), mine, :]
        return remote(both, both, yy_s.at[k], yy_r.at[k], peer(here, 1, 0, 0, 0))

    def ff_all(k):
        both = raw4.at[k, 0, mine, :]
        return remote(both, both, ff_s.at[k], ff_r.at[k], peer(here, 1, 0, 0, 0))

    def cc_all(k):
        three = raw4.at[k, pl.ds(0, 3), mine, :]
        return remote(three, three, cc_s.at[k], cc_r.at[k], peer(here, 0, 0, 0, 1))

    def zz_all(k):
        return remote(
            zs4.at[k % 2, :, pl.ds(0, 3 * BLK), :],
            za4.at[k, :, pl.ds(0, 3 * BLK), :],
            zz_s.at[k % 2],
            zz_r.at[k],
            peer(here, 0, 1, 0, 0),
        )

    def xx_all(k):
        return remote(
            xs4.at[k % 2, :, pl.ds(0, 3 * BLK), :],
            rows.at[1, :, pl.ds(0, 3 * BLK), ecols(k)],
            xx_s.at[k % 2],
            xx_r.at[k],
            peer(here, 0, 0, 1, 0),
        )

    def early_send(k):
        for i in range(2):
            yy_copy(k, i).start()

    def early_own(k):
        own_local(k).start()
        own_remote(k).start()

    def early_pass(k):
        yy_all(k).wait_recv()
        for i in range(2):
            ff_copy(k, i).start()
            cc_copy(k, i).start()

    def early_rest(k):
        ff_all(k).wait_recv()
        cc_copy(k, 2).start()

    def early_select(k):
        own_local(k).wait()
        own_remote(k).wait()
        cc_all(k).wait_recv()

        def block(b, carry):
            for out in tiles(EW):
                picked = nn(sel[b], raw4[k, b, :, out]) * gp[b, :, 0:1]
                zs4[k % 2, b, :, out] = picked.astype(BF)
            za4[k, b, at(z, BLK, 16), :] = zs4[k % 2, b, at(z, BLK, 16), :]
            return carry

        lax.fori_loop(0, 4, block, 0)
        for d in (2, 1, 3):
            zz_copy(k, d).start()

    def early_turn(k):
        zz_all(k).wait_recv()

        def block(b, carry):
            for out in tiles(EW):
                xs4[k % 2, b, :, out] = nn(perm[...], za4[k, b, :, out]).astype(BF)
            return carry

        lax.fori_loop(0, 4, block, 0)
        for d in (2, 1, 3):
            xx_copy(k, d).start()
        xx_own(k).start()

    def early_fetch(k):
        xx_all(k).wait_recv()
        xx_own(k).wait()
        stage4_copy(k).start()

    def early_accumulate(k):
        stage4_copy(k).wait()
        acc[2] += nt(stage4[k % 2].reshape(4 * ROWS, EW), wd[:, ecols(k)])

    def which(i):
        a = i // FC
        return a, cols(i - a * (FC - F_DONE))

    def raw_start(i):
        def begin(src):
            dst = raw.at[i, mine, :]
            pltpu.make_async_copy(src, dst, raw_l.at[i]).start()
            remote(src, dst, raw_s.at[i], raw_r.at[i], peer(here, 0, 0, 0, 1)).start()

        pl.when(i // FC == 0)(lambda: begin(tok_ref.at[:, cols(i)]))
        pl.when(i // FC == 1)(lambda: begin(cot_ref.at[:, cols(i - FC + F_DONE)]))

    def raw_waits(i):
        src = tok_ref.at[:, cols(0)]
        dst = raw.at[i, mine, :]
        return (
            pltpu.make_async_copy(src, dst, raw_l.at[i]),
            remote(src, dst, raw_s.at[i], raw_r.at[i], peer(here, 0, 0, 0, 1)),
        )

    def z_copy(i, d):
        return remote(
            zs.at[i % 2, at((z + d) % 4, BLK, 16), :],
            za.at[i, at(z, BLK, 16), :],
            z_s.at[i % 2],
            z_r.at[i],
            peer(here, 0, d, 0, 0),
        )

    def x_copy(i, d):
        a, span = which(i)
        return remote(
            xs.at[i % 2, at((x + d) % 4, BLK, 16), :],
            rows.at[a, y, at(x, BLK, 16), span],
            x_s.at[i % 2],
            x_r.at[i],
            peer(here, 0, 0, d, 0),
        )

    def x_own(i):
        a, span = which(i)
        return pltpu.make_async_copy(
            xs.at[i % 2, at(x, BLK, 16), :], rows.at[a, y, at(x, BLK, 16), span], x_l.at[i % 2]
        )

    def y_copy(i, p):
        a, span = which(i)
        block = rows.at[a, y, :, span]
        return remote(
            block, block, y_s.at[i], y_r.at[i], peer(here, PLUS_MINUS[p], 0, 0, 0)
        )

    def f_copy(i, p):
        a, span = which(i)
        half = rows.at[a, (y + PLUS_MINUS[1 - p]) % 4, pl.ds(p * 96, 96), span]
        return remote(half, half, f_s.at[i], f_r.at[i], peer(here, PLUS_MINUS[p], 0, 0, 0))

    def stage_copy(i):
        a, span = which(i)
        return pltpu.make_async_copy(rows.at[a, :, :, span], stage.at[i % 2], st_l.at[i % 2])

    def z_all(i):
        return remote(
            zs.at[i % 2, pl.ds(0, 3 * BLK), :],
            za.at[i, pl.ds(0, 3 * BLK), :],
            z_s.at[i % 2],
            z_r.at[i],
            peer(here, 0, 1, 0, 0),
        )

    def x_all(i):
        a, span = which(i)
        return remote(
            xs.at[i % 2, pl.ds(0, 3 * BLK), :],
            rows.at[a, y, pl.ds(0, 3 * BLK), span],
            x_s.at[i % 2],
            x_r.at[i],
            peer(here, 0, 0, 1, 0),
        )

    def y_all(i):
        a, span = which(i)
        both = rows.at[a, pl.ds(0, 2), :, span]
        return remote(both, both, y_s.at[i], y_r.at[i], peer(here, 1, 0, 0, 0))

    def f_all(i):
        a, span = which(i)
        both = rows.at[a, y, :, span]
        return remote(both, both, f_s.at[i], f_r.at[i], peer(here, 1, 0, 0, 0))

    def late_select(i):
        for copy in raw_waits(i):
            copy.wait()
        scale = jnp.where(i // FC == 1, gp[y], 1.0)[:, 0:1]
        for out in tiles(FW):
            zs[i % 2, :, out] = (nn(sel[y], raw[i, :, out]) * scale).astype(BF)
        for d in (2, 1, 3):
            z_copy(i, d).start()
        za[i, at(z, BLK, 16), :] = zs[i % 2, at(z, BLK, 16), :]

    def late_turn(i):
        z_all(i).wait_recv()
        for out in tiles(FW):
            xs[i % 2, :, out] = nn(perm[...], za[i, :, out]).astype(BF)
        for d in (2, 1, 3):
            x_copy(i, d).start()
        x_own(i).start()

    def late_spread(i):
        x_all(i).wait_recv()
        x_own(i).wait()
        for p in range(2):
            y_copy(i, p).start()

    def late_pass(i):
        y_all(i).wait_recv()
        for p in range(2):
            f_copy(i, p).start()

    def late_fetch(i):
        f_all(i).wait_recv()
        stage_copy(i).start()

    def late_accumulate(i):
        stage_copy(i).wait()
        a, span = which(i)

        @pl.when(a == 0)
        def _():
            held = stage[i % 2].reshape(4 * ROWS, FW)
            acc[0] += nn(held, wg[span, :])
            acc[1] += nn(held, wu[span, :])

        @pl.when(a == 1)
        def _():
            acc[2] += nt(stage[i % 2].reshape(4 * ROWS, FW), wd[:, span])

    def drain(copy):
        return lambda k: copy(k).wait_send()

    perm[...] = swap_matrix()
    acc[...] = jnp.zeros_like(acc)
    met()
    for i in range(len(others)):
        meta_copy(i).start()
    early_send(0)
    early_send(1)
    for i in range(2):
        raw_start(i)
    early_own(0)
    early_own(1)
    for copy in weights:
        copy.start()
    for i in range(len(others)):
        meta_copy(i).wait()

    def plan(b, carry):
        earlier = (
            (
                lax.broadcasted_iota(jnp.int32, (TOK, TOK), 0)
                < lax.broadcasted_iota(jnp.int32, (TOK, TOK), 1)
            )
            .astype(F32)
            .astype(BF)
        )
        weight = jnp.zeros((ROWS, 1), F32)
        for m in range(2):
            route = metas[b, m, 0:1, :].astype(jnp.int32)
            prob = metas[b, m, 1:2, :]
            onehot = (lax.broadcasted_iota(jnp.int32, (32, TOK), 0) == route).astype(F32)
            before = nn(onehot.astype(BF), earlier)
            slot = jnp.sum(onehot * before, axis=0, keepdims=True).astype(jnp.int32)
            row = ((route >> 1) * 2 + m) * CAP + slot
            row = jnp.where((route & 1) == c, row, -1)
            chosen = lax.broadcasted_iota(jnp.int32, (ROWS, TOK), 0) == row
            sel[b, :, m * TOK : (m + 1) * TOK] = chosen.astype(F32).astype(BF)
            weight = weight + jnp.sum(jnp.where(chosen, prob, 0.0), axis=1, keepdims=True)
        gp[b] = jnp.broadcast_to(weight, (ROWS, 128))
        return carry

    lax.fori_loop(0, 4, plan, 0)

    def step(t, carry):
        when(t - 2, F_LATE, drain(z_all))
        when(t - 3, F_LATE, drain(x_all))
        when(t - 4, F_LATE, drain(y_all))
        when(t, F_EARLY, drain(yy_all))
        when(t - 1, F_EARLY, drain(ff_all))
        when(t - 2, F_EARLY, drain(cc_all))
        when(t - 3, F_EARLY, drain(zz_all))
        when(t - 4, F_EARLY, drain(xx_all))

        when(t, F_LATE, late_select)
        when(t + 2, F_EARLY, early_send)
        when(t + 2, F_EARLY, early_own)
        when(t + 2, F_LATE, raw_start)
        when(t + 1, F_EARLY, early_pass)
        when(t - 1, F_LATE, late_turn)
        when(t, F_EARLY, early_rest)
        when(t - 1, F_EARLY, early_select)
        when(t - 2, F_LATE, late_spread)
        when(t - 2, F_EARLY, early_turn)
        when(t - 3, F_LATE, late_pass)
        when(t - 4, F_LATE, late_fetch)
        when(t - 4, F_LATE, drain(f_all))
        when(t - 3, F_EARLY, early_fetch)

        @pl.when(t == 4)
        def _():
            for copy in weights:
                copy.wait()

        when(t - 4, F_EARLY, early_accumulate)
        when(t - 4, F_LATE, late_accumulate)
        return carry

    early_pass(0)
    lax.fori_loop(0, F_LATE + 4, step, 0)

    def finish(b, carry):
        part = at(b, Q, 256)
        gate, up, grad = acc[0, part, :], acc[1, part, :], acc[2, part, :]
        sig = jax.nn.sigmoid(gate)
        silu = gate * sig
        hidden = silu * up
        gate_grad = grad * up * sig * (1.0 + gate * (1.0 - sig))
        up_grad = grad * silu
        acts[0, part, :] = gate_grad.astype(BF)
        acts[1, part, :] = up_grad.astype(BF)
        acts[2, part, :] = hidden.astype(BF)
        return carry

    lax.fori_loop(0, 3, finish, 0)


def backward_kernel(
    acts,
    sel,
    rows,
    wg_hbm,
    wu_hbm,
    moment_ref,
    grad_hbm,
    update_hbm,
    second_ref,
    acts_t,
    grad_ref,
    update_ref,
    perm,
    far,
    relay,
    near,
    summed,
    xs,
    xa,
    zs,
    za,
    co,
    cr,
    xs4,
    xa4,
    zs4,
    za4,
    co4,
    cr4,
    relay4,
    summed4,
    stage,
    dw,
    squares,
    wg,
    wu,
    w_sem,
    p_s,
    p_r,
    n_s,
    n_r,
    x_s,
    x_r,
    z_s,
    z_r,
    c_s,
    c_r,
    xx_s,
    xx_r,
    zz_s,
    zz_r,
    cc_s,
    cc_r,
    pp_s,
    pp_r,
    nn_s,
    nn_r,
    st_l,
    out_l,
):
    here = place()
    y, z, x, c = here

    def cols(k):
        return at(k, BW, 128)

    def grad_out(span):
        return pltpu.make_async_copy(grad_ref.at[:, span], grad_hbm.at[:, span], out_l.at[0])

    def update_out(span):
        return pltpu.make_async_copy(update_ref.at[:, span], update_hbm.at[:, span], out_l.at[1])

    def ecols(k):
        return pl.ds(pl.multiple_of(B_FROM + k * CW, 128), CW)

    def tile(k, out):
        return pl.ds(pl.multiple_of(k * BW + out.start, 128), out.stop - out.start)

    def etile(k, out):
        return pl.ds(pl.multiple_of(B_FROM + k * CW + out.start, 128), out.stop - out.start)

    met = greet(here, ACROSS + COLUMN[:2])
    spans = ((0, BW), (B_FROM, CW), (BW, B_FROM - BW), (B_FROM + CW, D - B_FROM - CW))
    weights = [
        pltpu.make_async_copy(
            src.at[pl.ds(first, size)], dst.at[pl.ds(first, size)], w_sem.at[n, i]
        )
        for n, (first, size) in enumerate(spans)
        for i, (src, dst) in enumerate(((wg_hbm, wg), (wu_hbm, wu)))
    ]
    for copy in weights:
        copy.start()

    def stage_copy(a, k):
        return pltpu.make_async_copy(
            rows.at[a, :, :, cols(k)], stage.at[a, k % 2], st_l.at[a, k % 2]
        )

    for a in range(2):
        stage_copy(a, 0).start()
    squares[...] = jnp.zeros_like(squares)
    perm[...] = swap_matrix()
    met()
    for copy in weights[:4]:
        copy.wait()

    def partial(block, span):
        block_rows = at(block, ROWS, 16)
        total = nt(acts[0, block_rows, :], wg[span, :])
        total = total + nt(acts[1, block_rows, :], wu[span, :])
        return total.astype(BF)

    def p_copy(k, i):
        return remote(
            far.at[k % 2, pl.ds(i * 96, 96), :],
            relay.at[k, i],
            p_s.at[k % 2],
            p_r.at[k],
            peer(here, PLUS_MINUS[i], 0, 0, 0),
        )

    def n_copy(k, i):
        return remote(
            near.at[i, k % 2],
            summed.at[k, i],
            n_s.at[k % 2],
            n_r.at[k],
            peer(here, PLUS_MINUS[i], 0, 0, 0),
        )

    def x_copy(k, d):
        return remote(
            xs.at[k % 2, at((x + d) % 4, BLK, 16), :],
            xa.at[k, at(x, BLK, 16), :],
            x_s.at[k % 2],
            x_r.at[k],
            peer(here, 0, 0, d, 0),
        )

    def z_copy(k, d):
        return remote(
            zs.at[k % 2, at((z + d) % 4, BLK, 16), :],
            za.at[k, at(z, BLK, 16), :],
            z_s.at[k % 2],
            z_r.at[k],
            peer(here, 0, d, 0, 0),
        )

    def c_copy(k):
        return remote(
            co.at[k % 2, at(1 - c, TOK, TOK), :],
            cr.at[k],
            c_s.at[k % 2],
            c_r.at[k],
            peer(here, 0, 0, 0, 1),
        )

    def whole(src, dst, send, recv):
        return remote(src, dst, send, recv, peer(here, 1, 0, 0, 0))

    def p_all(k):
        return whole(far.at[k % 2], relay.at[k], p_s.at[k % 2], p_r.at[k])

    def n_all(k):
        return whole(near.at[:, k % 2], summed.at[k], n_s.at[k % 2], n_r.at[k])

    def x_all(k):
        three = pl.ds(0, 3 * BLK)
        return whole(xs.at[k % 2, three, :], xa.at[k, three, :], x_s.at[k % 2], x_r.at[k])

    def z_all(k):
        three = pl.ds(0, 3 * BLK)
        return whole(zs.at[k % 2, three, :], za.at[k, three, :], z_s.at[k % 2], z_r.at[k])

    def xx_all(k):
        three = pl.ds(0, 3 * BLK)
        return whole(
            xs4.at[k % 2, :, three, :], xa4.at[k, :, three, :], xx_s.at[k % 2], xx_r.at[k]
        )

    def zz_all(k):
        three = pl.ds(0, 3 * BLK)
        return whole(
            zs4.at[k % 2, :, three, :], za4.at[k, :, three, :], zz_s.at[k % 2], zz_r.at[k]
        )

    def pp_all(k):
        return whole(cr4.at[k, 0], relay4.at[k], pp_s.at[k], pp_r.at[k])

    def nn_all(k):
        return whole(cr4.at[k, pl.ds(0, 2)], summed4.at[k], nn_s.at[k], nn_r.at[k])

    def late_far(k):
        for out in tiles(BW):
            far[k % 2, :, out] = partial((y + 2) % 4, tile(k, out))
        for i in range(2):
            p_copy(k, i).start()

    def late_near(k):
        p_all(k).wait_recv()
        for i in range(2):
            added, plain = slice(i * 96, i * 96 + 96), slice(96 - i * 96, 192 - i * 96)
            for out in tiles(BW):
                term = partial((y + PLUS_MINUS[i]) % 4, tile(k, out))
                both = term[added].astype(F32) + relay[k, i, :, out].astype(F32)
                near[i, k % 2, added, out] = both.astype(BF)
                near[i, k % 2, plain, out] = term[plain]
            n_copy(k, i).start()

    def late_total(k):
        n_all(k).wait_recv()
        for out in tiles(BW):
            whole = partial(y, tile(k, out)).astype(F32)
            whole = whole + summed[k, 0, :, out].astype(F32)
            whole = whole + summed[k, 1, :, out].astype(F32)
            xs[k % 2, :, out] = whole.astype(BF)
        for d in (2, 1, 3):
            x_copy(k, d).start()
        xa[k, at(x, BLK, 16), :] = xs[k % 2, at(x, BLK, 16), :]

    def late_turn(k):
        x_all(k).wait_recv()
        for out in tiles(BW):
            zs[k % 2, :, out] = nn(perm[...], xa[k, :, out]).astype(BF)
        for d in (2, 1, 3):
            z_copy(k, d).start()
        za[k, at(z, BLK, 16), :] = zs[k % 2, at(z, BLK, 16), :]

    def late_unselect(k):
        z_all(k).wait_recv()
        for out in tiles(BW):
            block = za[k, :, out]
            co[k % 2, :, out] = tn(sel[y], block).astype(BF)
        c_copy(k).start()

    def late_join(k):
        c_copy(k).wait()
        both = co[k % 2, at(c, TOK, TOK), :].astype(F32) + cr[k].astype(F32)
        grad_ref[:, cols(k)] = both.astype(BF)
        grad_out(cols(k)).start()

    def xx_copy(k, d):
        return remote(
            xs4.at[k % 2, :, at((x + d) % 4, BLK, 16), :],
            xa4.at[k, :, at(x, BLK, 16), :],
            xx_s.at[k % 2],
            xx_r.at[k],
            peer(here, 0, 0, d, 0),
        )

    def zz_copy(k, d):
        return remote(
            zs4.at[k % 2, :, at((z + d) % 4, BLK, 16), :],
            za4.at[k, :, at(z, BLK, 16), :],
            zz_s.at[k % 2],
            zz_r.at[k],
            peer(here, 0, d, 0, 0),
        )

    def cc_copy(k):
        return remote(
            co4.at[k % 2, :, at(1 - c, TOK, TOK), :],
            cr4.at[k],
            cc_s.at[k % 2],
            cc_r.at[k],
            peer(here, 0, 0, 0, 1),
        )

    def pp_copy(k, i):
        return remote(
            cr4.at[k, (y + 2) % 4, pl.ds(i * 64, 64), :],
            relay4.at[k, i],
            pp_s.at[k],
            pp_r.at[k],
            peer(here, PLUS_MINUS[i], 0, 0, 0),
        )

    def nn_copy(k, i):
        return remote(
            cr4.at[k, (y + PLUS_MINUS[i]) % 4],
            summed4.at[k, i],
            nn_s.at[k],
            nn_r.at[k],
            peer(here, PLUS_MINUS[i], 0, 0, 0),
        )

    def early_terms(k):
        for out in tiles(CW):
            span = etile(k, out)
            term = nt(acts[0], wg[span, :]) + nt(acts[1], wu[span, :])
            xs4[k % 2, :, :, out] = term.astype(BF).reshape(4, ROWS, out.stop - out.start)
        xa4[k, :, at(x, BLK, 16), :] = xs4[k % 2, :, at(x, BLK, 16), :]
        for d in (2, 1, 3):
            xx_copy(k, d).start()

    def early_turn(k):
        xx_all(k).wait_recv()

        def block(b, carry):
            for out in tiles(CW):
                zs4[k % 2, b, :, out] = nn(perm[...], xa4[k, b, :, out]).astype(BF)
            za4[k, b, at(z, BLK, 16), :] = zs4[k % 2, b, at(z, BLK, 16), :]
            return carry

        lax.fori_loop(0, 4, block, 0)
        for d in (2, 1, 3):
            zz_copy(k, d).start()

    def early_unselect(k):
        zz_all(k).wait_recv()

        def block(b, carry):
            for out in tiles(CW):
                co4[k % 2, b, :, out] = tn(sel[b], za4[k, b, :, out]).astype(BF)
            return carry

        lax.fori_loop(0, 4, block, 0)
        cc_copy(k).start()

    def early_far(k):
        cc_copy(k).wait()

        def block(b, carry):
            both = co4[k % 2, b, at(c, TOK, TOK), :].astype(F32) + cr4[k, b].astype(F32)
            cr4[k, b] = both.astype(BF)
            return carry

        lax.fori_loop(0, 4, block, 0)
        for i in range(2):
            pp_copy(k, i).start()

    def early_near(k):
        pp_all(k).wait_recv()
        for i in range(2):
            block, added = (y + PLUS_MINUS[i]) % 4, slice(i * 64, i * 64 + 64)
            both = cr4[k, block, added, :].astype(F32) + relay4[k, i].astype(F32)
            cr4[k, block, added, :] = both.astype(BF)
            nn_copy(k, i).start()

    def early_join(k):
        nn_all(k).wait()
        both = cr4[k, y].astype(F32)
        for i in range(2):
            both = both + summed4[k, i].astype(F32)
        grad_ref[:, ecols(k)] = both.astype(BF)
        grad_out(ecols(k)).start()

    def turn_acts():
        def block(b, carry):
            part = at(b, Q, 256)
            for n, source in enumerate((2, 0, 1)):
                acts_t[n, :, part] = acts[source, part, :].astype(F32).T.astype(BF)
            return carry

        lax.fori_loop(0, 3, block, 0)

    def weight_grads(k):
        for a in range(2):
            stage_copy(a, k).wait()

        @pl.when(k + 1 < BC)
        def _():
            for a in range(2):
                stage_copy(a, k + 1).start()

        for out in tiles(BW):
            cot_rows = stage[1, k % 2, :, :, out].reshape(4 * ROWS, SUB)
            tok_rows = stage[0, k % 2, :, :, out].reshape(4 * ROWS, SUB)
            down = nn(acts_t[0], cot_rows)
            dw[:, tile(k, out)] = down
            gate = nn(acts_t[1], tok_rows)
            up = nn(acts_t[2], tok_rows)
            sq = down * down + gate * gate + up * up
            squares[...] += sq[:, 0:128] + sq[:, 128:256]

    def update(k):
        @pl.when(k == 0)
        def _():
            mean = jnp.sum(squares[...], axis=1, keepdims=True) / (3.0 * D)
            old = jnp.broadcast_to(moment_ref[...], (128, Q)).T
            second = moment_decay * old + (1.0 - moment_decay) * mean
            second_ref[...] = second.T[0:1, :]
            squares[...] = 1.0 / (jnp.sqrt(second) + epsilon)

        for j in range(BW // 128):
            out = pl.ds(pl.multiple_of(k * BW + j * 128, 128), 128)
            update_ref[:, out] = (dw[:, out] * squares[...]).astype(BF)
        update_out(cols(k)).start()

    def drain(copy):
        return lambda k: copy(k).wait_send()

    def step(t, carry):
        when(t - 2, B_LATE, drain(p_all))
        when(t - 3, B_LATE, drain(n_all))
        when(t - 4, B_LATE, drain(x_all))
        when(t - 5, B_LATE, drain(z_all))
        when(t - 2, B_EARLY, drain(xx_all))
        when(t - 3, B_EARLY, drain(zz_all))
        when(t - 5, B_EARLY, drain(pp_all))

        @pl.when(t == 1)
        def _():
            for copy in weights[4:]:
                copy.wait()

        when(t, B_LATE, late_far)
        when(t - 1, B_LATE, late_near)
        when(t, B_EARLY, early_terms)
        pl.when(t == 0)(turn_acts)
        when(t * 2, BC, weight_grads)
        when(t - 1, B_EARLY, early_turn)
        when(t - 2, B_LATE, late_total)
        when(t - 2, B_EARLY, early_unselect)
        when(t - 3, B_LATE, late_turn)
        when(t * 2 + 1, BC, weight_grads)
        when(t - 3, B_EARLY, early_far)
        when(t - 4, B_LATE, late_unselect)
        when(t - 4, B_EARLY, early_near)
        when(t - 5, B_LATE, late_join)
        when(t - 5, B_EARLY, early_join)
        for n in range(3):
            when((t - BC // 2) * 3 + n, BC, update)
        return carry

    lax.fori_loop(0, B_LATE + 5, step, 0)
    grad_out(pl.ds(0, D)).wait()
    update_out(pl.ds(0, D)).wait()


def shards(tokens, grad_out, routes, gate_prob, w_gate, w_up, w_down, moment_prev):
    vmem = pl.BlockSpec(memory_space=pltpu.VMEM)
    hbm = pl.BlockSpec(memory_space=pltpu.HBM)
    dma = pltpu.SemaphoreType.DMA

    def held(*shape):
        return pltpu.VMEM(shape, BF)

    rows, acts, sel = pl.pallas_call(
        forward_kernel,
        name="dispatch",
        out_shape=(
            jax.ShapeDtypeStruct((2, 4, ROWS, D), BF),
            jax.ShapeDtypeStruct((3, 4 * ROWS, Q), BF),
            jax.ShapeDtypeStruct((4, ROWS, 2 * TOK), BF),
        ),
        in_specs=[vmem, vmem, hbm, hbm, hbm, hbm, hbm],
        out_specs=(hbm, vmem, vmem),
        scratch_shapes=[
            pltpu.VMEM((4, 2, 8, TOK), F32),
            pltpu.VMEM((4, ROWS, 128), F32),
            held(ROWS, ROWS),
            held(F_LATE, 2 * TOK, FW),
            held(2, ROWS, FW),
            held(F_LATE, ROWS, FW),
            held(2, ROWS, FW),
            held(F_EARLY, 4, 2 * TOK, EW),
            held(2, 4, ROWS, EW),
            held(F_EARLY, 4, ROWS, EW),
            held(2, 4, ROWS, EW),
            held(2, 4, ROWS, FW),
            held(2, 4, ROWS, EW),
            pltpu.VMEM((3, 4 * ROWS, Q), F32),
            held(D, Q),
            held(D, Q),
            held(Q, D),
            dma((3,)),
            dma((7,)),
            dma((7,)),
            dma((F_LATE,)),
            dma((F_LATE,)),
            dma((F_LATE,)),
            dma((2,)),
            dma((F_LATE,)),
            dma((2,)),
            dma((F_LATE,)),
            dma((2,)),
            dma((F_LATE,)),
            dma((F_LATE,)),
            dma((F_LATE,)),
            dma((F_LATE,)),
            dma((2,)),
            dma((F_EARLY,)),
            dma((F_EARLY,)),
            dma((F_EARLY,)),
            dma((F_EARLY,)),
            dma((F_EARLY,)),
            dma((F_EARLY,)),
            dma((F_EARLY,)),
            dma((F_EARLY,)),
            dma((F_EARLY,)),
            dma((2,)),
            dma((F_EARLY,)),
            dma((2,)),
            dma((F_EARLY,)),
            dma((2,)),
            dma((2,)),
        ],
        compiler_params=pltpu.CompilerParams(
            collective_id=0, has_side_effects=True, vmem_limit_bytes=60 * 2**20
        ),
    )(
        routes.reshape(1, TOK),
        gate_prob.reshape(1, TOK),
        tokens,
        grad_out,
        w_gate[0],
        w_up[0],
        w_down[0],
    )
    grad_in, update, second = pl.pallas_call(
        backward_kernel,
        name="combine",
        out_shape=(
            jax.ShapeDtypeStruct((TOK, D), BF),
            jax.ShapeDtypeStruct((Q, D), BF),
            jax.ShapeDtypeStruct((1, Q), F32),
        ),
        in_specs=[vmem, vmem, hbm, hbm, hbm, vmem],
        out_specs=(hbm, hbm, vmem),
        scratch_shapes=[
            held(3, Q, 4 * ROWS),
            held(TOK, D),
            held(Q, D),
            held(ROWS, ROWS),
            held(2, ROWS, BW),
            held(B_LATE, 2, 96, BW),
            held(2, 2, ROWS, BW),
            held(B_LATE, 2, ROWS, BW),
            held(2, ROWS, BW),
            held(B_LATE, ROWS, BW),
            held(2, ROWS, BW),
            held(B_LATE, ROWS, BW),
            held(2, 2 * TOK, BW),
            held(B_LATE, TOK, BW),
            held(2, 4, ROWS, CW),
            held(B_EARLY, 4, ROWS, CW),
            held(2, 4, ROWS, CW),
            held(B_EARLY, 4, ROWS, CW),
            held(2, 4, 2 * TOK, CW),
            held(B_EARLY, 4, TOK, CW),
            held(B_EARLY, 2, 64, CW),
            held(B_EARLY, 2, TOK, CW),
            held(2, 2, 4, ROWS, BW),
            pltpu.VMEM((Q, D), F32),
            pltpu.VMEM((Q, 128), F32),
            held(D, Q),
            held(D, Q),
            dma((4, 2)),
            dma((2,)),
            dma((B_LATE,)),
            dma((2,)),
            dma((B_LATE,)),
            dma((2,)),
            dma((B_LATE,)),
            dma((2,)),
            dma((B_LATE,)),
            dma((2,)),
            dma((B_LATE,)),
            dma((2,)),
            dma((B_EARLY,)),
            dma((2,)),
            dma((B_EARLY,)),
            dma((2,)),
            dma((B_EARLY,)),
            dma((B_EARLY,)),
            dma((B_EARLY,)),
            dma((B_EARLY,)),
            dma((B_EARLY,)),
            dma((2, 2)),
            dma((2,)),
        ],
        compiler_params=pltpu.CompilerParams(
            collective_id=1, has_side_effects=True, vmem_limit_bytes=60 * 2**20
        ),
    )(acts, sel, rows, w_gate[0], w_up[0], moment_prev)
    return grad_in, update[None], second


def solution(mesh):
    placed = (
        P(("dp", "expert"), None),
        P(("dp", "expert"), None),
        P(("dp", "expert"), None),
        P(("dp", "expert"), None),
        P("expert", None, "dp"),
        P("expert", None, "dp"),
        P("expert", "dp", None),
        P("expert", "dp"),
    )
    return jax.shard_map(
        shards,
        mesh=mesh,
        in_specs=placed,
        out_specs=(P(("dp", "expert"), None), P("expert", "dp", None), P("expert", "dp")),
        check_vma=False,
    )
```
